512 devices in a mesh: row: 64 (over z_lo, x, core), col: 8 (over z_hi, y).
Axes of the slice: x: 4, y: 4, z: 16 (z_hi: 2, z_lo: 8; z = z_hi * 8 + z_lo), core: 2. Of those that a mesh axis runs over, the one named last changes fastest.
Arguments:
- node_features: bfloat16 [65536, 128], P(('row', 'col')), may hold values from -6 to 6
- tile_values: bfloat16 [64, 8, 112, 128, 128], P('row', 'col'), may hold values from -0.046875 to 0.046875
- tile_rows: int32 [64, 8, 112], P('row', 'col'), may hold values from 0 to 7
- tile_cols: int32 [64, 8, 112], P('row', 'col'), may hold values from 0 to 63
- weight_self: bfloat16 [128, 256], replicated, may hold values from -0.5 to 0.5
- weight_neighbour: bfloat16 [128, 256], replicated, may hold values from -0.5 to 0.5
- node_bias: float32 [256], replicated, may hold values from -4 to 4
- output_grad: bfloat16 [65536, 256], P(('row', 'col')), may hold values from -6 to 6
Outputs:
- out_features: bfloat16 [65536, 256], P(('row', 'col'))
- input_grad: bfloat16 [65536, 128], P(('row', 'col'))
- grad_self: float32 [128, 256], replicated
- grad_neighbour: float32 [128, 256], replicated
- grad_bias: float32 [256], replicated
The draws below stay inside these ranges and needn't reach their ends.
All inputs are finite; a program needn't handle non-finite values.
Results may differ from the reference program's by a relative error of at most 0.015.
Values may be sent and summed in bfloat16 or wider, within the bound.
A program may use at most 64 MiB of HBM per device.

```python
from functools import partial
import jax
import jax.numpy as jnp
from jax import lax

FEAT = 128
UNITS = 256
BLK = 128
ROWS_DEV = 128
TILES = 112
NODES = 65536
N_ROW = 64
N_COL = 8


def set_ends(array, stream_key, least, largest):
    longest = array.shape.index(max(array.shape))
    spots = []
    for shift in (0, 1):
        where = [jax.random.randint(jax.random.fold_in(stream_key, axis), (), 0, length) for axis, length in enumerate(array.shape)]
        where[longest] = (where[longest] + shift) % array.shape[longest]
        spots.append(tuple(where))
    return array.at[spots[0]].set(least).at[spots[1]].set(largest)


def block_scale(own_key, dims, split, low, high):
    factor_of, own = 1.0, jax.random.fold_in(own_key, 6)
    for axis_at, blocks in split:
        steps = jnp.exp(jax.random.uniform(jax.random.fold_in(own, axis_at), (blocks,), jnp.float32, low / len(split), high / len(split)))
        factor_of = factor_of * jnp.repeat(steps, dims[axis_at] // blocks).reshape([-1 if axis == axis_at else 1 for axis in range(len(dims))])
    return factor_of


def scatter_about(own_key, shape, width, bound, split=(), kind=jnp.bfloat16):
    gain = block_scale(own_key, shape, split, -0.22, 0.18) if split else 1.0
    values = jax.random.normal(own_key, shape, jnp.float32) * width * gain
    return jnp.minimum(jnp.maximum(values, -bound), bound).astype(kind)


def setup_inputs(seed: int = 0) -> dict:
    arg_keys = jax.random.split(jax.random.key(seed), 9)
    return {
        "node_features": scatter_about(arg_keys[0], (NODES, FEAT), 1.0, 6.0, ((0, 512),)),
        "tile_values": scatter_about(arg_keys[1], (N_ROW, N_COL, TILES, BLK, BLK), (TILES * 16384 // ROWS_DEV) ** -0.5, 0.046875, ((0, 64), (1, 8))),
        "tile_rows": set_ends(jax.random.randint(arg_keys[2], (N_ROW, N_COL, TILES), 0, N_COL * ROWS_DEV // 128), jax.random.fold_in(arg_keys[2], 1), 0, (N_COL * ROWS_DEV // 128) - 1).astype(jnp.int32),
        "tile_cols": set_ends(jax.random.randint(arg_keys[3], (N_ROW, N_COL, TILES), 0, N_ROW * ROWS_DEV // 128), jax.random.fold_in(arg_keys[3], 1), 0, (N_ROW * ROWS_DEV // 128) - 1).astype(jnp.int32),
        "weight_self": scatter_about(arg_keys[4], (FEAT, UNITS), FEAT ** -0.5, 0.5),
        "weight_neighbour": scatter_about(arg_keys[5], (FEAT, UNITS), FEAT ** -0.5, 0.5),
        "node_bias": scatter_about(arg_keys[6], (UNITS,), 1.0, 4.0, (), jnp.float32),
        "output_grad": scatter_about(arg_keys[7], (NODES, UNITS), 1.0, 6.0, ((0, 512),)),
    }


def collect_tiles(tile_block, row_index, col_index, panels, blocks):
    picked = jnp.take(panels, col_index, axis=0).astype(jnp.float32)
    product = jnp.einsum("tij,tjf->tif", tile_block.astype(jnp.float32), picked)
    placement = (row_index[:, None] == jnp.arange(blocks, dtype=jnp.int32)[None, :]).astype(jnp.float32)
    return jnp.einsum("tr,tif->rif", placement, product).reshape(blocks * 128, -1)


def spread_tiles(tile_block, row_index, col_index, grad_blocks, blocks):
    picked = jnp.take(grad_blocks, row_index, axis=0).astype(jnp.float32)
    product = jnp.einsum("tij,tif->tjf", tile_block.astype(jnp.float32), picked)
    placement = (col_index[:, None] == jnp.arange(blocks, dtype=jnp.int32)[None, :]).astype(jnp.float32)
    return jnp.einsum("tc,tjf->cjf", placement, product).reshape(blocks * 128, -1)


def reference(node_features, tile_values, tile_rows, tile_cols, weight_self, weight_neighbour, node_bias, output_grad):
    row_blocks = N_COL * ROWS_DEV // 128
    col_blocks = N_ROW * ROWS_DEV // 128
    grid_feats = node_features.reshape(N_ROW, N_COL, ROWS_DEV, FEAT)
    panels = jnp.transpose(grid_feats, (1, 0, 2, 3)).reshape(N_COL, col_blocks, 128, FEAT)

    def shard_sum(shard_args):
        tile_block, row_index, col_index = shard_args
        shard_parts = jax.vmap(partial(collect_tiles, blocks=row_blocks))(tile_block, row_index, col_index, panels)
        return jnp.sum(shard_parts, axis=0)

    neighbour_sum = lax.map(shard_sum, (tile_values, tile_rows, tile_cols)).reshape(-1, FEAT).astype(jnp.bfloat16)
    preact = (jnp.dot(node_features, weight_self, preferred_element_type=jnp.float32)
              + jnp.dot(neighbour_sum, weight_neighbour, preferred_element_type=jnp.float32) + node_bias)
    out_features = jax.nn.silu(preact).astype(jnp.bfloat16)
    sigmoid_v = jax.nn.sigmoid(preact)
    pre_grad = (output_grad.astype(jnp.float32) * sigmoid_v * (1.0 + preact * (1.0 - sigmoid_v))).astype(jnp.bfloat16)
    grad_bias = jnp.sum(pre_grad.astype(jnp.float32), axis=0)
    grad_self = jnp.dot(node_features.T, pre_grad, preferred_element_type=jnp.float32)
    grad_neighbour = jnp.dot(neighbour_sum.T, pre_grad, preferred_element_type=jnp.float32)
    sum_grad = jnp.dot(pre_grad, weight_neighbour.T, preferred_element_type=jnp.float32).astype(jnp.bfloat16)
    grad_shards = sum_grad.reshape(N_ROW, row_blocks, 128, FEAT)

    def scan_step(running, shard_args):
        tile_block, row_index, col_index, grad_blocks = shard_args
        shard_parts = jax.vmap(partial(spread_tiles, grad_blocks=grad_blocks, blocks=col_blocks))(tile_block, row_index, col_index)
        return running + shard_parts, None

    zero_total = jnp.zeros((N_COL, N_ROW * ROWS_DEV, FEAT), jnp.float32)
    running, _ = lax.scan(scan_step, zero_total, (tile_values, tile_rows, tile_cols, grad_shards))
    neighbour_grad = jnp.transpose(running.reshape(N_COL, N_ROW, ROWS_DEV, FEAT), (1, 0, 2, 3)).reshape(-1, FEAT)
    input_grad = (jnp.dot(pre_grad, weight_self.T, preferred_element_type=jnp.float32) + neighbour_grad).astype(jnp.bfloat16)
    return out_features, input_grad, grad_self, grad_neighbour, grad_bias
```

```python
import functools

import jax
import jax.numpy as jnp
from jax import lax
from jax.experimental import pallas as pl
from jax.experimental.pallas import tpu as pltpu
from jax.sharding import PartitionSpec as P

MESH = pl.DeviceIdType.MESH
BLK = 128
F32 = jnp.float32
BF16 = jnp.bfloat16
VMEM_LIMIT = 64 * 2**20

NX, NC = 4, 2
NY = 4


def dot_nn(a, b):
    return lax.dot_general(a, b, (((1,), (0,)), ((), ())), preferred_element_type=F32)


def dot_nt(a, b):
    return lax.dot_general(a, b, (((1,), (1,)), ((), ())), preferred_element_type=F32)


def dot_tn(a, b):
    return lax.dot_general(a, b, (((0,), (0,)), ((), ())), preferred_element_type=F32)


class Links:
    def __init__(self, send_sems, recv_sems):
        self.send_sems, self.recv_sems, self.copies = send_sems, recv_sems, []

    def send(self, src, dst, device_id):
        at = len(self.copies)
        copy = pltpu.make_async_remote_copy(
            src_ref=src,
            dst_ref=dst,
            send_sem=self.send_sems.at[at],
            recv_sem=self.recv_sems.at[at],
            device_id=device_id,
            device_id_type=MESH,
        )
        copy.start()
        self.copies.append(copy)
        return copy

    def finish(self):
        for copy in self.copies:
            copy.wait_send()


def send_sorted(block, carried, n_blocks, index, at):
    tiles = block.shape[1]
    shape = (tiles, tiles)
    down = lax.broadcasted_iota(jnp.int32, shape, 0)
    across = lax.broadcasted_iota(jnp.int32, shape, 1)

    def turned(line):
        return jnp.sum(jnp.where(down == across, line, 0), axis=1, keepdims=True)

    block_down, carried_down = turned(block), turned(carried)
    before = (block < block_down) | ((block == block_down) & (across < down))
    rank = jnp.sum(before.astype(jnp.int32), axis=1, keepdims=True)
    goes_on = jnp.sum(
        ((block == block_down) & (across < down)).astype(jnp.int32), axis=1, keepdims=True
    )
    hot = rank == across

    def sorted_line(values):
        return jnp.sum(jnp.where(hot, values, 0), axis=0, keepdims=True)

    index[at : at + 1, :tiles] = sorted_line(down)
    index[at + 1 : at + 2, :tiles] = sorted_line(carried_down)
    index[at + 2 : at + 3, :tiles] = sorted_line(jnp.minimum(goes_on, 1))
    ids = lax.broadcasted_iota(jnp.int32, (tiles, n_blocks), 1)
    up_to = jnp.sum((block_down <= ids).astype(jnp.int32), axis=0, keepdims=True)
    held = jnp.sum((block_down == ids).astype(jnp.int32), axis=0, keepdims=True)
    index[at + 3 : at + 4, :n_blocks] = jnp.maximum(up_to - 1, 0)
    index[at + 4 : at + 5, :n_blocks] = jnp.minimum(held, 1)


def kernel(
    nz,
    tiles,
    x_hbm,
    ws_hbm,
    wn_hbm,
    bias_hbm,
    og_hbm,
    rows_hbm,
    cols_hbm,
    tiles_hbm,
    out_hbm,
    ingrad_hbm,
    gself_hbm,
    gneigh_hbm,
    gbias_hbm,
    out_ref,
    ingrad_ref,
    gself_ref,
    gneigh_ref,
    gbias_ref,
    ws_ref,
    wn_ref,
    bias_ref,
    og_ref,
    rows_ref,
    cols_ref,
    index_buf,
    index,
    tile_buf,
    panels,
    runs,
    self_pre,
    self_grad,
    y_send,
    y_recv,
    zh_send,
    zh_recv,
    gt,
    core_send,
    core_recv,
    far_send,
    far_recv,
    near_send,
    near_recv,
    quad_send,
    quad_recv,
    pair_send,
    pair_recv,
    wy_send,
    wy_recv,
    wz_send,
    wz_recv,
    wh_send,
    wh_recv,
    wx_recv,
    wc_send,
    wc_recv,
    w_out,
    load_sems,
    store_sems,
    send_sems,
    recv_sems,
):
    half = nz // 2
    n_cols = nz * NX * NC
    n_rows = 2 * NY
    row = lax.axis_index("row")
    col = lax.axis_index("col")
    core = lax.rem(row, NC)
    x = lax.rem(row // NC, NX)
    z = row // (NC * NX)
    zq = z // half
    zi = lax.rem(z, half)
    y = lax.rem(col, NY)
    zh = col // NY
    other = 1 - core

    def at_row(z_to, x_to, core_to):
        return {"row": (z_to * NX + x_to) * NC + core_to, "col": col}

    def at_col(zh_to, y_to):
        return {"row": row, "col": zh_to * NY + y_to}

    def turn_z(d):
        return lax.rem(z + d, nz)

    def turn_zi(d):
        return lax.rem(zi + d, half)

    def turn_x(d):
        return lax.rem(x + d, NX)

    def turn_y(d):
        return lax.rem(y + d, NY)

    def to_z(d):
        return at_row(turn_z(d), x, core)

    def to_mate(e):
        return at_row(zq * half + turn_zi(e), x, core)

    def to_x(d):
        return at_row(z, turn_x(d), core)

    def to_y(d):
        return at_col(zh, turn_y(d))

    to_pair = at_row((1 - zq) * half + zi, x, core)
    to_core = at_row(z, x, other)
    to_zh = at_col(1 - zh, y)
    mates = [e for e in (1, half - 1) if e] + list(range(2, half - 1))
    mates = list(dict.fromkeys(mates))

    ord_r, pan, keep_r, end_r, has_r, ord_c, grow, keep_c, end_c, has_c = range(10)

    def slot(core_of, x_of, z_of):
        return (core_of * NX + x_of) * nz + z_of

    own = slot(core, x, z)
    loads = []
    for src, dst in (
        (x_hbm, panels.at[own]),
        (rows_hbm, rows_ref),
        (cols_hbm, cols_ref),
        (ws_hbm, ws_ref),
        (bias_hbm, bias_ref),
        (tiles_hbm.at[0, 0], tile_buf),
        (wn_hbm, wn_ref),
        (og_hbm, og_ref),
    ):
        loads.append(pltpu.make_async_copy(src, dst, load_sems.at[len(loads)]))
        loads[-1].start()
    load_x, load_rows, load_cols, load_ws, load_bias, load_tiles, load_wn, load_og = loads

    barrier = pltpu.get_barrier_semaphore()
    partners = [to_z(d) for d in range(1, nz)] + [to_x(d) for d in range(1, NX)]
    partners += [to_y(d) for d in range(1, NY)] + [to_core, to_zh]
    for partner in partners:
        pl.semaphore_signal(barrier, inc=1, device_id=partner, device_id_type=MESH)
    load_x.wait()
    pl.semaphore_wait(barrier, len(partners))

    links = Links(send_sems, recv_sems)
    stores = []

    def store(src, dst):
        stores.append(pltpu.make_async_copy(src, dst, store_sems.at[len(stores)]))
        stores[-1].start()

    def panel_to(slot_at, device_id):
        return links.send(panels.at[slot_at], panels.at[slot_at], device_id)

    pair_copy = panel_to(own, to_pair)
    z_copies = {e: panel_to(own, to_mate(e)) for e in mates}
    pair_z = (1 - zq) * half + zi
    relayed = {}

    def mate_z(e, q):
        return q * half + turn_zi(half - e)

    arrivals = [(z, None)] + [(mate_z(e, zq), z_copies[e]) for e in mates[:2]]
    arrivals += [(pair_z, pair_copy)] + [(mate_z(e, zq), z_copies[e]) for e in mates[2:]]
    arrivals += [(mate_z(e, 1 - zq), e) for e in mates]
    plus, minus, far, crossed = {}, {}, {}, []

    def cross(slot_at):
        crossed.append(panel_to(slot_at, to_core))

    def own_step(i):
        z_of, copy = arrivals[i]
        here = slot(core, x, z_of)
        if copy is not None:
            (relayed[copy] if isinstance(copy, int) else copy).wait_recv()
        if copy is pair_copy:
            for e in mates:
                relayed[e] = panel_to(here, to_mate(e))
        plus[i] = panel_to(here, to_x(1))
        minus[i] = panel_to(here, to_x(NX - 1))
        cross(here)

    def near_step(i):
        z_of = arrivals[i][0]
        from_minus = slot(core, turn_x(NX - 1), z_of)
        from_plus = slot(core, turn_x(1), z_of)
        plus[i].wait_recv()
        if i % 2 == 0:
            far[i] = panel_to(from_minus, to_x(1))
        cross(from_minus)
        minus[i].wait_recv()
        if i % 2 == 1:
            far[i] = panel_to(from_plus, to_x(NX - 1))
        cross(from_plus)

    def far_step(i):
        far[i].wait_recv()
        cross(slot(core, turn_x(2), arrivals[i][0]))

    def prepare():
        load_rows.wait()
        load_cols.wait()
        rows = rows_ref[...]
        cols = cols_ref[...]
        slots = slot(cols & (NC - 1), (cols // NC) & (NX - 1), cols // (NC * NX))
        send_sorted(rows, slots, n_rows, index_buf, 0)
        send_sorted(slots, rows, n_cols, index_buf, 5)
        index_copy = pltpu.make_async_copy(index_buf, index, load_sems.at[len(loads)])
        index_copy.start()
        load_ws.wait()
        load_bias.wait()
        self_pre[...] = dot_nn(panels[own], ws_ref[...]) + bias_ref[...]
        index_copy.wait()

    for i in range(nz + 2):
        if i < nz:
            own_step(i)
        if i == 0:
            prepare()
        if 0 <= i - 1 < nz:
            near_step(i - 1)
        if 0 <= i - 2 < nz:
            far_step(i - 2)
    load_tiles.wait()
    load_wn.wait()
    load_og.wait()
    for copy in crossed:
        copy.wait_recv()

    step = 8

    def collect(k, acc):
        for u in range(step):
            n = k * step + u
            term = dot_nn(tile_buf[index[ord_r, n]], panels[index[pan, n]])
            acc = acc * index[keep_r, n].astype(F32) + term
            runs[n] = acc
        return acc

    lax.fori_loop(0, tiles // step, collect, jnp.zeros((BLK, BLK), F32))

    parts = 2
    width = BLK // parts

    def lines(p):
        return slice(p * width, (p + 1) * width)

    def row_sum(r, p):
        return runs[index[end_r, r], lines(p), :] * index[has_r, r].astype(F32)

    y_copies, zh_copies = {}, {}
    for p in range(parts):
        for d in (2, 1, 3):
            for h in range(2):
                y_send[p, d - 1, h] = row_sum(h * NY + turn_y(d), p).astype(BF16)
            y_copies[p, d] = links.send(y_send.at[p, d - 1], y_recv.at[p, d - 1], to_y(d))
    for p in range(parts):
        theirs = row_sum((1 - zh) * NY + y, p)
        for d in (1, 3, 2):
            y_copies[p, d].wait_recv()
            theirs = theirs + y_recv[p, d - 1, 1 - zh].astype(F32)
        zh_send[p] = theirs.astype(BF16)
        zh_copies[p] = links.send(zh_send.at[p], zh_recv.at[p], to_zh)
    mine = []
    for p in range(parts):
        total_here = row_sum(zh * NY + y, p)
        for d in (1, 3, 2):
            total_here = total_here + y_recv[p, d - 1, zh].astype(F32)
        mine.append(total_here)
    for p in range(parts):
        zh_copies[p].wait_recv()
        mine[p] = (mine[p] + zh_recv[p].astype(F32)).astype(BF16)
    sums = jnp.concatenate(mine, axis=0)

    pre = self_pre[...] + dot_nn(sums, wn_ref[...])
    sig = 1.0 / (1.0 + jnp.exp(-pre))
    pre_grad = (og_ref[...].astype(F32) * sig * (1.0 + pre * (1.0 - sig))).astype(BF16)

    me = zh * NY + y
    they = (1 - zh) * NY + y
    gt[me] = dot_nt(wn_ref[...], pre_grad).astype(BF16)

    def gt_part(r, p):
        return gt.at[r, pl.ds(p * width, width)]

    zh_gt = [links.send(gt_part(me, p), gt_part(me, p), to_zh) for p in range(parts)]
    gt_copies = [links.send(gt.at[me], gt.at[me], to_y(d)) for d in (2, 1, 3)]
    out_ref[...] = (pre * sig).astype(BF16)
    store(out_ref, out_hbm)
    self_grad[...] = dot_nt(ws_ref[...], pre_grad)

    wide_self = dot_tn(panels[own], pre_grad).astype(BF16)
    wide_neigh = dot_tn(sums, pre_grad).astype(BF16)
    for q, block in enumerate(
        (wide_self[:, :BLK], wide_self[:, BLK:], wide_neigh[:, :BLK], wide_neigh[:, BLK:])
    ):
        wy_send[q, :BLK] = block
    bias_sum = jnp.sum(pre_grad.astype(F32), axis=0, keepdims=True)
    spot = lax.broadcasted_iota(jnp.int32, (16, BLK), 0)
    bias_rows = jnp.where(
        spot == 0, bias_sum[:, :BLK], jnp.where(spot == 1, bias_sum[:, BLK:], 0.0)
    ).astype(BF16)
    for q in range(4):
        wy_send[q, BLK:] = bias_rows
    wy_recv[y] = wy_send[y]

    for p in range(parts):
        zh_gt[p].wait_recv()
        gt_copies += [links.send(gt_part(they, p), gt_part(they, p), to_y(d)) for d in (2, 1, 3)]
    wy_copies = [links.send(wy_send.at[turn_y(d)], wy_recv.at[y], to_y(d)) for d in (2, 1, 3)]
    for copy in gt_copies:
        copy.wait_recv()

    def spread(k, acc):
        for u in range(step):
            n = k * step + u
            term = dot_nn(gt[index[grow, n]], tile_buf[index[ord_c, n]])
            acc = acc * index[keep_c, n].astype(F32) + term
            runs[n] = acc
        return acc

    steps = tiles // step
    acc = lax.fori_loop(0, steps // 2, spread, jnp.zeros((BLK, BLK), F32))

    for copy in wy_copies:
        copy.wait_recv()
    w_sum = wy_recv[0].astype(F32)
    for q in range(1, NY):
        w_sum = w_sum + wy_recv[q].astype(F32)
    part = BLK // nz
    for q in range(nz):
        wz_send[q, :part] = w_sum[q * part : (q + 1) * part]
        wz_send[q, part:] = w_sum[BLK : BLK + 8]
    wz_recv[z] = wz_send[z]
    wz_copies = [links.send(wz_send.at[turn_z(d)], wz_recv.at[z], to_z(d)) for d in range(1, nz)]

    lax.fori_loop(steps // 2, steps, spread, acc)

    def chunk(core_of, d):
        return slot(core_of, turn_x(d), 0)

    def col_sum(c, p):
        return runs[index[end_c, c], lines(p), :] * index[has_c, c].astype(F32)

    def paired(p, d, i):
        return col_sum(chunk(core, d) + i, p) + core_recv[p, turn_x(d) * nz + i].astype(F32)

    lower, upper = pl.ds(0, half), pl.ds(half, half)
    core_copies, far_copies, near_copies, quad_copies, pair_copies = {}, {}, {}, {}, {}

    def core_stage(p):
        for d in (2, 1, 3, 0):
            base, first = chunk(other, d), turn_x(d) * nz

            def fill(i, carry, base=base, first=first):
                core_send[p, first + i] = col_sum(base + i, p).astype(BF16)
                return carry

            lax.fori_loop(0, nz, fill, 0)
            blocks = pl.ds(first, nz)
            core_copies[p, d] = links.send(
                core_send.at[p, blocks], core_recv.at[p, blocks], to_core
            )

    def far_stage(p):
        core_copies[p, 2].wait_recv()

        def fill(i, carry):
            far_send[p, i] = paired(p, 2, i).astype(BF16)
            return carry

        lax.fori_loop(0, nz, fill, 0)
        far_copies[p, 0] = links.send(far_send.at[p, lower], far_recv.at[p, lower], to_x(1))
        far_copies[p, 1] = links.send(far_send.at[p, upper], far_recv.at[p, upper], to_x(NX - 1))

    def near_stage(p, way, with_far):
        d = (1, NX - 1)[way]
        if with_far:
            far_copies[p, way].wait_recv()
        else:
            core_copies[p, d].wait_recv()
        first = half * (way if with_far else 1 - way)

        def fill(i, carry):
            value = paired(p, d, i)
            if with_far:
                value = value + far_recv[p, i].astype(F32)
            near_send[p, way, i] = value.astype(BF16)
            return carry

        lax.fori_loop(first, first + half, fill, 0)
        blocks = pl.ds(first, half)
        near_copies[p, way, with_far] = links.send(
            near_send.at[p, way, blocks], near_recv.at[p, way, blocks], to_x(d)
        )

    def z_total(p, i):
        return (
            paired(p, 0, i) + near_recv[p, 0, i].astype(F32) + near_recv[p, 1, i].astype(F32)
        )

    def quad_stage(p):
        core_copies[p, 0].wait_recv()
        for way in range(2):
            for with_far in (False, True):
                near_copies[p, way, with_far].wait_recv()
        for e in mates:
            quad_send[p, e, 0] = z_total(p, zq * half + turn_zi(e)).astype(BF16)
            quad_send[p, e, 1] = z_total(p, (1 - zq) * half + turn_zi(e)).astype(BF16)
            quad_copies[p, e] = links.send(quad_send.at[p, e], quad_recv.at[p, e], to_mate(e))

    def pair_stage(p):
        value = z_total(p, pair_z)
        for e in mates:
            quad_copies[p, e].wait_recv()
            value = value + quad_recv[p, e, 1].astype(F32)
        pair_send[p] = value.astype(BF16)
        pair_copies[p] = links.send(pair_send.at[p], pair_recv.at[p], to_pair)

    def last_stage(p):
        value = z_total(p, z) + self_grad[lines(p), :]
        for e in mates:
            value = value + quad_recv[p, e, 0].astype(F32)
        pair_copies[p].wait_recv()
        return value + pair_recv[p].astype(F32)

    for p in range(parts):
        core_stage(p)
    far_stage(0)
    near_stage(0, 0, False)
    near_stage(0, 1, False)

    for copy in wz_copies:
        copy.wait_recv()
    w_part = wz_recv[0]
    for q in range(1, nz):
        w_part = w_part + wz_recv[q]
    wh_send[...] = w_part
    wh_copy = links.send(wh_send, wh_recv, to_zh)

    far_stage(1)
    near_stage(0, 0, True)
    near_stage(0, 1, True)
    near_stage(1, 0, False)
    near_stage(1, 1, False)

    wh_copy.wait_recv()
    w_part = w_part + wh_recv[...]
    wx_recv[x] = w_part
    wx_copies = [links.send(wx_recv.at[x], wx_recv.at[x], to_x(d)) for d in (2, 1, 3)]

    near_stage(1, 0, True)
    near_stage(1, 1, True)
    quad_stage(0)

    for copy in wx_copies:
        copy.wait_recv()
    w_part = wx_recv[0]
    for q in range(1, NX):
        w_part = w_part + wx_recv[q]
    wc_send[...] = w_part
    wc_copy = links.send(wc_send, wc_recv, to_core)

    pair_stage(0)
    quad_stage(1)

    wc_copy.wait_recv()
    w_part = w_part + wc_recv[...]
    gbias_ref[...] = jnp.concatenate(
        [w_part[part : part + 1], w_part[part + 1 : part + 2]], axis=1
    )
    store(gbias_ref, gbias_hbm)
    rows_here = pl.ds(pl.multiple_of(z * part, part), part)
    w_out[y, rows_here] = w_part[:part]
    gz_copies = [
        links.send(w_out.at[y, rows_here], w_out.at[y, rows_here], to_z(d)) for d in range(1, nz)
    ]

    pair_stage(1)
    for copy in gz_copies:
        copy.wait_recv()
    gy_copies = [links.send(w_out.at[y], w_out.at[y], to_y(d)) for d in (2, 1, 3)]
    grad = jnp.concatenate([last_stage(p) for p in range(parts)], axis=0)
    ingrad_ref[...] = jnp.transpose(grad).astype(BF16)
    store(ingrad_ref, ingrad_hbm)

    for copy in gy_copies:
        copy.wait_recv()
    gself_ref[:, :BLK] = w_out[0]
    gself_ref[:, BLK:] = w_out[1]
    gneigh_ref[:, :BLK] = w_out[2]
    gneigh_ref[:, BLK:] = w_out[3]
    store(gself_ref, gself_hbm)
    store(gneigh_ref, gneigh_hbm)
    links.finish()
    for copy in stores:
        copy.wait()


def place(*refs):
    count = len(refs) // 2
    copies = [
        pltpu.make_async_copy(refs[i], refs[count + i], refs[-1].at[i]) for i in range(count)
    ]
    for copy in copies:
        copy.start()
    for copy in copies:
        copy.wait()


def body(
    node_features,
    tile_values,
    tile_rows,
    tile_cols,
    weight_self,
    weight_neighbour,
    node_bias,
    output_grad,
):
    nz = lax.axis_size("row") // (NX * NC)
    half = nz // 2
    n_cols, n_rows = nz * NX * NC, lax.axis_size("col")
    tiles = tile_values.shape[2]
    feat, units = weight_self.shape
    hbm = pl.BlockSpec(memory_space=pltpu.HBM)
    block = (BLK, BLK)
    lines = (2, BLK // 2, BLK)
    part = BLK // nz + 8
    sems = 256
    results = (
        jax.ShapeDtypeStruct((BLK, units), BF16),
        jax.ShapeDtypeStruct((BLK, feat), BF16),
        jax.ShapeDtypeStruct((feat, units), F32),
        jax.ShapeDtypeStruct((feat, units), F32),
        jax.ShapeDtypeStruct((1, units), F32),
    )

    def halves(*lead):
        return pltpu.VMEM((2,) + lead + (BLK // 2, BLK), BF16)

    outs = pl.pallas_call(
        functools.partial(kernel, nz, tiles),
        out_shape=results,
        in_specs=[hbm] * 8,
        out_specs=(hbm,) * 5,
        scratch_shapes=[
            *(pltpu.VMEM(result.shape, result.dtype) for result in results),
            pltpu.VMEM((feat, units), BF16),
            pltpu.VMEM((feat, units), BF16),
            pltpu.VMEM((1, units), F32),
            pltpu.VMEM((BLK, units), BF16),
            pltpu.VMEM((1, tiles), jnp.int32),
            pltpu.VMEM((1, tiles), jnp.int32),
            pltpu.VMEM((16, BLK), jnp.int32),
            pltpu.SMEM((16, BLK), jnp.int32),
            pltpu.VMEM((tiles,) + block, BF16),
            pltpu.VMEM((n_cols,) + block, BF16),
            pltpu.VMEM((tiles,) + block, F32),
            pltpu.VMEM((BLK, units), F32),
            pltpu.VMEM(block, F32),
            halves(3, 2),
            halves(3, 2),
            halves(),
            halves(),
            pltpu.VMEM((n_rows,) + block, BF16),
            halves(NX * nz),
            halves(NX * nz),
            halves(nz),
            halves(nz),
            halves(2, nz),
            halves(2, nz),
            halves(half, 2),
            halves(half, 2),
            halves(),
            halves(),
            pltpu.VMEM((4, BLK + 16, BLK), BF16),
            pltpu.VMEM((4, BLK + 16, BLK), BF16),
            pltpu.VMEM((nz, part, BLK), F32),
            pltpu.VMEM((nz, part, BLK), F32),
            pltpu.VMEM((part, BLK), F32),
            pltpu.VMEM((part, BLK), F32),
            pltpu.VMEM((NX, part, BLK), F32),
            pltpu.VMEM((part, BLK), F32),
            pltpu.VMEM((part, BLK), F32),
            pltpu.VMEM((4,) + block, F32),
            pltpu.SemaphoreType.DMA((9,)),
            pltpu.SemaphoreType.DMA((5,)),
            pltpu.SemaphoreType.DMA((sems,)),
            pltpu.SemaphoreType.DMA((sems,)),
        ],
        compiler_params=pltpu.CompilerParams(
            collective_id=0, has_side_effects=True, vmem_limit_bytes=VMEM_LIMIT
        ),
        cost_estimate=pl.CostEstimate(
            flops=4 * tiles * BLK**3, bytes_accessed=2 * tiles * BLK**2, transcendentals=BLK * units
        ),
    )(
        node_features,
        weight_self,
        weight_neighbour,
        node_bias.reshape(1, units),
        output_grad,
        tile_rows.reshape(1, tiles),
        tile_cols.reshape(1, tiles),
        tile_values,
    )
    outs = pl.pallas_call(
        place,
        out_shape=results,
        in_specs=[hbm] * 5,
        out_specs=(hbm,) * 5,
        scratch_shapes=[pltpu.SemaphoreType.DMA((5,))],
        compiler_params=pltpu.CompilerParams(vmem_limit_bytes=VMEM_LIMIT),
    )(*outs)
    return (*outs[:4], outs[4].reshape(units))


def solution(mesh):
    placed = (
        P(("row", "col"), None),
        P("row", "col", None, None, None),
        P("row", "col", None),
        P("row", "col", None),
        P(),
        P(),
        P(),
        P(("row", "col"), None),
    )
    return jax.shard_map(
        body,
        mesh=mesh,
        in_specs=placed,
        out_specs=(P(("row", "col"), None), P(("row", "col"), None), P(), P(), P()),
        check_vma=False,
    )
```

```python
import functools

import jax
import jax.numpy as jnp
from jax import lax
from jax.experimental import pallas as pl
from jax.experimental.pallas import tpu as pltpu
from jax.sharding import PartitionSpec as P

MESH = pl.DeviceIdType.MESH
BLK = 128
F32 = jnp.float32
BF16 = jnp.bfloat16
VMEM_LIMIT = 64 * 2**20

NX, NC = 4, 2
NY = 4


def dot_nn(a, b):
    return lax.dot_general(a, b, (((1,), (0,)), ((), ())), preferred_element_type=F32)


def dot_nt(a, b):
    return lax.dot_general(a, b, (((1,), (1,)), ((), ())), preferred_element_type=F32)


def dot_tn(a, b):
    return lax.dot_general(a, b, (((0,), (0,)), ((), ())), preferred_element_type=F32)


class Links:
    def __init__(self, send_sems, recv_sems):
        self.send_sems, self.recv_sems, self.copies, self.sent = send_sems, recv_sems, [], 0

    def send(self, src, dst, device_id):
        at = len(self.copies)
        copy = pltpu.make_async_remote_copy(
            src_ref=src,
            dst_ref=dst,
            send_sem=self.send_sems.at[at],
            recv_sem=self.recv_sems.at[at],
            device_id=device_id,
            device_id_type=MESH,
        )
        copy.start()
        self.copies.append(copy)
        return copy

    def finish(self, upto=None):
        upto = len(self.copies) if upto is None else upto
        for copy in self.copies[self.sent : upto]:
            copy.wait_send()
        self.sent = max(self.sent, upto)


def send_sorted(block, carried, n_blocks, index, at):
    tiles = block.shape[1]
    shape = (tiles, tiles)
    down = lax.broadcasted_iota(jnp.int32, shape, 0)
    across = lax.broadcasted_iota(jnp.int32, shape, 1)

    def turned(line):
        return jnp.sum(jnp.where(down == across, line, 0), axis=1, keepdims=True)

    block_down, carried_down = turned(block), turned(carried)
    before = (block < block_down) | ((block == block_down) & (across < down))
    rank = jnp.sum(before.astype(jnp.int32), axis=1, keepdims=True)
    goes_on = jnp.sum(
        ((block == block_down) & (across < down)).astype(jnp.int32), axis=1, keepdims=True
    )
    hot = rank == across

    def sorted_line(values):
        return jnp.sum(jnp.where(hot, values, 0), axis=0, keepdims=True)

    index[at : at + 1, :tiles] = sorted_line(down)
    index[at + 1 : at + 2, :tiles] = sorted_line(carried_down)
    index[at + 2 : at + 3, :tiles] = sorted_line(jnp.minimum(goes_on, 1))
    ids = lax.broadcasted_iota(jnp.int32, (tiles, n_blocks), 1)
    up_to = jnp.sum((block_down <= ids).astype(jnp.int32), axis=0, keepdims=True)
    held = jnp.sum((block_down == ids).astype(jnp.int32), axis=0, keepdims=True)
    index[at + 3 : at + 4, :n_blocks] = jnp.where(held > 0, up_to - 1, tiles)


def kernel(
    nz,
    tiles,
    x_hbm,
    ws_hbm,
    wn_hbm,
    bias_hbm,
    og_hbm,
    rows_hbm,
    cols_hbm,
    tiles_hbm,
    out_hbm,
    ingrad_hbm,
    gself_hbm,
    gneigh_hbm,
    gbias_hbm,
    out_ref,
    ingrad_ref,
    gself_ref,
    gneigh_ref,
    gbias_ref,
    ws_ref,
    wn_ref,
    bias_ref,
    og_ref,
    x_their,
    rows_ref,
    cols_ref,
    index_buf,
    index,
    tile_buf,
    panels,
    runs,
    self_pre,
    self_grad,
    y_send,
    y_recv,
    zh_send,
    zh_recv,
    gt,
    core_send,
    core_recv,
    far_send,
    far_recv,
    near_send,
    near_recv,
    quad_send,
    quad_recv,
    pair_send,
    pair_recv,
    wy_send,
    wy_recv,
    wz_send,
    wz_recv,
    wh_send,
    wh_recv,
    wx_recv,
    wc_send,
    wc_recv,
    w_out,
    load_sems,
    store_sems,
    send_sems,
    recv_sems,
):
    half = nz // 2
    n_cols = nz * NX * NC
    n_rows = 2 * NY
    row = lax.axis_index("row")
    col = lax.axis_index("col")
    core = lax.rem(row, NC)
    x = lax.rem(row // NC, NX)
    z = row // (NC * NX)
    zq = z // half
    zi = lax.rem(z, half)
    y = lax.rem(col, NY)
    zh = col // NY
    other = 1 - core

    def at_row(z_to, x_to, core_to):
        return {"row": (z_to * NX + x_to) * NC + core_to, "col": col}

    def at_col(zh_to, y_to):
        return {"row": row, "col": zh_to * NY + y_to}

    def turn_z(d):
        return lax.rem(z + d, nz)

    def turn_zi(d):
        return lax.rem(zi + d, half)

    def turn_x(d):
        return lax.rem(x + d, NX)

    def turn_y(d):
        return lax.rem(y + d, NY)

    def to_z(d):
        return at_row(turn_z(d), x, core)

    def to_mate(e):
        return at_row(zq * half + turn_zi(e), x, core)

    def to_x(d):
        return at_row(z, turn_x(d), core)

    def to_y(d):
        return at_col(zh, turn_y(d))

    to_pair = at_row((1 - zq) * half + zi, x, core)
    to_core = at_row(z, x, other)
    to_zh = at_col(1 - zh, y)
    mates = [e for e in (1, half - 1) if e] + list(range(2, half - 1))
    mates = list(dict.fromkeys(mates))

    ord_r, pan, keep_r, end_r, ord_c, grow, keep_c, end_c = range(8)

    def slot(core_of, x_of, z_of):
        return (core_of * NX + x_of) * nz + z_of

    own = slot(core, x, z)
    loads = []
    for src, dst in (
        (x_hbm, panels.at[own]),
        (rows_hbm, rows_ref),
        (cols_hbm, cols_ref),
        (ws_hbm, ws_ref),
        (bias_hbm, bias_ref),
        (tiles_hbm.at[0, 0], tile_buf),
        (wn_hbm, wn_ref),
        (og_hbm, og_ref.at[0]),
    ):
        loads.append(pltpu.make_async_copy(src, dst, load_sems.at[len(loads)]))
        loads[-1].start()
    load_x, load_rows, load_cols, load_ws, load_bias, load_tiles, load_wn, load_og = loads

    barrier = pltpu.get_barrier_semaphore()
    partners = [to_z(d) for d in range(1, nz)] + [to_x(d) for d in range(1, NX)]
    partners += [to_y(d) for d in range(1, NY)] + [to_core, to_zh]
    for partner in partners:
        pl.semaphore_signal(barrier, inc=1, device_id=partner, device_id_type=MESH)
    load_x.wait()
    pl.semaphore_wait(barrier, len(partners))

    links = Links(send_sems, recv_sems)
    stores = []

    def store(src, dst):
        stores.append(pltpu.make_async_copy(src, dst, store_sems.at[len(stores)]))
        stores[-1].start()

    def panel_to(slot_at, device_id):
        return links.send(panels.at[slot_at], panels.at[slot_at], device_id)

    pair_copy = panel_to(own, to_pair)
    z_copies = {e: panel_to(own, to_mate(e)) for e in mates}
    pair_z = (1 - zq) * half + zi
    relayed = {}

    def mate_z(e, q):
        return q * half + turn_zi(half - e)

    arrivals = [(z, None)] + [(mate_z(e, zq), z_copies[e]) for e in mates[:2]]
    arrivals += [(pair_z, pair_copy)] + [(mate_z(e, zq), z_copies[e]) for e in mates[2:]]
    arrivals += [(mate_z(e, 1 - zq), e) for e in mates]
    plus, minus, far, crossed = {}, {}, {}, []

    def cross(slot_at):
        crossed.append(panel_to(slot_at, to_core))

    def own_step(i):
        z_of, copy = arrivals[i]
        here = slot(core, x, z_of)
        if copy is not None:
            (relayed[copy] if isinstance(copy, int) else copy).wait_recv()
        if copy is pair_copy:
            for e in mates:
                relayed[e] = panel_to(here, to_mate(e))
        plus[i] = panel_to(here, to_x(1))
        minus[i] = panel_to(here, to_x(NX - 1))
        cross(here)

    def near_step(i):
        z_of = arrivals[i][0]
        from_minus = slot(core, turn_x(NX - 1), z_of)
        from_plus = slot(core, turn_x(1), z_of)
        plus[i].wait_recv()
        if i % 2 == 0:
            far[i] = panel_to(from_minus, to_x(1))
        cross(from_minus)
        minus[i].wait_recv()
        if i % 2 == 1:
            far[i] = panel_to(from_plus, to_x(NX - 1))
        cross(from_plus)

    def far_step(i):
        far[i].wait_recv()
        cross(slot(core, turn_x(2), arrivals[i][0]))

    def prepare():
        load_rows.wait()
        load_cols.wait()
        rows = rows_ref[...]
        cols = cols_ref[...]
        slots = slot(cols & (NC - 1), (cols // NC) & (NX - 1), cols // (NC * NX))
        send_sorted(rows, slots, n_rows, index_buf, 0)
        send_sorted(slots, (rows & (NY - 1)) * 2 + rows // NY, n_cols, index_buf, 4)
        runs[tiles] = jnp.zeros((BLK, BLK), F32)
        index_copy = pltpu.make_async_copy(index_buf, index, load_sems.at[len(loads)])
        index_copy.start()
        load_ws.wait()
        load_bias.wait()
        self_pre[0] = dot_nn(panels[own], ws_ref[...]) + bias_ref[...]
        index_copy.wait()

    for i in range(nz + 2):
        if i < nz:
            own_step(i)
        if i == 0:
            prepare()
        if i == nz - 1:
            load_og.wait()
            x_copy = links.send(panels.at[own], x_their, to_zh)
            og_copy = links.send(og_ref.at[0], og_ref.at[1], to_zh)
        if 0 <= i - 1 < nz:
            near_step(i - 1)
        if 0 <= i - 2 < nz:
            far_step(i - 2)
    load_tiles.wait()
    load_wn.wait()
    for copy in crossed:
        copy.wait_recv()
    gathered = len(links.copies)

    step = 8

    def collect(k, acc):
        for u in range(step):
            n = k * step + u
            term = dot_nn(tile_buf[index[ord_r, n]], panels[index[pan, n]])
            acc = acc * index[keep_r, n].astype(F32) + term
            runs[n] = acc
        return acc

    lax.fori_loop(0, tiles // step, collect, jnp.zeros((BLK, BLK), F32))

    parts = 2
    width = BLK // parts

    def lines(p):
        return slice(p * width, (p + 1) * width)

    def row_sum(r, p):
        return runs[index[end_r, r], lines(p), :]

    y_copies, zh_copies = {}, {}
    for p in range(parts):
        for d in (2, 1, 3):
            for h in range(2):
                y_send[p, d - 1, h] = row_sum(h * NY + turn_y(d), p).astype(BF16)
            y_copies[p, d] = links.send(y_send.at[p, d - 1], y_recv.at[p, d - 1], to_y(d))
    x_copy.wait_recv()
    self_pre[1] = dot_nn(x_their[...], ws_ref[...]) + bias_ref[...]
    og_copy.wait_recv()
    links.finish(gathered)
    sides = (zh, 1 - zh)
    totals = {}
    for p in range(parts):
        for d in (1, 3, 2):
            y_copies[p, d].wait_recv()
        for k, h in enumerate(sides):
            value = row_sum(h * NY + y, p)
            for d in (1, 3, 2):
                value = value + y_recv[p, d - 1, h].astype(F32)
            totals[k, p] = value
            zh_send[p, h] = value.astype(BF16)
        zh_copies[p] = links.send(zh_send.at[p], zh_recv.at[p], to_zh)
    for p in range(parts):
        zh_copies[p].wait_recv()
        for k, h in enumerate(sides):
            totals[k, p] = (totals[k, p] + zh_recv[p, h].astype(F32)).astype(BF16)

    def layer(k):
        sums = jnp.concatenate([totals[k, p] for p in range(parts)], axis=0)
        pre = self_pre[k] + dot_nn(sums, wn_ref[...])
        sig = 1.0 / (1.0 + jnp.exp(-pre))
        slope = sig * (1.0 + pre * (1.0 - sig))
        return sums, pre * sig, (og_ref[k].astype(F32) * slope).astype(BF16)

    sums, activated, pre_grad = layer(0)
    gt[y * 2 + zh] = dot_nt(wn_ref[...], pre_grad).astype(BF16)
    gt[y * 2 + 1 - zh] = dot_nt(wn_ref[...], layer(1)[2]).astype(BF16)
    gt_here = gt.at[pl.ds(y * 2, 2)]
    gt_copies = [links.send(gt_here, gt_here, to_y(d)) for d in (2, 1, 3)]
    out_ref[...] = activated.astype(BF16)
    store(out_ref, out_hbm)
    self_grad[...] = dot_nt(ws_ref[...], pre_grad)

    wide_self = dot_tn(panels[own], pre_grad).astype(BF16)
    wide_neigh = dot_tn(sums, pre_grad).astype(BF16)
    for q, block in enumerate(
        (wide_self[:, :BLK], wide_self[:, BLK:], wide_neigh[:, :BLK], wide_neigh[:, BLK:])
    ):
        wy_send[q, :BLK] = block
    bias_sum = jnp.sum(pre_grad.astype(F32), axis=0, keepdims=True)
    spot = lax.broadcasted_iota(jnp.int32, (16, BLK), 0)
    bias_rows = jnp.where(
        spot == 0, bias_sum[:, :BLK], jnp.where(spot == 1, bias_sum[:, BLK:], 0.0)
    ).astype(BF16)
    for q in range(4):
        wy_send[q, BLK:] = bias_rows
    wy_recv[y] = wy_send[y]

    wy_copies = [links.send(wy_send.at[turn_y(d)], wy_recv.at[y], to_y(d)) for d in (2, 1, 3)]
    links.finish(len(links.copies) - 6)
    for copy in gt_copies:
        copy.wait_recv()

    def spread(k, acc):
        for u in range(step):
            n = k * step + u
            term = dot_nn(gt[index[grow, n]], tile_buf[index[ord_c, n]])
            acc = acc * index[keep_c, n].astype(F32) + term
            runs[n] = acc
        return acc

    steps = tiles // step
    acc = lax.fori_loop(0, steps // 2, spread, jnp.zeros((BLK, BLK), F32))

    for copy in wy_copies:
        copy.wait_recv()
    w_sum = wy_recv[0].astype(F32)
    for q in range(1, NY):
        w_sum = w_sum + wy_recv[q].astype(F32)
    part = BLK // nz
    for q in range(nz):
        wz_send[q, :part] = w_sum[q * part : (q + 1) * part]
        wz_send[q, part:] = w_sum[BLK : BLK + 8]
    wz_recv[z] = wz_send[z]
    wz_copies = [links.send(wz_send.at[turn_z(d)], wz_recv.at[z], to_z(d)) for d in range(1, nz)]

    lax.fori_loop(steps // 2, steps, spread, acc)

    def chunk(core_of, d):
        return slot(core_of, turn_x(d), 0)

    def col_sum(c, p):
        return runs[index[end_c, c], lines(p), :]

    def paired(p, d, i):
        return col_sum(chunk(core, d) + i, p) + core_recv[p, turn_x(d) * nz + i].astype(F32)

    lower, upper = pl.ds(0, half), pl.ds(half, half)
    core_copies, far_copies, near_copies, quad_copies, pair_copies = {}, {}, {}, {}, {}

    def core_stage(p):
        for d in (2, 1, 3, 0):
            base, first = chunk(other, d), turn_x(d) * nz
            for i in range(nz):
                core_send[p, first + i] = col_sum(base + i, p).astype(BF16)
            blocks = pl.ds(first, nz)
            core_copies[p, d] = links.send(
                core_send.at[p, blocks], core_recv.at[p, blocks], to_core
            )

    def far_stage(p):
        core_copies[p, 2].wait_recv()
        for i in range(nz):
            far_send[p, i] = paired(p, 2, i).astype(BF16)
        far_copies[p, 0] = links.send(far_send.at[p, lower], far_recv.at[p, lower], to_x(1))
        far_copies[p, 1] = links.send(far_send.at[p, upper], far_recv.at[p, upper], to_x(NX - 1))

    def near_stage(p, way, with_far):
        d = (1, NX - 1)[way]
        if with_far:
            far_copies[p, way].wait_recv()
        else:
            core_copies[p, d].wait_recv()
        first = half * (way if with_far else 1 - way)
        for i in range(first, first + half):
            value = paired(p, d, i)
            if with_far:
                value = value + far_recv[p, i].astype(F32)
            near_send[p, way, i] = value.astype(BF16)
        blocks = pl.ds(first, half)
        near_copies[p, way, with_far] = links.send(
            near_send.at[p, way, blocks], near_recv.at[p, way, blocks], to_x(d)
        )

    def z_total(p, i):
        return (
            paired(p, 0, i) + near_recv[p, 0, i].astype(F32) + near_recv[p, 1, i].astype(F32)
        )

    def quad_stage(p):
        core_copies[p, 0].wait_recv()
        for way in range(2):
            for with_far in (False, True):
                near_copies[p, way, with_far].wait_recv()
        for e in mates:
            quad_send[p, e, 0] = z_total(p, zq * half + turn_zi(e)).astype(BF16)
            quad_send[p, e, 1] = z_total(p, (1 - zq) * half + turn_zi(e)).astype(BF16)
            quad_copies[p, e] = links.send(quad_send.at[p, e], quad_recv.at[p, e], to_mate(e))

    def pair_stage(p):
        value = z_total(p, pair_z)
        for e in mates:
            quad_copies[p, e].wait_recv()
            value = value + quad_recv[p, e, 1].astype(F32)
        pair_send[p] = value.astype(BF16)
        pair_copies[p] = links.send(pair_send.at[p], pair_recv.at[p], to_pair)

    def last_stage(p):
        value = z_total(p, z) + self_grad[lines(p), :]
        for e in mates:
            value = value + quad_recv[p, e, 0].astype(F32)
        pair_copies[p].wait_recv()
        return value + pair_recv[p].astype(F32)

    for p in range(parts):
        core_stage(p)
    far_stage(0)
    near_stage(0, 0, False)
    near_stage(0, 1, False)

    for copy in wz_copies:
        copy.wait_recv()
    w_part = wz_recv[0]
    for q in range(1, nz):
        w_part = w_part + wz_recv[q]
    wh_send[...] = w_part
    wh_copy = links.send(wh_send, wh_recv, to_zh)

    far_stage(1)
    near_stage(0, 0, True)
    near_stage(0, 1, True)
    near_stage(1, 0, False)
    near_stage(1, 1, False)

    wh_copy.wait_recv()
    w_part = w_part + wh_recv[...]
    wx_recv[x] = w_part
    wx_copies = [links.send(wx_recv.at[x], wx_recv.at[x], to_x(d)) for d in (2, 1, 3)]

    near_stage(1, 0, True)
    near_stage(1, 1, True)
    quad_stage(0)

    for copy in wx_copies:
        copy.wait_recv()
    w_part = wx_recv[0]
    for q in range(1, NX):
        w_part = w_part + wx_recv[q]
    wc_send[...] = w_part
    wc_copy = links.send(wc_send, wc_recv, to_core)

    pair_stage(0)
    quad_stage(1)

    wc_copy.wait_recv()
    w_part = w_part + wc_recv[...]
    gbias_ref[...] = jnp.concatenate(
        [w_part[part : part + 1], w_part[part + 1 : part + 2]], axis=1
    )
    store(gbias_ref, gbias_hbm)
    rows_here = pl.ds(pl.multiple_of(z * part, part), part)
    w_out[y, rows_here] = w_part[:part]
    gz_copies = [
        links.send(w_out.at[y, rows_here], w_out.at[y, rows_here], to_z(d)) for d in range(1, nz)
    ]

    pair_stage(1)
    links.finish(len(links.copies) - nz)
    for copy in gz_copies:
        copy.wait_recv()
    gy_copies = [links.send(w_out.at[y], w_out.at[y], to_y(d)) for d in (2, 1, 3)]
    grad = jnp.concatenate([last_stage(p) for p in range(parts)], axis=0)
    ingrad_ref[...] = jnp.transpose(grad).astype(BF16)
    store(ingrad_ref, ingrad_hbm)

    for copy in gy_copies:
        copy.wait_recv()
    gself_ref[:, :BLK] = w_out[0]
    gself_ref[:, BLK:] = w_out[1]
    gneigh_ref[:, :BLK] = w_out[2]
    gneigh_ref[:, BLK:] = w_out[3]
    store(gself_ref, gself_hbm)
    store(gneigh_ref, gneigh_hbm)
    links.finish()
    for copy in stores:
        copy.wait()


def place(*refs):
    count = (len(refs) - 2) // 3
    sources, targets, held = (refs[i * count : (i + 1) * count] for i in range(3))
    ins, outs = refs[-2:]
    moves = []
    for i in range(count):
        moves.append(
            (
                pltpu.make_async_copy(sources[i], held[i], ins.at[i]),
                pltpu.make_async_copy(held[i], targets[i], outs.at[i]),
            )
        )
        moves[-1][0].start()
    for into, out in moves:
        into.wait()
        out.start()
    for _, out in moves:
        out.wait()


def body(
    node_features,
    tile_values,
    tile_rows,
    tile_cols,
    weight_self,
    weight_neighbour,
    node_bias,
    output_grad,
):
    nz = lax.axis_size("row") // (NX * NC)
    half = nz // 2
    n_cols, n_rows = nz * NX * NC, lax.axis_size("col")
    tiles = tile_values.shape[2]
    feat, units = weight_self.shape
    hbm = pl.BlockSpec(memory_space=pltpu.HBM)
    block = (BLK, BLK)
    lines = (2, BLK // 2, BLK)
    part = BLK // nz + 8
    sems = 256
    results = (
        jax.ShapeDtypeStruct((BLK, units), BF16),
        jax.ShapeDtypeStruct((BLK, feat), BF16),
        jax.ShapeDtypeStruct((feat, units), F32),
        jax.ShapeDtypeStruct((feat, units), F32),
        jax.ShapeDtypeStruct((1, units), F32),
    )

    def halves(*lead):
        return pltpu.VMEM((2,) + lead + (BLK // 2, BLK), BF16)

    outs = pl.pallas_call(
        functools.partial(kernel, nz, tiles),
        out_shape=results,
        in_specs=[hbm] * 8,
        out_specs=(hbm,) * 5,
        scratch_shapes=[
            *(pltpu.VMEM(result.shape, result.dtype) for result in results),
            pltpu.VMEM((feat, units), BF16),
            pltpu.VMEM((feat, units), BF16),
            pltpu.VMEM((1, units), F32),
            pltpu.VMEM((2, BLK, units), BF16),
            pltpu.VMEM((BLK, feat), BF16),
            pltpu.VMEM((1, tiles), jnp.int32),
            pltpu.VMEM((1, tiles), jnp.int32),
            pltpu.VMEM((16, BLK), jnp.int32),
            pltpu.SMEM((16, BLK), jnp.int32),
            pltpu.VMEM((tiles,) + block, BF16),
            pltpu.VMEM((n_cols,) + block, BF16),
            pltpu.VMEM((tiles + 1,) + block, F32),
            pltpu.VMEM((2, BLK, units), F32),
            pltpu.VMEM(block, F32),
            halves(3, 2),
            halves(3, 2),
            halves(2),
            halves(2),
            pltpu.VMEM((n_rows,) + block, BF16),
            halves(NX * nz),
            halves(NX * nz),
            halves(nz),
            halves(nz),
            halves(2, nz),
            halves(2, nz),
            halves(half, 2),
            halves(half, 2),
            halves(),
            halves(),
            pltpu.VMEM((4, BLK + 16, BLK), BF16),
            pltpu.VMEM((4, BLK + 16, BLK), BF16),
            pltpu.VMEM((nz, part, BLK), F32),
            pltpu.VMEM((nz, part, BLK), F32),
            pltpu.VMEM((part, BLK), F32),
            pltpu.VMEM((part, BLK), F32),
            pltpu.VMEM((NX, part, BLK), F32),
            pltpu.VMEM((part, BLK), F32),
            pltpu.VMEM((part, BLK), F32),
            pltpu.VMEM((4,) + block, F32),
            pltpu.SemaphoreType.DMA((9,)),
            pltpu.SemaphoreType.DMA((5,)),
            pltpu.SemaphoreType.DMA((sems,)),
            pltpu.SemaphoreType.DMA((sems,)),
        ],
        compiler_params=pltpu.CompilerParams(
            collective_id=0, has_side_effects=True, vmem_limit_bytes=VMEM_LIMIT
        ),
        cost_estimate=pl.CostEstimate(
            flops=4 * tiles * BLK**3, bytes_accessed=2 * tiles * BLK**2, transcendentals=BLK * units
        ),
    )(
        node_features,
        weight_self,
        weight_neighbour,
        node_bias.reshape(1, units),
        output_grad,
        tile_rows.reshape(1, tiles),
        tile_cols.reshape(1, tiles),
        tile_values,
    )
    outs = pl.pallas_call(
        place,
        out_shape=results,
        in_specs=[hbm] * 5,
        out_specs=(hbm,) * 5,
        scratch_shapes=[
            *(pltpu.VMEM(result.shape, result.dtype) for result in results),
            pltpu.SemaphoreType.DMA((5,)),
            pltpu.SemaphoreType.DMA((5,)),
        ],
        compiler_params=pltpu.CompilerParams(vmem_limit_bytes=VMEM_LIMIT),
    )(*outs)
    return (*outs[:4], outs[4].reshape(units))


def solution(mesh):
    placed = (
        P(("row", "col"), None),
        P("row", "col", None, None, None),
        P("row", "col", None),
        P("row", "col", None),
        P(),
        P(),
        P(),
        P(("row", "col"), None),
    )
    return jax.shard_map(
        body,
        mesh=mesh,
        in_specs=placed,
        out_specs=(P(("row", "col"), None), P(("row", "col"), None), P(), P(), P()),
        check_vma=False,
    )
```

```python
import functools

import jax
import jax.numpy as jnp
from jax import lax
from jax.experimental import pallas as pl
from jax.experimental.pallas import tpu as pltpu
from jax.sharding import PartitionSpec as P

MESH = pl.DeviceIdType.MESH
BLK = 128
F32 = jnp.float32
BF16 = jnp.bfloat16
VMEM_LIMIT = 64 * 2**20

NX, NC = 4, 2
NY = 4


def dot_nn(a, b):
    return lax.dot_general(a, b, (((1,), (0,)), ((), ())), preferred_element_type=F32)


def dot_nt(a, b):
    return lax.dot_general(a, b, (((1,), (1,)), ((), ())), preferred_element_type=F32)


def dot_tn(a, b):
    return lax.dot_general(a, b, (((0,), (0,)), ((), ())), preferred_element_type=F32)


class Links:
    def __init__(self, send_sems, recv_sems):
        self.send_sems, self.recv_sems, self.copies, self.sent = send_sems, recv_sems, [], 0

    def send(self, src, dst, device_id):
        at = len(self.copies)
        copy = pltpu.make_async_remote_copy(
            src_ref=src,
            dst_ref=dst,
            send_sem=self.send_sems.at[at],
            recv_sem=self.recv_sems.at[at],
            device_id=device_id,
            device_id_type=MESH,
        )
        copy.start()
        self.copies.append(copy)
        return copy

    def finish(self, upto=None):
        upto = len(self.copies) if upto is None else upto
        for copy in self.copies[self.sent : upto]:
            copy.wait_send()
        self.sent = max(self.sent, upto)


def iota(shape, axis):
    return lax.broadcasted_iota(jnp.int32, shape, axis)


def turned(line):
    n = line.shape[1]
    diagonal = iota((n, n), 0) == iota((n, n), 1)
    return jnp.sum(jnp.where(diagonal, line, 0), axis=1, keepdims=True)


def laid(column):
    n = column.shape[0]
    diagonal = iota((n, n), 0) == iota((n, n), 1)
    return jnp.sum(jnp.where(diagonal, column, 0), axis=0, keepdims=True)


def order_pairs(block, carried, gate, n_blocks, index, at):
    tiles = block.shape[1]
    places = tiles + n_blocks
    shape = (tiles, tiles)
    block_down = turned(block)
    earlier = (block == block_down) & (iota(shape, 1) < iota(shape, 0))
    rank = jnp.sum(earlier.astype(jnp.int32), axis=1, keepdims=True)
    ids = iota((tiles, n_blocks), 1)
    held = jnp.sum((block_down == ids).astype(jnp.int32), axis=0, keepdims=True)
    padded = ((held + 1) // 2) * 2
    base = jnp.sum(jnp.where(ids < block_down, padded, 0), axis=1, keepdims=True)
    place = base + rank
    hot = place == iota((tiles, places), 1)

    def by_place(column):
        return jnp.sum(jnp.where(hot, column, 0), axis=0, keepdims=True)

    index[at : at + 1, :places] = tiles - by_place(tiles - iota((tiles, 1), 0))
    index[at + 1 : at + 2, :places] = by_place(turned(carried))
    index[at + 2 : at + 3, :places] = by_place(jnp.minimum(rank // 2, 1))
    index[at + 3 : at + 4, :places] = by_place(gate(block_down))
    small = (n_blocks, n_blocks)
    up_to = jnp.where(iota(small, 0) <= iota(small, 1), turned(padded), 0)
    last = jnp.sum(up_to, axis=0, keepdims=True) // 2 - 1
    index[at + 4 : at + 5, :n_blocks] = jnp.where(held > 0, last, tiles)
    return laid(place)


def order_tiles(block, carried, n_blocks, index, at):
    tiles = block.shape[1]
    shape = (tiles, tiles)
    block_down = turned(block)
    earlier = (block == block_down) & (iota(shape, 1) < iota(shape, 0))
    before = (block < block_down) | earlier
    place = jnp.sum(before.astype(jnp.int32), axis=1, keepdims=True)
    rank = jnp.sum(earlier.astype(jnp.int32), axis=1, keepdims=True)
    hot = place == iota(shape, 1)

    def by_place(column):
        return jnp.sum(jnp.where(hot, column, 0), axis=0, keepdims=True)

    index[at : at + 1, :tiles] = by_place(turned(carried))
    index[at + 1 : at + 2, :tiles] = by_place(jnp.minimum(rank, 1))
    ids = iota((tiles, n_blocks), 1)
    up_to = jnp.sum((block_down <= ids).astype(jnp.int32), axis=0, keepdims=True)
    held = jnp.sum((block_down == ids).astype(jnp.int32), axis=0, keepdims=True)
    index[at + 2 : at + 3, :n_blocks] = jnp.where(held > 0, up_to - 1, tiles)


def kernel(
    nz,
    tiles,
    x_hbm,
    ws_hbm,
    wn_hbm,
    bias_hbm,
    og_hbm,
    rows_hbm,
    cols_hbm,
    tiles_hbm,
    out_hbm,
    ingrad_hbm,
    gself_hbm,
    gneigh_hbm,
    gbias_hbm,
    out_ref,
    ingrad_ref,
    gself_ref,
    gneigh_ref,
    gbias_ref,
    ws_ref,
    wn_ref,
    bias_ref,
    og_ref,
    x_their,
    rows_ref,
    cols_ref,
    index_buf,
    index,
    tile_buf,
    panels,
    runs,
    products,
    self_pre,
    self_grad,
    y_send,
    y_recv,
    zh_send,
    zh_recv,
    gt,
    core_send,
    core_recv,
    far_send,
    far_recv,
    near_send,
    near_recv,
    quad_send,
    quad_recv,
    pair_send,
    pair_recv,
    wy_send,
    wy_recv,
    wz_send,
    wz_recv,
    wh_send,
    wh_recv,
    wx_recv,
    wc_send,
    wc_recv,
    w_out,
    load_sems,
    store_sems,
    send_sems,
    recv_sems,
):
    half = nz // 2
    n_cols = nz * NX * NC
    n_rows = 2 * NY
    row = lax.axis_index("row")
    col = lax.axis_index("col")
    core = lax.rem(row, NC)
    x = lax.rem(row // NC, NX)
    z = row // (NC * NX)
    zq = z // half
    zi = lax.rem(z, half)
    y = lax.rem(col, NY)
    zh = col // NY
    other = 1 - core

    def at_row(z_to, x_to, core_to):
        return {"row": (z_to * NX + x_to) * NC + core_to, "col": col}

    def at_col(zh_to, y_to):
        return {"row": row, "col": zh_to * NY + y_to}

    def turn_z(d):
        return lax.rem(z + d, nz)

    def turn_zi(d):
        return lax.rem(zi + d, half)

    def turn_x(d):
        return lax.rem(x + d, NX)

    def turn_y(d):
        return lax.rem(y + d, NY)

    def to_z(d):
        return at_row(turn_z(d), x, core)

    def to_mate(e):
        return at_row(zq * half + turn_zi(e), x, core)

    def to_x(d):
        return at_row(z, turn_x(d), core)

    def to_y(d):
        return at_col(zh, turn_y(d))

    to_pair = at_row((1 - zq) * half + zi, x, core)
    to_core = at_row(z, x, other)
    to_zh = at_col(1 - zh, y)
    mates = [e for e in (1, half - 1) if e] + list(range(2, half - 1))
    mates = list(dict.fromkeys(mates))

    ord_r, pan, keep_r, grow, end_r, made, keep_c, end_c = range(8)

    def slot(core_of, x_of, z_of):
        return (core_of * NX + x_of) * nz + z_of

    own = slot(core, x, z)
    loads = []
    for src, dst in (
        (x_hbm, panels.at[own]),
        (rows_hbm, rows_ref),
        (cols_hbm, cols_ref),
        (ws_hbm, ws_ref),
        (bias_hbm, bias_ref),
        (tiles_hbm.at[0, 0], tile_buf.at[pl.ds(0, tiles)]),
        (wn_hbm, wn_ref),
        (og_hbm, og_ref.at[0]),
    ):
        loads.append(pltpu.make_async_copy(src, dst, load_sems.at[len(loads)]))
        loads[-1].start()
    load_x, load_rows, load_cols, load_ws, load_bias, load_tiles, load_wn, load_og = loads

    barrier = pltpu.get_barrier_semaphore()
    partners = [to_z(d) for d in range(1, nz)] + [to_x(d) for d in range(1, NX)]
    partners += [to_y(d) for d in range(1, NY)] + [to_core, to_zh]
    for partner in partners:
        pl.semaphore_signal(barrier, inc=1, device_id=partner, device_id_type=MESH)
    load_x.wait()
    pl.semaphore_wait(barrier, len(partners))

    links = Links(send_sems, recv_sems)
    stores = []

    def store(src, dst):
        stores.append(pltpu.make_async_copy(src, dst, store_sems.at[len(stores)]))
        stores[-1].start()

    def panel_to(slot_at, device_id):
        return links.send(panels.at[slot_at], panels.at[slot_at], device_id)

    pair_copy = panel_to(own, to_pair)
    z_copies = {e: panel_to(own, to_mate(e)) for e in mates}
    pair_z = (1 - zq) * half + zi
    relayed = {}

    def mate_z(e, q):
        return q * half + turn_zi(half - e)

    arrivals = [(z, None)] + [(mate_z(e, zq), z_copies[e]) for e in mates[:2]]
    arrivals += [(pair_z, pair_copy)] + [(mate_z(e, zq), z_copies[e]) for e in mates[2:]]
    arrivals += [(mate_z(e, 1 - zq), e) for e in mates]
    plus, minus, far, crossed = {}, {}, {}, []

    def cross(slot_at):
        crossed.append(panel_to(slot_at, to_core))

    def own_step(i):
        z_of, copy = arrivals[i]
        here = slot(core, x, z_of)
        if copy is not None:
            (relayed[copy] if isinstance(copy, int) else copy).wait_recv()
        if copy is pair_copy:
            for e in mates:
                relayed[e] = panel_to(here, to_mate(e))
        plus[i] = panel_to(here, to_x(1))
        minus[i] = panel_to(here, to_x(NX - 1))
        cross(here)

    def near_step(i):
        z_of = arrivals[i][0]
        from_minus = slot(core, turn_x(NX - 1), z_of)
        from_plus = slot(core, turn_x(1), z_of)
        plus[i].wait_recv()
        if i % 2 == 0:
            far[i] = panel_to(from_minus, to_x(1))
        cross(from_minus)
        minus[i].wait_recv()
        if i % 2 == 1:
            far[i] = panel_to(from_plus, to_x(NX - 1))
        cross(from_plus)

    def far_step(i):
        far[i].wait_recv()
        cross(slot(core, turn_x(2), arrivals[i][0]))

    def prepare():
        load_rows.wait()
        load_cols.wait()
        rows = rows_ref[...]
        cols = cols_ref[...]
        slots = slot(cols & (NC - 1), (cols // NC) & (NX - 1), cols // (NC * NX))
        place = order_pairs(
            rows, slots, lambda r: (r & (NY - 1)) * 2 + r // NY, n_rows, index_buf, 0
        )
        order_tiles(slots, place, n_cols, index_buf, 5)
        runs[tiles] = jnp.zeros((BLK, BLK), F32)
        tile_buf[tiles] = jnp.zeros((BLK, BLK), BF16)
        index_copy = pltpu.make_async_copy(index_buf, index, load_sems.at[len(loads)])
        index_copy.start()
        load_ws.wait()
        load_bias.wait()
        self_pre[0] = dot_nn(panels[own], ws_ref[...]) + bias_ref[...]
        index_copy.wait()

    for i in range(nz + 2):
        if i < nz:
            own_step(i)
        if i == 0:
            prepare()
        if i == nz - 1:
            load_og.wait()
            x_copy = links.send(panels.at[own], x_their, to_zh)
            og_copy = links.send(og_ref.at[0], og_ref.at[1], to_zh)
        if 0 <= i - 1 < nz:
            near_step(i - 1)
        if 0 <= i - 2 < nz:
            far_step(i - 2)
    load_tiles.wait()
    load_wn.wait()
    for copy in crossed:
        copy.wait_recv()
    gathered = len(links.copies)

    n_pairs = (tiles + n_rows) // 2
    step = 4

    def collect(k, acc):
        for u in range(step):
            n = k * step + u
            here = [2 * n, 2 * n + 1]
            left = jnp.concatenate([tile_buf[index[ord_r, i]] for i in here], axis=1)
            right = jnp.concatenate([panels[index[pan, i]] for i in here], axis=0)
            acc = acc * index[keep_r, 2 * n].astype(F32) + dot_nn(left, right)
            runs[n] = acc
        return acc

    lax.fori_loop(0, n_pairs // step, collect, jnp.zeros((BLK, BLK), F32))

    parts = 2
    width = BLK // parts

    def lines(p):
        return slice(p * width, (p + 1) * width)

    def row_sum(r, p):
        return runs[index[end_r, r], lines(p), :]

    y_copies, zh_copies = {}, {}
    for p in range(parts):
        for d in (2, 1, 3):
            for h in range(2):
                y_send[p, d - 1, h] = row_sum(h * NY + turn_y(d), p).astype(BF16)
            y_copies[p, d] = links.send(y_send.at[p, d - 1], y_recv.at[p, d - 1], to_y(d))
    x_copy.wait_recv()
    self_pre[1] = dot_nn(x_their[...], ws_ref[...]) + bias_ref[...]
    og_copy.wait_recv()
    links.finish(gathered)
    sides = (zh, 1 - zh)
    totals = {}
    for p in range(parts):
        for d in (1, 3, 2):
            y_copies[p, d].wait_recv()
        for k, h in enumerate(sides):
            value = row_sum(h * NY + y, p)
            for d in (1, 3, 2):
                value = value + y_recv[p, d - 1, h].astype(F32)
            totals[k, p] = value
            zh_send[p, h] = value.astype(BF16)
        zh_copies[p] = links.send(zh_send.at[p], zh_recv.at[p], to_zh)
    for p in range(parts):
        zh_copies[p].wait_recv()
        for k, h in enumerate(sides):
            totals[k, p] = (totals[k, p] + zh_recv[p, h].astype(F32)).astype(BF16)

    def layer(k):
        sums = jnp.concatenate([totals[k, p] for p in range(parts)], axis=0)
        pre = self_pre[k] + dot_nn(sums, wn_ref[...])
        sig = 1.0 / (1.0 + jnp.exp(-pre))
        slope = sig * (1.0 + pre * (1.0 - sig))
        return sums, pre * sig, (og_ref[k].astype(F32) * slope).astype(BF16)

    sums, activated, pre_grad = layer(0)
    gt[y * 2 + zh] = dot_nt(wn_ref[...], pre_grad).astype(BF16)
    gt[y * 2 + 1 - zh] = dot_nt(wn_ref[...], layer(1)[2]).astype(BF16)
    gt_here = gt.at[pl.ds(y * 2, 2)]
    gt_copies = [links.send(gt_here, gt_here, to_y(d)) for d in (2, 1, 3)]
    out_ref[...] = activated.astype(BF16)
    store(out_ref, out_hbm)
    self_grad[...] = dot_nt(ws_ref[...], pre_grad)

    wide_self = dot_tn(panels[own], pre_grad).astype(BF16)
    wide_neigh = dot_tn(sums, pre_grad).astype(BF16)
    for q, block in enumerate(
        (wide_self[:, :BLK], wide_self[:, BLK:], wide_neigh[:, :BLK], wide_neigh[:, BLK:])
    ):
        wy_send[q, :BLK] = block
    bias_sum = jnp.sum(pre_grad.astype(F32), axis=0, keepdims=True)
    spot = lax.broadcasted_iota(jnp.int32, (16, BLK), 0)
    bias_rows = jnp.where(
        spot == 0, bias_sum[:, :BLK], jnp.where(spot == 1, bias_sum[:, BLK:], 0.0)
    ).astype(BF16)
    for q in range(4):
        wy_send[q, BLK:] = bias_rows
    wy_recv[y] = wy_send[y]

    wy_copies = [links.send(wy_send.at[turn_y(d)], wy_recv.at[y], to_y(d)) for d in (2, 1, 3)]
    links.finish(len(links.copies) - 6)
    for copy in gt_copies:
        copy.wait_recv()

    def spread(k, carry):
        for u in range(step):
            n = k * step + u
            right = jnp.concatenate(
                [tile_buf[index[ord_r, 2 * n]], tile_buf[index[ord_r, 2 * n + 1]]], axis=1
            )
            terms = dot_nn(gt[index[grow, 2 * n]], right)
            products[2 * n] = terms[:, :BLK]
            products[2 * n + 1] = terms[:, BLK:]
        return carry

    def add_up(p):
        def add(k, acc):
            for u in range(8):
                n = k * 8 + u
                term = products[index[made, n], lines(p), :]
                acc = acc * index[keep_c, n].astype(F32) + term
                runs[n, lines(p), :] = acc
            return acc

        lax.fori_loop(0, tiles // 8, add, jnp.zeros((width, BLK), F32))

    steps = n_pairs // step
    lax.fori_loop(0, steps // 2, spread, 0)

    for copy in wy_copies:
        copy.wait_recv()
    w_sum = wy_recv[0].astype(F32)
    for q in range(1, NY):
        w_sum = w_sum + wy_recv[q].astype(F32)
    part = BLK // nz
    for q in range(nz):
        wz_send[q, :part] = w_sum[q * part : (q + 1) * part]
        wz_send[q, part:] = w_sum[BLK : BLK + 8]
    wz_recv[z] = wz_send[z]
    wz_copies = [links.send(wz_send.at[turn_z(d)], wz_recv.at[z], to_z(d)) for d in range(1, nz)]

    lax.fori_loop(steps // 2, steps, spread, 0)

    def chunk(core_of, d):
        return slot(core_of, turn_x(d), 0)

    def col_sum(c, p):
        return runs[index[end_c, c], lines(p), :]

    def paired(p, d, i):
        return col_sum(chunk(core, d) + i, p) + core_recv[p, turn_x(d) * nz + i].astype(F32)

    lower, upper = pl.ds(0, half), pl.ds(half, half)
    core_copies, far_copies, near_copies, quad_copies, pair_copies = {}, {}, {}, {}, {}

    def core_stage(p):
        for d in (2, 1, 3, 0):
            base, first = chunk(other, d), turn_x(d) * nz
            for i in range(nz):
                core_send[p, first + i] = col_sum(base + i, p).astype(BF16)
            blocks = pl.ds(first, nz)
            core_copies[p, d] = links.send(
                core_send.at[p, blocks], core_recv.at[p, blocks], to_core
            )

    def far_stage(p):
        core_copies[p, 2].wait_recv()
        for i in range(nz):
            far_send[p, i] = paired(p, 2, i).astype(BF16)
        far_copies[p, 0] = links.send(far_send.at[p, lower], far_recv.at[p, lower], to_x(1))
        far_copies[p, 1] = links.send(far_send.at[p, upper], far_recv.at[p, upper], to_x(NX - 1))

    def near_stage(p, way, with_far):
        d = (1, NX - 1)[way]
        if with_far:
            far_copies[p, way].wait_recv()
        else:
            core_copies[p, d].wait_recv()
        first = half * (way if with_far else 1 - way)
        for i in range(first, first + half):
            value = paired(p, d, i)
            if with_far:
                value = value + far_recv[p, i].astype(F32)
            near_send[p, way, i] = value.astype(BF16)
        blocks = pl.ds(first, half)
        near_copies[p, way, with_far] = links.send(
            near_send.at[p, way, blocks], near_recv.at[p, way, blocks], to_x(d)
        )

    def z_total(p, i):
        return (
            paired(p, 0, i) + near_recv[p, 0, i].astype(F32) + near_recv[p, 1, i].astype(F32)
        )

    def quad_stage(p):
        core_copies[p, 0].wait_recv()
        for way in range(2):
            for with_far in (False, True):
                near_copies[p, way, with_far].wait_recv()
        for e in mates:
            quad_send[p, e, 0] = z_total(p, zq * half + turn_zi(e)).astype(BF16)
            quad_send[p, e, 1] = z_total(p, (1 - zq) * half + turn_zi(e)).astype(BF16)
            quad_copies[p, e] = links.send(quad_send.at[p, e], quad_recv.at[p, e], to_mate(e))

    def pair_stage(p):
        value = z_total(p, pair_z)
        for e in mates:
            quad_copies[p, e].wait_recv()
            value = value + quad_recv[p, e, 1].astype(F32)
        pair_send[p] = value.astype(BF16)
        pair_copies[p] = links.send(pair_send.at[p], pair_recv.at[p], to_pair)

    def last_stage(p):
        value = z_total(p, z) + self_grad[lines(p), :]
        for e in mates:
            value = value + quad_recv[p, e, 0].astype(F32)
        pair_copies[p].wait_recv()
        return value + pair_recv[p].astype(F32)

    add_up(0)
    core_stage(0)

    for copy in wz_copies:
        copy.wait_recv()
    w_part = wz_recv[0]
    for q in range(1, nz):
        w_part = w_part + wz_recv[q]
    wh_send[...] = w_part
    wh_copy = links.send(wh_send, wh_recv, to_zh)

    add_up(1)
    core_stage(1)
    far_stage(0)
    near_stage(0, 0, False)
    near_stage(0, 1, False)

    wh_copy.wait_recv()
    w_part = w_part + wh_recv[...]
    wx_recv[x] = w_part
    wx_copies = [links.send(wx_recv.at[x], wx_recv.at[x], to_x(d)) for d in (2, 1, 3)]

    far_stage(1)
    near_stage(0, 0, True)
    near_stage(0, 1, True)

    for copy in wx_copies:
        copy.wait_recv()
    w_part = wx_recv[0]
    for q in range(1, NX):
        w_part = w_part + wx_recv[q]
    wc_send[...] = w_part
    wc_copy = links.send(wc_send, wc_recv, to_core)

    near_stage(1, 0, False)
    near_stage(1, 1, False)
    near_stage(1, 0, True)
    near_stage(1, 1, True)

    wc_copy.wait_recv()
    w_part = w_part + wc_recv[...]
    gbias_ref[...] = jnp.concatenate(
        [w_part[part : part + 1], w_part[part + 1 : part + 2]], axis=1
    )
    store(gbias_ref, gbias_hbm)
    rows_here = pl.ds(pl.multiple_of(z * part, part), part)
    w_out[y, rows_here] = w_part[:part]
    gz_copies = [
        links.send(w_out.at[y, rows_here], w_out.at[y, rows_here], to_z(d)) for d in range(1, nz)
    ]

    quad_stage(0)
    for copy in gz_copies:
        copy.wait_recv()
    gy_copies = [links.send(w_out.at[y], w_out.at[y], to_y(d)) for d in (2, 1, 3)]
    pair_stage(0)
    quad_stage(1)
    pair_stage(1)
    links.finish(len(links.copies) - nz)
    grad = jnp.concatenate([last_stage(p) for p in range(parts)], axis=0)
    ingrad_ref[...] = jnp.transpose(grad).astype(BF16)
    store(ingrad_ref, ingrad_hbm)

    for copy in gy_copies:
        copy.wait_recv()
    gself_ref[:, :BLK] = w_out[0]
    gself_ref[:, BLK:] = w_out[1]
    gneigh_ref[:, :BLK] = w_out[2]
    gneigh_ref[:, BLK:] = w_out[3]
    store(gself_ref, gself_hbm)
    store(gneigh_ref, gneigh_hbm)
    links.finish()
    for copy in stores:
        copy.wait()


def place(*refs):
    count = (len(refs) - 2) // 3
    sources, targets, held = (refs[i * count : (i + 1) * count] for i in range(3))
    ins, outs = refs[-2:]
    moves = []
    for i in range(count):
        moves.append(
            (
                pltpu.make_async_copy(sources[i], held[i], ins.at[i]),
                pltpu.make_async_copy(held[i], targets[i], outs.at[i]),
            )
        )
        moves[-1][0].start()
    for into, out in moves:
        into.wait()
        out.start()
    for _, out in moves:
        out.wait()


def body(
    node_features,
    tile_values,
    tile_rows,
    tile_cols,
    weight_self,
    weight_neighbour,
    node_bias,
    output_grad,
):
    nz = lax.axis_size("row") // (NX * NC)
    half = nz // 2
    n_cols, n_rows = nz * NX * NC, lax.axis_size("col")
    tiles = tile_values.shape[2]
    feat, units = weight_self.shape
    hbm = pl.BlockSpec(memory_space=pltpu.HBM)
    block = (BLK, BLK)
    lines = (2, BLK // 2, BLK)
    part = BLK // nz + 8
    sems = 256
    results = (
        jax.ShapeDtypeStruct((BLK, units), BF16),
        jax.ShapeDtypeStruct((BLK, feat), BF16),
        jax.ShapeDtypeStruct((feat, units), F32),
        jax.ShapeDtypeStruct((feat, units), F32),
        jax.ShapeDtypeStruct((1, units), F32),
    )

    def halves(*lead):
        return pltpu.VMEM((2,) + lead + (BLK // 2, BLK), BF16)

    outs = pl.pallas_call(
        functools.partial(kernel, nz, tiles),
        out_shape=results,
        in_specs=[hbm] * 8,
        out_specs=(hbm,) * 5,
        scratch_shapes=[
            *(pltpu.VMEM(result.shape, result.dtype) for result in results),
            pltpu.VMEM((feat, units), BF16),
            pltpu.VMEM((feat, units), BF16),
            pltpu.VMEM((1, units), F32),
            pltpu.VMEM((2, BLK, units), BF16),
            pltpu.VMEM((BLK, feat), BF16),
            pltpu.VMEM((1, tiles), jnp.int32),
            pltpu.VMEM((1, tiles), jnp.int32),
            pltpu.VMEM((8, BLK), jnp.int32),
            pltpu.SMEM((8, BLK), jnp.int32),
            pltpu.VMEM((tiles + 1,) + block, BF16),
            pltpu.VMEM((n_cols,) + block, BF16),
            pltpu.VMEM((tiles + 1,) + block, F32),
            pltpu.VMEM((tiles + n_rows,) + block, F32),
            pltpu.VMEM((2, BLK, units), F32),
            pltpu.VMEM(block, F32),
            halves(3, 2),
            halves(3, 2),
            halves(2),
            halves(2),
            pltpu.VMEM((n_rows,) + block, BF16),
            halves(NX * nz),
            halves(NX * nz),
            halves(nz),
            halves(nz),
            halves(2, nz),
            halves(2, nz),
            halves(half, 2),
            halves(half, 2),
            halves(),
            halves(),
            pltpu.VMEM((4, BLK + 16, BLK), BF16),
            pltpu.VMEM((4, BLK + 16, BLK), BF16),
            pltpu.VMEM((nz, part, BLK), F32),
            pltpu.VMEM((nz, part, BLK), F32),
            pltpu.VMEM((part, BLK), F32),
            pltpu.VMEM((part, BLK), F32),
            pltpu.VMEM((NX, part, BLK), F32),
            pltpu.VMEM((part, BLK), F32),
            pltpu.VMEM((part, BLK), F32),
            pltpu.VMEM((4,) + block, F32),
            pltpu.SemaphoreType.DMA((9,)),
            pltpu.SemaphoreType.DMA((5,)),
            pltpu.SemaphoreType.DMA((sems,)),
            pltpu.SemaphoreType.DMA((sems,)),
        ],
        compiler_params=pltpu.CompilerParams(
            collective_id=0, has_side_effects=True, vmem_limit_bytes=VMEM_LIMIT
        ),
        cost_estimate=pl.CostEstimate(
            flops=4 * tiles * BLK**3, bytes_accessed=2 * tiles * BLK**2, transcendentals=BLK * units
        ),
    )(
        node_features,
        weight_self,
        weight_neighbour,
        node_bias.reshape(1, units),
        output_grad,
        tile_rows.reshape(1, tiles),
        tile_cols.reshape(1, tiles),
        tile_values,
    )
    outs = pl.pallas_call(
        place,
        out_shape=results,
        in_specs=[hbm] * 5,
        out_specs=(hbm,) * 5,
        scratch_shapes=[
            *(pltpu.VMEM(result.shape, result.dtype) for result in results),
            pltpu.SemaphoreType.DMA((5,)),
            pltpu.SemaphoreType.DMA((5,)),
        ],
        compiler_params=pltpu.CompilerParams(vmem_limit_bytes=VMEM_LIMIT),
    )(*outs)
    return (*outs[:4], outs[4].reshape(units))


def solution(mesh):
    placed = (
        P(("row", "col"), None),
        P("row", "col", None, None, None),
        P("row", "col", None),
        P("row", "col", None),
        P(),
        P(),
        P(),
        P(("row", "col"), None),
    )
    return jax.shard_map(
        body,
        mesh=mesh,
        in_specs=placed,
        out_specs=(P(("row", "col"), None), P(("row", "col"), None), P(), P(), P()),
        check_vma=False,
    )
```

```python
import functools

import jax
import jax.numpy as jnp
from jax import lax
from jax.experimental import pallas as pl
from jax.experimental.pallas import tpu as pltpu
from jax.sharding import PartitionSpec as P

MESH = pl.DeviceIdType.MESH
BLK = 128
F32 = jnp.float32
BF16 = jnp.bfloat16
VMEM_LIMIT = 64 * 2**20

NX, NC = 4, 2
NY = 4


def dot_nn(a, b):
    return lax.dot_general(a, b, (((1,), (0,)), ((), ())), preferred_element_type=F32)


def dot_nt(a, b):
    return lax.dot_general(a, b, (((1,), (1,)), ((), ())), preferred_element_type=F32)


def dot_tn(a, b):
    return lax.dot_general(a, b, (((0,), (0,)), ((), ())), preferred_element_type=F32)


class Links:
    def __init__(self, send_sems, recv_sems):
        self.send_sems, self.recv_sems, self.copies, self.sent = send_sems, recv_sems, [], 0

    def send(self, src, dst, device_id):
        at = len(self.copies)
        copy = pltpu.make_async_remote_copy(
            src_ref=src,
            dst_ref=dst,
            send_sem=self.send_sems.at[at],
            recv_sem=self.recv_sems.at[at],
            device_id=device_id,
            device_id_type=MESH,
        )
        copy.start()
        self.copies.append(copy)
        return copy

    def finish(self, upto=None):
        upto = len(self.copies) if upto is None else upto
        for copy in self.copies[self.sent : upto]:
            copy.wait_send()
        self.sent = max(self.sent, upto)


def iota(shape, axis):
    return lax.broadcasted_iota(jnp.int32, shape, axis)


def turned(line):
    n = line.shape[1]
    diagonal = iota((n, n), 0) == iota((n, n), 1)
    return jnp.sum(jnp.where(diagonal, line, 0), axis=1, keepdims=True)


def order_pairs(block, carried, n_blocks, index, at):
    tiles = block.shape[1]
    places = tiles + n_blocks
    shape = (tiles, tiles)
    block_down = turned(block)
    earlier = (block == block_down) & (iota(shape, 1) < iota(shape, 0))
    rank = jnp.sum(earlier.astype(jnp.int32), axis=1, keepdims=True)
    ids = iota((tiles, n_blocks), 1)
    held = jnp.sum((block_down == ids).astype(jnp.int32), axis=0, keepdims=True)
    padded = ((held + 1) // 2) * 2
    base = jnp.sum(jnp.where(ids < block_down, padded, 0), axis=1, keepdims=True)
    place = base + rank
    hot = place == iota((tiles, places), 1)

    def by_place(column):
        return jnp.sum(jnp.where(hot, column, 0), axis=0, keepdims=True)

    index[at : at + 1, :places] = tiles - by_place(tiles - iota((tiles, 1), 0))
    index[at + 1 : at + 2, :places] = by_place(turned(carried))
    index[at + 2 : at + 3, :places] = by_place(jnp.minimum(rank // 2, 1))
    small = (n_blocks, n_blocks)
    up_to = jnp.where(iota(small, 0) <= iota(small, 1), turned(padded), 0)
    last = jnp.sum(up_to, axis=0, keepdims=True) // 2 - 1
    index[at + 3 : at + 4, :n_blocks] = jnp.where(held > 0, last, tiles)


def order_tiles(block, carried, n_blocks, index, at):
    tiles = block.shape[1]
    shape = (tiles, tiles)
    block_down = turned(block)
    earlier = (block == block_down) & (iota(shape, 1) < iota(shape, 0))
    before = (block < block_down) | earlier
    place = jnp.sum(before.astype(jnp.int32), axis=1, keepdims=True)
    rank = jnp.sum(earlier.astype(jnp.int32), axis=1, keepdims=True)
    hot = place == iota(shape, 1)

    def by_place(column):
        return jnp.sum(jnp.where(hot, column, 0), axis=0, keepdims=True)

    index[at : at + 1, :tiles] = by_place(iota((tiles, 1), 0))
    index[at + 1 : at + 2, :tiles] = by_place(turned(carried))
    index[at + 2 : at + 3, :tiles] = by_place(jnp.minimum(rank, 1))
    ids = iota((tiles, n_blocks), 1)
    up_to = jnp.sum((block_down <= ids).astype(jnp.int32), axis=0, keepdims=True)
    held = jnp.sum((block_down == ids).astype(jnp.int32), axis=0, keepdims=True)
    index[at + 3 : at + 4, :n_blocks] = jnp.where(held > 0, up_to - 1, tiles)


def kernel(
    nz,
    tiles,
    x_hbm,
    ws_hbm,
    wn_hbm,
    bias_hbm,
    og_hbm,
    rows_hbm,
    cols_hbm,
    tiles_hbm,
    out_hbm,
    ingrad_hbm,
    gself_hbm,
    gneigh_hbm,
    gbias_hbm,
    out_ref,
    ingrad_ref,
    gself_ref,
    gneigh_ref,
    gbias_ref,
    ws_ref,
    wn_ref,
    bias_ref,
    nodes,
    nodes_relay,
    rows_ref,
    cols_ref,
    index_buf,
    index,
    tile_buf,
    panels,
    runs,
    self_pre,
    self_grad,
    y_send,
    y_recv,
    zh_send,
    zh_relay,
    zh_recv,
    gt,
    core_send,
    core_recv,
    far_send,
    far_recv,
    near_send,
    near_recv,
    quad_send,
    quad_recv,
    pair_send,
    pair_recv,
    wy_send,
    wy_recv,
    wz_send,
    wz_recv,
    wh_send,
    wh_recv,
    wx_recv,
    wc_send,
    wc_recv,
    w_out,
    load_sems,
    store_sems,
    send_sems,
    recv_sems,
):
    half = nz // 2
    n_cols = nz * NX * NC
    n_rows = 2 * NY
    row = lax.axis_index("row")
    col = lax.axis_index("col")
    core = lax.rem(row, NC)
    x = lax.rem(row // NC, NX)
    z = row // (NC * NX)
    zq = z // half
    zi = lax.rem(z, half)
    y = lax.rem(col, NY)
    zh = col // NY
    other = 1 - core

    def at_row(z_to, x_to, core_to):
        return {"row": (z_to * NX + x_to) * NC + core_to, "col": col}

    def at_col(zh_to, y_to):
        return {"row": row, "col": zh_to * NY + y_to}

    parts = 2
    width = BLK // parts

    def lines(p):
        return pl.ds(p * width, width)

    def turn_z(d):
        return lax.rem(z + d, nz)

    def turn_zi(d):
        return lax.rem(zi + d, half)

    def turn_x(d):
        return lax.rem(x + d, NX)

    def turn_y(d):
        return lax.rem(y + d, NY)

    def to_z(d):
        return at_row(turn_z(d), x, core)

    def to_mate(e):
        return at_row(zq * half + turn_zi(e), x, core)

    def to_x(d):
        return at_row(z, turn_x(d), core)

    def to_y(d):
        return at_col(zh, turn_y(d))

    to_pair = at_row((1 - zq) * half + zi, x, core)
    to_core = at_row(z, x, other)
    to_zh = at_col(1 - zh, y)

    def along_z(d):
        z_to = lax.rem(zh * nz + z + d, 2 * nz)
        return {"row": (lax.rem(z_to, nz) * NX + x) * NC + core, "col": z_to // nz * NY + y}

    first_leg = [along_z(nz - 1), along_z(nz + 1)]
    last_leg = [along_z(1), along_z(2 * nz - 1)]
    mates = [e for e in (1, half - 1) if e] + list(range(2, half - 1))
    mates = list(dict.fromkeys(mates))

    ord_r, pan, keep_r, end_r, ord_c, grow, keep_c, end_c = range(8)

    def slot(core_of, x_of, z_of):
        return (core_of * NX + x_of) * nz + z_of

    own = slot(core, x, z)
    loads = []
    for src, dst in (
        (x_hbm, panels.at[own]),
        (rows_hbm, rows_ref),
        (cols_hbm, cols_ref),
        (ws_hbm, ws_ref),
        (bias_hbm, bias_ref),
        (tiles_hbm.at[0, 0], tile_buf.at[pl.ds(0, tiles)]),
        (wn_hbm, wn_ref),
        (x_hbm, nodes.at[0, :, pl.ds(0, BLK)]),
        (og_hbm, nodes.at[0, :, pl.ds(BLK, 2 * BLK)]),
    ):
        loads.append(pltpu.make_async_copy(src, dst, load_sems.at[len(loads)]))
        loads[-1].start()
    load_x, load_rows, load_cols, load_ws, load_bias, load_tiles, load_wn, load_own, load_og = loads

    barrier = pltpu.get_barrier_semaphore()
    partners = [to_z(d) for d in range(1, nz)] + [to_x(d) for d in range(1, NX)]
    partners += [to_y(d) for d in range(1, NY)] + [to_core, to_zh]
    partners += first_leg + last_leg
    for partner in partners:
        pl.semaphore_signal(barrier, inc=1, device_id=partner, device_id_type=MESH)
    load_x.wait()
    pl.semaphore_wait(barrier, len(partners))

    links = Links(send_sems, recv_sems)
    stores = []

    def store(src, dst):
        stores.append(pltpu.make_async_copy(src, dst, store_sems.at[len(stores)]))
        stores[-1].start()

    def panel_to(slot_at, device_id):
        return links.send(panels.at[slot_at], panels.at[slot_at], device_id)

    pair_copy = panel_to(own, to_pair)
    z_copies = {e: panel_to(own, to_mate(e)) for e in mates}
    pair_z = (1 - zq) * half + zi
    relayed = {}

    def mate_z(e, q):
        return q * half + turn_zi(half - e)

    arrivals = [(z, None)] + [(mate_z(e, zq), z_copies[e]) for e in mates[:2]]
    arrivals += [(pair_z, pair_copy)] + [(mate_z(e, zq), z_copies[e]) for e in mates[2:]]
    arrivals += [(mate_z(e, 1 - zq), e) for e in mates]
    plus, minus, far, crossed = {}, {}, {}, []

    def cross(slot_at):
        crossed.append(panel_to(slot_at, to_core))

    def own_step(i):
        z_of, copy = arrivals[i]
        here = slot(core, x, z_of)
        if copy is not None:
            (relayed[copy] if isinstance(copy, int) else copy).wait_recv()
        if copy is pair_copy:
            for e in mates:
                relayed[e] = panel_to(here, to_mate(e))
        plus[i] = panel_to(here, to_x(1))
        minus[i] = panel_to(here, to_x(NX - 1))
        cross(here)

    def near_step(i):
        z_of = arrivals[i][0]
        from_minus = slot(core, turn_x(NX - 1), z_of)
        from_plus = slot(core, turn_x(1), z_of)
        plus[i].wait_recv()
        if i % 2 == 0:
            far[i] = panel_to(from_minus, to_x(1))
        cross(from_minus)
        minus[i].wait_recv()
        if i % 2 == 1:
            far[i] = panel_to(from_plus, to_x(NX - 1))
        cross(from_plus)

    def far_step(i):
        far[i].wait_recv()
        cross(slot(core, turn_x(2), arrivals[i][0]))

    def prepare():
        load_rows.wait()
        load_cols.wait()
        rows = rows_ref[...]
        cols = cols_ref[...]
        slots = slot(cols & (NC - 1), (cols // NC) & (NX - 1), cols // (NC * NX))
        order_pairs(rows, slots, n_rows, index_buf, 0)
        order_tiles(slots, (rows & (NY - 1)) * 2 + rows // NY, n_cols, index_buf, 4)
        runs[tiles] = jnp.zeros((BLK, BLK), F32)
        tile_buf[tiles] = jnp.zeros((BLK, BLK), BF16)
        index_copy = pltpu.make_async_copy(index_buf, index, load_sems.at[len(loads)])
        index_copy.start()
        load_ws.wait()
        load_bias.wait()
        self_pre[0] = dot_nn(panels[own], ws_ref[...]) + bias_ref[...]
        index_copy.wait()

    for i in range(nz + 2):
        if i < nz:
            own_step(i)
        if i == 0:
            prepare()
        if i == nz - 1:
            load_own.wait()
            load_og.wait()
            own_copies = [
                links.send(nodes.at[0, lines(p)], nodes_relay.at[lines(p)], first_leg[p])
                for p in range(parts)
            ]
        if 0 <= i - 1 < nz:
            near_step(i - 1)
        if 0 <= i - 2 < nz:
            far_step(i - 2)
    load_tiles.wait()
    load_wn.wait()
    for copy in crossed:
        copy.wait_recv()
    gathered = len(links.copies)
    for p in range(parts):
        own_copies[p].wait_recv()
        own_copies[p] = links.send(
            nodes_relay.at[lines(p)], nodes.at[1, lines(p)], last_leg[p]
        )

    n_pairs = (tiles + n_rows) // 2
    step = 4

    def collect(k, acc):
        for u in range(step):
            n = k * step + u
            here = [2 * n, 2 * n + 1]
            left = jnp.concatenate([tile_buf[index[ord_r, i]] for i in here], axis=1)
            right = jnp.concatenate([panels[index[pan, i]] for i in here], axis=0)
            acc = acc * index[keep_r, 2 * n].astype(F32) + dot_nn(left, right)
            runs[n] = acc
        return acc

    lax.fori_loop(0, n_pairs // step, collect, jnp.zeros((BLK, BLK), F32))

    def row_sum(r, p):
        return runs[index[end_r, r], lines(p), :]

    y_copies, zh_copies = {}, {}
    for p in range(parts):
        for d in (2, 1, 3):
            for h in range(2):
                y_send[p, d - 1, h] = row_sum(h * NY + turn_y(d), p).astype(BF16)
            y_copies[p, d] = links.send(y_send.at[p, d - 1], y_recv.at[p, d - 1], to_y(d))
    for copy in own_copies:
        copy.wait_recv()
    self_pre[1] = dot_nn(nodes[1, :, :BLK], ws_ref[...]) + bias_ref[...]
    links.finish(gathered)
    sides = (zh, 1 - zh)
    totals = {}
    for p in range(parts):
        for d in (1, 3, 2):
            y_copies[p, d].wait_recv()
        for k, h in enumerate(sides):
            value = row_sum(h * NY + y, p)
            for d in (1, 3, 2):
                value = value + y_recv[p, d - 1, h].astype(F32)
            totals[k, p] = value
            zh_send[p, h] = value.astype(BF16)
        zh_copies[p] = links.send(zh_send.at[p], zh_relay.at[p], first_leg[p])
    for p in range(parts):
        zh_copies[p].wait_recv()
        zh_copies[p] = links.send(zh_relay.at[p], zh_recv.at[p], last_leg[p])
    for p in range(parts):
        zh_copies[p].wait_recv()
        for k, h in enumerate(sides):
            totals[k, p] = (totals[k, p] + zh_recv[p, h].astype(F32)).astype(BF16)

    def layer(k):
        sums = jnp.concatenate([totals[k, p] for p in range(parts)], axis=0)
        pre = self_pre[k] + dot_nn(sums, wn_ref[...])
        sig = 1.0 / (1.0 + jnp.exp(-pre))
        slope = sig * (1.0 + pre * (1.0 - sig))
        return sums, pre * sig, (nodes[k, :, BLK:].astype(F32) * slope).astype(BF16)

    sums, activated, pre_grad = layer(0)
    gt[y * 2 + zh] = dot_nt(wn_ref[...], pre_grad).astype(BF16)
    gt[y * 2 + 1 - zh] = dot_nt(wn_ref[...], layer(1)[2]).astype(BF16)
    gt_here = gt.at[pl.ds(y * 2, 2)]
    gt_copies = [links.send(gt_here, gt_here, to_y(d)) for d in (2, 1, 3)]
    out_ref[...] = activated.astype(BF16)
    store(out_ref, out_hbm)
    self_grad[...] = dot_nt(ws_ref[...], pre_grad)

    wide_self = dot_tn(panels[own], pre_grad).astype(BF16)
    wide_neigh = dot_tn(sums, pre_grad).astype(BF16)
    for q, block in enumerate(
        (wide_self[:, :BLK], wide_self[:, BLK:], wide_neigh[:, :BLK], wide_neigh[:, BLK:])
    ):
        wy_send[q, :BLK] = block
    bias_sum = jnp.sum(pre_grad.astype(F32), axis=0, keepdims=True)
    spot = lax.broadcasted_iota(jnp.int32, (16, BLK), 0)
    bias_rows = jnp.where(
        spot == 0, bias_sum[:, :BLK], jnp.where(spot == 1, bias_sum[:, BLK:], 0.0)
    ).astype(BF16)
    for q in range(4):
        wy_send[q, BLK:] = bias_rows
    wy_recv[y] = wy_send[y]

    wy_copies = [links.send(wy_send.at[turn_y(d)], wy_recv.at[y], to_y(d)) for d in (2, 1, 3)]
    links.finish(len(links.copies) - 6)
    for copy in gt_copies:
        copy.wait_recv()

    def spread(k, acc):
        for u in range(8):
            n = k * 8 + u
            term = dot_nn(gt[index[grow, n]], tile_buf[index[ord_c, n]])
            acc = acc * index[keep_c, n].astype(F32) + term
            runs[n] = acc
        return acc

    steps = tiles // 8
    acc = lax.fori_loop(0, steps // 2, spread, jnp.zeros((BLK, BLK), F32))

    for copy in wy_copies:
        copy.wait_recv()
    w_sum = wy_recv[0].astype(F32)
    for q in range(1, NY):
        w_sum = w_sum + wy_recv[q].astype(F32)
    part = BLK // nz
    for q in range(nz):
        wz_send[q, :part] = w_sum[q * part : (q + 1) * part]
        wz_send[q, part:] = w_sum[BLK : BLK + 8]
    wz_recv[z] = wz_send[z]
    wz_copies = [links.send(wz_send.at[turn_z(d)], wz_recv.at[z], to_z(d)) for d in range(1, nz)]

    lax.fori_loop(steps // 2, steps, spread, acc)

    def chunk(core_of, d):
        return slot(core_of, turn_x(d), 0)

    def col_sum(c, p):
        return runs[index[end_c, c], lines(p), :]

    def paired(p, d, i):
        return col_sum(chunk(core, d) + i, p) + core_recv[p, turn_x(d) * nz + i].astype(F32)

    lower, upper = pl.ds(0, half), pl.ds(half, half)
    core_copies, far_copies, near_copies, quad_copies, pair_copies = {}, {}, {}, {}, {}

    def core_stage(p):
        for d in (2, 1, 3, 0):
            base, first = chunk(other, d), turn_x(d) * nz
            for i in range(nz):
                core_send[p, first + i] = col_sum(base + i, p).astype(BF16)
            blocks = pl.ds(first, nz)
            core_copies[p, d] = links.send(
                core_send.at[p, blocks], core_recv.at[p, blocks], to_core
            )

    def far_stage(p):
        core_copies[p, 2].wait_recv()
        for i in range(nz):
            far_send[p, i] = paired(p, 2, i).astype(BF16)
        far_copies[p, 0] = links.send(far_send.at[p, lower], far_recv.at[p, lower], to_x(1))
        far_copies[p, 1] = links.send(far_send.at[p, upper], far_recv.at[p, upper], to_x(NX - 1))

    def near_stage(p, way, with_far):
        d = (1, NX - 1)[way]
        if with_far:
            far_copies[p, way].wait_recv()
        else:
            core_copies[p, d].wait_recv()
        first = half * (way if with_far else 1 - way)
        for i in range(first, first + half):
            value = paired(p, d, i)
            if with_far:
                value = value + far_recv[p, i].astype(F32)
            near_send[p, way, i] = value.astype(BF16)
        blocks = pl.ds(first, half)
        near_copies[p, way, with_far] = links.send(
            near_send.at[p, way, blocks], near_recv.at[p, way, blocks], to_x(d)
        )

    def z_total(p, i):
        return (
            paired(p, 0, i) + near_recv[p, 0, i].astype(F32) + near_recv[p, 1, i].astype(F32)
        )

    def quad_stage(p):
        core_copies[p, 0].wait_recv()
        for way in range(2):
            for with_far in (False, True):
                near_copies[p, way, with_far].wait_recv()
        for e in mates:
            quad_send[p, e, 0] = z_total(p, zq * half + turn_zi(e)).astype(BF16)
            quad_send[p, e, 1] = z_total(p, (1 - zq) * half + turn_zi(e)).astype(BF16)
            quad_copies[p, e] = links.send(quad_send.at[p, e], quad_recv.at[p, e], to_mate(e))

    def pair_stage(p):
        value = z_total(p, pair_z)
        for e in mates:
            quad_copies[p, e].wait_recv()
            value = value + quad_recv[p, e, 1].astype(F32)
        pair_send[p] = value.astype(BF16)
        pair_copies[p] = links.send(pair_send.at[p], pair_recv.at[p], to_pair)

    def last_stage(p):
        value = z_total(p, z) + self_grad[lines(p), :]
        for e in mates:
            value = value + quad_recv[p, e, 0].astype(F32)
        pair_copies[p].wait_recv()
        return value + pair_recv[p].astype(F32)

    for p in range(parts):
        core_stage(p)
    far_stage(0)
    near_stage(0, 0, False)
    near_stage(0, 1, False)

    for copy in wz_copies:
        copy.wait_recv()
    w_part = wz_recv[0]
    for q in range(1, nz):
        w_part = w_part + wz_recv[q]
    wh_send[...] = w_part
    wh_copy = links.send(wh_send, wh_recv, to_zh)

    far_stage(1)
    near_stage(0, 0, True)
    near_stage(0, 1, True)
    near_stage(1, 0, False)
    near_stage(1, 1, False)

    wh_copy.wait_recv()
    w_part = w_part + wh_recv[...]
    wx_recv[x] = w_part
    wx_copies = [links.send(wx_recv.at[x], wx_recv.at[x], to_x(d)) for d in (2, 1, 3)]

    near_stage(1, 0, True)
    near_stage(1, 1, True)
    quad_stage(0)

    for copy in wx_copies:
        copy.wait_recv()
    w_part = wx_recv[0]
    for q in range(1, NX):
        w_part = w_part + wx_recv[q]
    wc_send[...] = w_part
    wc_copy = links.send(wc_send, wc_recv, to_core)

    pair_stage(0)
    quad_stage(1)

    wc_copy.wait_recv()
    w_part = w_part + wc_recv[...]
    gbias_ref[...] = jnp.concatenate(
        [w_part[part : part + 1], w_part[part + 1 : part + 2]], axis=1
    )
    store(gbias_ref, gbias_hbm)
    rows_here = pl.ds(pl.multiple_of(z * part, part), part)
    w_out[y, rows_here] = w_part[:part]
    gz_copies = [
        links.send(w_out.at[y, rows_here], w_out.at[y, rows_here], to_z(d)) for d in range(1, nz)
    ]

    pair_stage(1)
    links.finish(len(links.copies) - nz)
    for copy in gz_copies:
        copy.wait_recv()
    gy_copies = [links.send(w_out.at[y], w_out.at[y], to_y(d)) for d in (2, 1, 3)]
    grad = jnp.concatenate([last_stage(p) for p in range(parts)], axis=0)
    ingrad_ref[...] = jnp.transpose(grad).astype(BF16)
    store(ingrad_ref, ingrad_hbm)

    for copy in gy_copies:
        copy.wait_recv()
    gself_ref[:, :BLK] = w_out[0]
    gself_ref[:, BLK:] = w_out[1]
    gneigh_ref[:, :BLK] = w_out[2]
    gneigh_ref[:, BLK:] = w_out[3]
    store(gself_ref, gself_hbm)
    store(gneigh_ref, gneigh_hbm)
    links.finish()
    for copy in stores:
        copy.wait()


def place(*refs):
    count = (len(refs) - 2) // 3
    sources, targets, held = (refs[i * count : (i + 1) * count] for i in range(3))
    ins, outs = refs[-2:]
    moves = []
    for i in range(count):
        moves.append(
            (
                pltpu.make_async_copy(sources[i], held[i], ins.at[i]),
                pltpu.make_async_copy(held[i], targets[i], outs.at[i]),
            )
        )
        moves[-1][0].start()
    for into, out in moves:
        into.wait()
        out.start()
    for _, out in moves:
        out.wait()


def body(
    node_features,
    tile_values,
    tile_rows,
    tile_cols,
    weight_self,
    weight_neighbour,
    node_bias,
    output_grad,
):
    nz = lax.axis_size("row") // (NX * NC)
    half = nz // 2
    n_cols, n_rows = nz * NX * NC, lax.axis_size("col")
    tiles = tile_values.shape[2]
    feat, units = weight_self.shape
    hbm = pl.BlockSpec(memory_space=pltpu.HBM)
    block = (BLK, BLK)
    lines = (2, BLK // 2, BLK)
    part = BLK // nz + 8
    sems = 256
    results = (
        jax.ShapeDtypeStruct((BLK, units), BF16),
        jax.ShapeDtypeStruct((BLK, feat), BF16),
        jax.ShapeDtypeStruct((feat, units), F32),
        jax.ShapeDtypeStruct((feat, units), F32),
        jax.ShapeDtypeStruct((1, units), F32),
    )

    def halves(*lead):
        return pltpu.VMEM((2,) + lead + (BLK // 2, BLK), BF16)

    outs = pl.pallas_call(
        functools.partial(kernel, nz, tiles),
        out_shape=results,
        in_specs=[hbm] * 8,
        out_specs=(hbm,) * 5,
        scratch_shapes=[
            *(pltpu.VMEM(result.shape, result.dtype) for result in results),
            pltpu.VMEM((feat, units), BF16),
            pltpu.VMEM((feat, units), BF16),
            pltpu.VMEM((1, units), F32),
            pltpu.VMEM((2, BLK, feat + units), BF16),
            pltpu.VMEM((BLK, feat + units), BF16),
            pltpu.VMEM((1, tiles), jnp.int32),
            pltpu.VMEM((1, tiles), jnp.int32),
            pltpu.VMEM((8, BLK), jnp.int32),
            pltpu.SMEM((8, BLK), jnp.int32),
            pltpu.VMEM((tiles + 1,) + block, BF16),
            pltpu.VMEM((n_cols,) + block, BF16),
            pltpu.VMEM((tiles + 1,) + block, F32),
            pltpu.VMEM((2, BLK, units), F32),
            pltpu.VMEM(block, F32),
            halves(3, 2),
            halves(3, 2),
            halves(2),
            halves(2),
            halves(2),
            pltpu.VMEM((n_rows,) + block, BF16),
            halves(NX * nz),
            halves(NX * nz),
            halves(nz),
            halves(nz),
            halves(2, nz),
            halves(2, nz),
            halves(half, 2),
            halves(half, 2),
            halves(),
            halves(),
            pltpu.VMEM((4, BLK + 16, BLK), BF16),
            pltpu.VMEM((4, BLK + 16, BLK), BF16),
            pltpu.VMEM((nz, part, BLK), F32),
            pltpu.VMEM((nz, part, BLK), F32),
            pltpu.VMEM((part, BLK), F32),
            pltpu.VMEM((part, BLK), F32),
            pltpu.VMEM((NX, part, BLK), F32),
            pltpu.VMEM((part, BLK), F32),
            pltpu.VMEM((part, BLK), F32),
            pltpu.VMEM((4,) + block, F32),
            pltpu.SemaphoreType.DMA((10,)),
            pltpu.SemaphoreType.DMA((5,)),
            pltpu.SemaphoreType.DMA((sems,)),
            pltpu.SemaphoreType.DMA((sems,)),
        ],
        compiler_params=pltpu.CompilerParams(
            collective_id=0, has_side_effects=True, vmem_limit_bytes=VMEM_LIMIT
        ),
        cost_estimate=pl.CostEstimate(
            flops=4 * tiles * BLK**3, bytes_accessed=2 * tiles * BLK**2, transcendentals=BLK * units
        ),
    )(
        node_features,
        weight_self,
        weight_neighbour,
        node_bias.reshape(1, units),
        output_grad,
        tile_rows.reshape(1, tiles),
        tile_cols.reshape(1, tiles),
        tile_values,
    )
    outs = pl.pallas_call(
        place,
        out_shape=results,
        in_specs=[hbm] * 5,
        out_specs=(hbm,) * 5,
        scratch_shapes=[
            *(pltpu.VMEM(result.shape, result.dtype) for result in results),
            pltpu.SemaphoreType.DMA((5,)),
            pltpu.SemaphoreType.DMA((5,)),
        ],
        compiler_params=pltpu.CompilerParams(vmem_limit_bytes=VMEM_LIMIT),
    )(*outs)
    return (*outs[:4], outs[4].reshape(units))


def solution(mesh):
    placed = (
        P(("row", "col"), None),
        P("row", "col", None, None, None),
        P("row", "col", None),
        P("row", "col", None),
        P(),
        P(),
        P(),
        P(("row", "col"), None),
    )
    return jax.shard_map(
        body,
        mesh=mesh,
        in_specs=placed,
        out_specs=(P(("row", "col"), None), P(("row", "col"), None), P(), P(), P()),
        check_vma=False,
    )
```

```python
import functools

import jax
import jax.numpy as jnp
from jax import lax
from jax.experimental import pallas as pl
from jax.experimental.pallas import tpu as pltpu
from jax.sharding import PartitionSpec as P

MESH = pl.DeviceIdType.MESH
BLK = 128
F32 = jnp.float32
BF16 = jnp.bfloat16
VMEM_LIMIT = 64 * 2**20

NX, NC = 4, 2
NY = 4


def dot_nn(a, b):
    return lax.dot_general(a, b, (((1,), (0,)), ((), ())), preferred_element_type=F32)


def dot_nt(a, b):
    return lax.dot_general(a, b, (((1,), (1,)), ((), ())), preferred_element_type=F32)


def dot_tn(a, b):
    return lax.dot_general(a, b, (((0,), (0,)), ((), ())), preferred_element_type=F32)


class Links:
    def __init__(self, send_sems, recv_sems):
        self.send_sems, self.recv_sems, self.copies, self.sent = send_sems, recv_sems, [], 0

    def send(self, src, dst, device_id):
        at = len(self.copies)
        copy = pltpu.make_async_remote_copy(
            src_ref=src,
            dst_ref=dst,
            send_sem=self.send_sems.at[at],
            recv_sem=self.recv_sems.at[at],
            device_id=device_id,
            device_id_type=MESH,
        )
        copy.start()
        self.copies.append(copy)
        return copy

    def finish(self, upto=None):
        upto = len(self.copies) if upto is None else upto
        for copy in self.copies[self.sent : upto]:
            copy.wait_send()
        self.sent = max(self.sent, upto)


def iota(shape, axis):
    return lax.broadcasted_iota(jnp.int32, shape, axis)


def turned(line):
    n = line.shape[1]
    diagonal = iota((n, n), 0) == iota((n, n), 1)
    return jnp.sum(jnp.where(diagonal, line, 0), axis=1, keepdims=True)


def order_pairs(block, carried, n_blocks, index, at):
    tiles = block.shape[1]
    places = tiles + n_blocks
    shape = (tiles, tiles)
    block_down = turned(block)
    earlier = (block == block_down) & (iota(shape, 1) < iota(shape, 0))
    rank = jnp.sum(earlier.astype(jnp.int32), axis=1, keepdims=True)
    ids = iota((tiles, n_blocks), 1)
    held = jnp.sum((block_down == ids).astype(jnp.int32), axis=0, keepdims=True)
    padded = ((held + 1) // 2) * 2
    base = jnp.sum(jnp.where(ids < block_down, padded, 0), axis=1, keepdims=True)
    place = base + rank
    hot = place == iota((tiles, places), 1)

    def by_place(column):
        return jnp.sum(jnp.where(hot, column, 0), axis=0, keepdims=True)

    index[at : at + 1, :places] = tiles - by_place(tiles - iota((tiles, 1), 0))
    index[at + 1 : at + 2, :places] = by_place(turned(carried))
    index[at + 2 : at + 3, :places] = by_place(jnp.minimum(rank // 2, 1))
    small = (n_blocks, n_blocks)
    up_to = jnp.where(iota(small, 0) <= iota(small, 1), turned(padded), 0)
    last = jnp.sum(up_to, axis=0, keepdims=True) // 2 - 1
    index[at + 3 : at + 4, :n_blocks] = jnp.where(held > 0, last, tiles)


def order_tiles(block, carried, n_blocks, index, at):
    tiles = block.shape[1]
    shape = (tiles, tiles)
    block_down = turned(block)
    earlier = (block == block_down) & (iota(shape, 1) < iota(shape, 0))
    before = (block < block_down) | earlier
    place = jnp.sum(before.astype(jnp.int32), axis=1, keepdims=True)
    rank = jnp.sum(earlier.astype(jnp.int32), axis=1, keepdims=True)
    hot = place == iota(shape, 1)

    def by_place(column):
        return jnp.sum(jnp.where(hot, column, 0), axis=0, keepdims=True)

    index[at : at + 1, :tiles] = by_place(iota((tiles, 1), 0))
    index[at + 1 : at + 2, :tiles] = by_place(turned(carried))
    index[at + 2 : at + 3, :tiles] = by_place(jnp.minimum(rank, 1))
    ids = iota((tiles, n_blocks), 1)
    up_to = jnp.sum((block_down <= ids).astype(jnp.int32), axis=0, keepdims=True)
    held = jnp.sum((block_down == ids).astype(jnp.int32), axis=0, keepdims=True)
    index[at + 3 : at + 4, :n_blocks] = jnp.where(held > 0, up_to - 1, tiles)


def kernel(
    nz,
    tiles,
    x_hbm,
    ws_hbm,
    wn_hbm,
    bias_hbm,
    og_hbm,
    rows_hbm,
    cols_hbm,
    tiles_hbm,
    out_hbm,
    ingrad_hbm,
    gself_hbm,
    gneigh_hbm,
    gbias_hbm,
    out_ref,
    ingrad_ref,
    gself_ref,
    gneigh_ref,
    gbias_ref,
    ws_ref,
    wn_ref,
    bias_ref,
    nodes,
    rows_ref,
    cols_ref,
    index_buf,
    index,
    tile_buf,
    panels,
    runs,
    self_pre,
    self_grad,
    y_send,
    y_recv,
    zh_send,
    zh_recv,
    gt,
    core_send,
    core_recv,
    far_send,
    far_recv,
    near_send,
    near_recv,
    quad_send,
    quad_recv,
    pair_send,
    pair_recv,
    wy_send,
    wy_recv,
    wz_send,
    wz_recv,
    wp_send,
    wp_recv,
    wh_send,
    wh_recv,
    wx_recv,
    wc_send,
    wc_recv,
    w_out,
    load_sems,
    store_sems,
    send_sems,
    recv_sems,
):
    half = nz // 2
    n_cols = nz * NX * NC
    n_rows = 2 * NY
    row = lax.axis_index("row")
    col = lax.axis_index("col")
    core = lax.rem(row, NC)
    x = lax.rem(row // NC, NX)
    z = row // (NC * NX)
    zq = z // half
    zi = lax.rem(z, half)
    y = lax.rem(col, NY)
    zh = col // NY
    other = 1 - core

    def at_row(z_to, x_to, core_to):
        return {"row": (z_to * NX + x_to) * NC + core_to, "col": col}

    def at_col(zh_to, y_to):
        return {"row": row, "col": zh_to * NY + y_to}

    parts = 2
    width = BLK // parts

    def lines(p):
        return pl.ds(p * width, width)

    def turn_zi(d):
        return lax.rem(zi + d, half)

    def turn_x(d):
        return lax.rem(x + d, NX)

    def turn_y(d):
        return lax.rem(y + d, NY)

    def to_mate(e):
        return at_row(zq * half + turn_zi(e), x, core)

    def to_x(d):
        return at_row(z, turn_x(d), core)

    def to_y(d):
        return at_col(zh, turn_y(d))

    to_pair = at_row((1 - zq) * half + zi, x, core)
    to_core = at_row(z, x, other)
    to_zh = at_col(1 - zh, y)
    mates = (1, 3, 2)

    ord_r, pan, keep_r, end_r, ord_c, grow, keep_c, end_c = range(8)

    def slot(core_of, x_of, e, q=0):
        return ((core_of * NX + x_of) * half + e) * 2 + q

    own = slot(core, x, 0)
    loads = []
    for src, dst in (
        (x_hbm, panels.at[own]),
        (rows_hbm, rows_ref),
        (cols_hbm, cols_ref),
        (ws_hbm, ws_ref),
        (bias_hbm, bias_ref),
        (tiles_hbm.at[0, 0], tile_buf.at[pl.ds(0, tiles)]),
        (wn_hbm, wn_ref),
        (x_hbm, nodes.at[0, :, pl.ds(0, BLK)]),
        (og_hbm, nodes.at[0, :, pl.ds(BLK, 2 * BLK)]),
    ):
        loads.append(pltpu.make_async_copy(src, dst, load_sems.at[len(loads)]))
        loads[-1].start()
    load_x, load_rows, load_cols, load_ws, load_bias, load_tiles, load_wn, load_own, load_og = loads

    barrier = pltpu.get_barrier_semaphore()
    partners = [to_mate(e) for e in mates] + [to_pair] + [to_x(d) for d in range(1, NX)]
    partners += [to_y(d) for d in range(1, NY)] + [to_core, to_zh]
    for partner in partners:
        pl.semaphore_signal(barrier, inc=1, device_id=partner, device_id_type=MESH)
    load_x.wait()
    pl.semaphore_wait(barrier, len(partners))

    links = Links(send_sems, recv_sems)
    stores = []

    def store(src, dst):
        stores.append(pltpu.make_async_copy(src, dst, store_sems.at[len(stores)]))
        stores[-1].start()

    def panels_to(first, count, device_id, dst=None):
        return links.send(
            panels.at[pl.ds(first, count)],
            panels.at[pl.ds(first if dst is None else dst, count)],
            device_id,
        )

    order = (0,) + mates
    plus, minus, far, crossed, from_mate = {}, {}, {}, [], {}

    def cross(x_of, i):
        if i % 2 == 1:
            first = slot(core, x_of, min(order[i - 1], order[i]))
            crossed.append(panels_to(first, half, to_core))

    def own_step(i):
        e = order[i]
        if e:
            from_mate[e].wait_recv()
        here = slot(core, x, e)
        plus[i] = panels_to(here, 2, to_x(1))
        minus[i] = panels_to(here, 2, to_x(NX - 1))
        cross(x, i)

    def near_step(i):
        plus[i].wait_recv()
        if i % 2 == 0:
            far[i] = panels_to(slot(core, turn_x(NX - 1), order[i]), 2, to_x(1))
        cross(turn_x(NX - 1), i)
        minus[i].wait_recv()
        if i % 2 == 1:
            far[i] = panels_to(slot(core, turn_x(1), order[i]), 2, to_x(NX - 1))
        cross(turn_x(1), i)

    def far_step(i):
        far[i].wait_recv()
        cross(turn_x(2), i)

    index_copy = pltpu.make_async_copy(index_buf, index, load_sems.at[len(loads)])

    def prepare():
        load_rows.wait()
        load_cols.wait()
        rows = rows_ref[...]
        cols = cols_ref[...]
        z_of = cols // (NC * NX)
        e_of = (zi - z_of) & (half - 1)
        slots = slot(cols & (NC - 1), (cols // NC) & (NX - 1), e_of, (z_of // half + zq) & 1)
        order_pairs(rows, slots, n_rows, index_buf, 0)
        order_tiles(slots, (rows & (NY - 1)) * 2 + rows // NY, n_cols, index_buf, 4)
        runs[tiles] = jnp.zeros((BLK, BLK), F32)
        tile_buf[tiles] = jnp.zeros((BLK, BLK), BF16)
        index_copy.start()
        load_ws.wait()
        load_bias.wait()
        self_pre[0] = dot_nn(panels[own], ws_ref[...]) + bias_ref[...]

    pair_copy = panels_to(own, 1, to_pair, dst=own + 1)
    prepare()
    pair_copy.wait_recv()
    for e in mates:
        from_mate[e] = panels_to(own, 2, to_mate(e), dst=slot(core, x, e))
    for i in range(half + 2):
        if i < half:
            own_step(i)
        if i == half - 1:
            load_own.wait()
            load_og.wait()
            own_copy = links.send(nodes.at[0], nodes.at[1], to_zh)
        if 0 <= i - 1 < half:
            near_step(i - 1)
        if 0 <= i - 2 < half:
            far_step(i - 2)
    load_tiles.wait()
    load_wn.wait()
    index_copy.wait()
    for copy in crossed:
        copy.wait_recv()
    gathered = len(links.copies)

    n_pairs = (tiles + n_rows) // 2
    step = 4

    def collect(k, acc):
        for u in range(step):
            n = k * step + u
            here = [2 * n, 2 * n + 1]
            left = jnp.concatenate([tile_buf[index[ord_r, i]] for i in here], axis=1)
            right = jnp.concatenate([panels[index[pan, i]] for i in here], axis=0)
            acc = acc * index[keep_r, 2 * n].astype(F32) + dot_nn(left, right)
            runs[n] = acc
        return acc

    lax.fori_loop(0, n_pairs // step, collect, jnp.zeros((BLK, BLK), F32))

    def row_sum(r):
        return runs[index[end_r, r]]

    y_copies = {}
    for d in (2, 1, 3):
        for h in range(2):
            y_send[d - 1, h] = row_sum(h * NY + turn_y(d)).astype(BF16)
        y_copies[d] = links.send(y_send.at[d - 1], y_recv.at[d - 1], to_y(d))
    own_copy.wait_recv()
    self_pre[1] = dot_nn(nodes[1, :, :BLK], ws_ref[...]) + bias_ref[...]
    links.finish(gathered)
    sides = (zh, 1 - zh)
    for d in (1, 3, 2):
        y_copies[d].wait_recv()
    totals = []
    for h in sides:
        value = row_sum(h * NY + y)
        for d in (1, 3, 2):
            value = value + y_recv[d - 1, h].astype(F32)
        totals.append(value)
        zh_send[h] = value.astype(BF16)
    zh_copy = links.send(zh_send, zh_recv, to_zh)
    zh_copy.wait_recv()
    totals = [
        (value + zh_recv[h].astype(F32)).astype(BF16) for value, h in zip(totals, sides)
    ]

    def layer(k):
        sums = totals[k]
        pre = self_pre[k] + dot_nn(sums, wn_ref[...])
        sig = 1.0 / (1.0 + jnp.exp(-pre))
        slope = sig * (1.0 + pre * (1.0 - sig))
        return sums, pre * sig, (nodes[k, :, BLK:].astype(F32) * slope).astype(BF16)

    sums, activated, pre_grad = layer(0)
    gt[y * 2 + zh] = dot_nt(wn_ref[...], pre_grad).astype(BF16)
    gt[y * 2 + 1 - zh] = dot_nt(wn_ref[...], layer(1)[2]).astype(BF16)
    gt_here = gt.at[pl.ds(y * 2, 2)]
    gt_copies = [links.send(gt_here, gt_here, to_y(d)) for d in (2, 1, 3)]
    out_ref[...] = activated.astype(BF16)
    store(out_ref, out_hbm)
    self_grad[...] = dot_nt(ws_ref[...], pre_grad)

    wide_self = dot_tn(panels[own], pre_grad).astype(BF16)
    wide_neigh = dot_tn(sums, pre_grad).astype(BF16)
    for q, block in enumerate(
        (wide_self[:, :BLK], wide_self[:, BLK:], wide_neigh[:, :BLK], wide_neigh[:, BLK:])
    ):
        wy_send[q, :BLK] = block
    bias_sum = jnp.sum(pre_grad.astype(F32), axis=0, keepdims=True)
    spot = lax.broadcasted_iota(jnp.int32, (16, BLK), 0)
    bias_rows = jnp.where(
        spot == 0, bias_sum[:, :BLK], jnp.where(spot == 1, bias_sum[:, BLK:], 0.0)
    ).astype(BF16)
    for q in range(4):
        wy_send[q, BLK:] = bias_rows
    wy_recv[y] = wy_send[y]

    wy_copies = [links.send(wy_send.at[turn_y(d)], wy_recv.at[y], to_y(d)) for d in (2, 1, 3)]
    links.finish(len(links.copies) - 6)
    for copy in gt_copies:
        copy.wait_recv()

    def spread(k, acc):
        for u in range(8):
            n = k * 8 + u
            term = dot_nn(gt[index[grow, n]], tile_buf[index[ord_c, n]])
            acc = acc * index[keep_c, n].astype(F32) + term
            runs[n] = acc
        return acc

    steps = tiles // 8
    acc = lax.fori_loop(0, steps // 2, spread, jnp.zeros((BLK, BLK), F32))

    for copy in wy_copies:
        copy.wait_recv()
    w_sum = wy_recv[0].astype(F32)
    for q in range(1, NY):
        w_sum = w_sum + wy_recv[q].astype(F32)
    part = BLK // half
    for q in range(half):
        wz_send[q, :part] = w_sum[q * part : (q + 1) * part]
        wz_send[q, part:] = w_sum[BLK : BLK + 8]
    wz_recv[zi] = wz_send[zi]
    wz_copies = [links.send(wz_send.at[turn_zi(e)], wz_recv.at[zi], to_mate(e)) for e in mates]

    lax.fori_loop(steps // 2, steps, spread, acc)

    turns = (2, 1, 3, 0)

    def col_sum(c, p):
        return runs[index[end_c, c], lines(p), :]

    def paired(p, d, i):
        mine = col_sum(slot(core, turn_x(d), 0) + i, p)
        return mine + core_recv[p, turns.index(d) * nz + i].astype(F32)

    lower, upper = pl.ds(0, half), pl.ds(half, half)
    core_copies, far_copies, near_copies, quad_copies, pair_copies = {}, {}, {}, {}, {}

    def core_stage(p):
        for at, d in enumerate(turns):
            for i in range(nz):
                core_send[p, at * nz + i] = col_sum(slot(other, turn_x(d), 0) + i, p).astype(BF16)
            if at in (0, NX - 1):
                blocks = pl.ds(0, nz) if at == 0 else pl.ds(nz, (NX - 1) * nz)
                core_copies[p, at] = links.send(
                    core_send.at[p, blocks], core_recv.at[p, blocks], to_core
                )

    def far_stage(p):
        core_copies[p, 0].wait_recv()
        for i in range(nz):
            far_send[p, i] = paired(p, 2, i).astype(BF16)
        far_copies[p, 0] = links.send(far_send.at[p, lower], far_recv.at[p, lower], to_x(1))
        far_copies[p, 1] = links.send(far_send.at[p, upper], far_recv.at[p, upper], to_x(NX - 1))

    def near_stage(p):
        core_copies[p, NX - 1].wait_recv()
        for way, d in enumerate((1, NX - 1)):
            far_copies[p, way].wait_recv()
            for i in range(nz):
                value = paired(p, d, i)
                if i // half == way:
                    value = value + far_recv[p, i].astype(F32)
                near_send[p, way, i] = value.astype(BF16)
            near_copies[p, way] = links.send(near_send.at[p, way], near_recv.at[p, way], to_x(d))

    def z_total(p, i):
        return (
            paired(p, 0, i) + near_recv[p, 0, i].astype(F32) + near_recv[p, 1, i].astype(F32)
        )

    def quad_stage(p):
        for way in range(2):
            near_copies[p, way].wait_recv()
        for e in mates:
            for q in range(2):
                quad_send[p, e, q] = z_total(p, 2 * e + q).astype(BF16)
            quad_copies[p, e] = links.send(
                quad_send.at[p, e], quad_recv.at[p, e], to_mate(half - e)
            )

    def pair_stage(p):
        value = z_total(p, 1)
        for e in mates:
            quad_copies[p, e].wait_recv()
            value = value + quad_recv[p, e, 1].astype(F32)
        pair_send[p] = value.astype(BF16)
        pair_copies[p] = links.send(pair_send.at[p], pair_recv.at[p], to_pair)

    def last_stage(p):
        value = z_total(p, 0) + self_grad[lines(p), :]
        for e in mates:
            value = value + quad_recv[p, e, 0].astype(F32)
        pair_copies[p].wait_recv()
        return value + pair_recv[p].astype(F32)

    for copy in wz_copies:
        copy.wait_recv()
    w_part = wz_recv[0]
    for q in range(1, half):
        w_part = w_part + wz_recv[q]
    wp_send[...] = w_part
    wp_copy = links.send(wp_send, wp_recv, to_pair)

    core_stage(0)
    core_stage(1)

    wp_copy.wait_recv()
    w_part = w_part + wp_recv[...]
    wh_send[...] = w_part
    wh_copy = links.send(wh_send, wh_recv, to_zh)

    far_stage(0)
    far_stage(1)
    near_stage(0)

    wh_copy.wait_recv()
    w_part = w_part + wh_recv[...]
    wx_recv[x] = w_part
    wx_copies = [links.send(wx_recv.at[x], wx_recv.at[x], to_x(d)) for d in (2, 1, 3)]

    near_stage(1)
    quad_stage(0)

    for copy in wx_copies:
        copy.wait_recv()
    w_part = wx_recv[0]
    for q in range(1, NX):
        w_part = w_part + wx_recv[q]
    wc_send[...] = w_part
    wc_copy = links.send(wc_send, wc_recv, to_core)

    pair_stage(0)

    wc_copy.wait_recv()
    w_part = w_part + wc_recv[...]
    gbias_ref[...] = jnp.concatenate(
        [w_part[part : part + 1], w_part[part + 1 : part + 2]], axis=1
    )
    store(gbias_ref, gbias_hbm)
    rows_here = pl.ds(pl.multiple_of(zi * part, part), part)
    w_out[y, rows_here] = w_part[:part]
    gz_copies = [
        links.send(w_out.at[y, rows_here], w_out.at[y, rows_here], to_mate(e)) for e in mates
    ]

    quad_stage(1)
    for copy in gz_copies:
        copy.wait_recv()
    gy_copies = [links.send(w_out.at[y], w_out.at[y], to_y(d)) for d in (2, 1, 3)]
    pair_stage(1)
    links.finish(len(links.copies) - 8)
    grad = jnp.concatenate([last_stage(p) for p in range(parts)], axis=0)
    ingrad_ref[...] = jnp.transpose(grad).astype(BF16)
    store(ingrad_ref, ingrad_hbm)

    for copy in gy_copies:
        copy.wait_recv()
    gself_ref[:, :BLK] = w_out[0]
    gself_ref[:, BLK:] = w_out[1]
    gneigh_ref[:, :BLK] = w_out[2]
    gneigh_ref[:, BLK:] = w_out[3]
    store(gself_ref, gself_hbm)
    store(gneigh_ref, gneigh_hbm)
    links.finish()
    for copy in stores:
        copy.wait()


def place(*refs):
    count = (len(refs) - 2) // 3
    sources, targets, held = (refs[i * count : (i + 1) * count] for i in range(3))
    ins, outs = refs[-2:]
    moves = []
    for i in range(count):
        moves.append(
            (
                pltpu.make_async_copy(sources[i], held[i], ins.at[i]),
                pltpu.make_async_copy(held[i], targets[i], outs.at[i]),
            )
        )
        moves[-1][0].start()
    for into, out in moves:
        into.wait()
        out.start()
    for _, out in moves:
        out.wait()


def body(
    node_features,
    tile_values,
    tile_rows,
    tile_cols,
    weight_self,
    weight_neighbour,
    node_bias,
    output_grad,
):
    nz = lax.axis_size("row") // (NX * NC)
    half = nz // 2
    n_cols, n_rows = nz * NX * NC, lax.axis_size("col")
    tiles = tile_values.shape[2]
    feat, units = weight_self.shape
    hbm = pl.BlockSpec(memory_space=pltpu.HBM)
    block = (BLK, BLK)
    lines = (2, BLK // 2, BLK)
    part = BLK // half + 8
    sems = 256
    results = (
        jax.ShapeDtypeStruct((BLK, units), BF16),
        jax.ShapeDtypeStruct((BLK, feat), BF16),
        jax.ShapeDtypeStruct((feat, units), F32),
        jax.ShapeDtypeStruct((feat, units), F32),
        jax.ShapeDtypeStruct((1, units), F32),
    )

    def halves(*lead):
        return pltpu.VMEM((2,) + lead + (BLK // 2, BLK), BF16)

    outs = pl.pallas_call(
        functools.partial(kernel, nz, tiles),
        out_shape=results,
        in_specs=[hbm] * 8,
        out_specs=(hbm,) * 5,
        scratch_shapes=[
            *(pltpu.VMEM(result.shape, result.dtype) for result in results),
            pltpu.VMEM((feat, units), BF16),
            pltpu.VMEM((feat, units), BF16),
            pltpu.VMEM((1, units), F32),
            pltpu.VMEM((2, BLK, feat + units), BF16),
            pltpu.VMEM((1, tiles), jnp.int32),
            pltpu.VMEM((1, tiles), jnp.int32),
            pltpu.VMEM((8, BLK), jnp.int32),
            pltpu.SMEM((8, BLK), jnp.int32),
            pltpu.VMEM((tiles + 1,) + block, BF16),
            pltpu.VMEM((n_cols,) + block, BF16),
            pltpu.VMEM((tiles + 1,) + block, F32),
            pltpu.VMEM((2, BLK, units), F32),
            pltpu.VMEM(block, F32),
            pltpu.VMEM((3, 2) + block, BF16),
            pltpu.VMEM((3, 2) + block, BF16),
            pltpu.VMEM((2,) + block, BF16),
            pltpu.VMEM((2,) + block, BF16),
            pltpu.VMEM((n_rows,) + block, BF16),
            halves(NX * nz),
            halves(NX * nz),
            halves(nz),
            halves(nz),
            halves(2, nz),
            halves(2, nz),
            halves(half, 2),
            halves(half, 2),
            halves(),
            halves(),
            pltpu.VMEM((4, BLK + 16, BLK), BF16),
            pltpu.VMEM((4, BLK + 16, BLK), BF16),
            pltpu.VMEM((half, part, BLK), F32),
            pltpu.VMEM((half, part, BLK), F32),
            pltpu.VMEM((part, BLK), F32),
            pltpu.VMEM((part, BLK), F32),
            pltpu.VMEM((part, BLK), F32),
            pltpu.VMEM((part, BLK), F32),
            pltpu.VMEM((NX, part, BLK), F32),
            pltpu.VMEM((part, BLK), F32),
            pltpu.VMEM((part, BLK), F32),
            pltpu.VMEM((4,) + block, F32),
            pltpu.SemaphoreType.DMA((10,)),
            pltpu.SemaphoreType.DMA((5,)),
            pltpu.SemaphoreType.DMA((sems,)),
            pltpu.SemaphoreType.DMA((sems,)),
        ],
        compiler_params=pltpu.CompilerParams(
            collective_id=0, has_side_effects=True, vmem_limit_bytes=VMEM_LIMIT
        ),
        cost_estimate=pl.CostEstimate(
            flops=4 * tiles * BLK**3, bytes_accessed=2 * tiles * BLK**2, transcendentals=BLK * units
        ),
    )(
        node_features,
        weight_self,
        weight_neighbour,
        node_bias.reshape(1, units),
        output_grad,
        tile_rows.reshape(1, tiles),
        tile_cols.reshape(1, tiles),
        tile_values,
    )
    outs = pl.pallas_call(
        place,
        out_shape=results,
        in_specs=[hbm] * 5,
        out_specs=(hbm,) * 5,
        scratch_shapes=[
            *(pltpu.VMEM(result.shape, result.dtype) for result in results),
            pltpu.SemaphoreType.DMA((5,)),
            pltpu.SemaphoreType.DMA((5,)),
        ],
        compiler_params=pltpu.CompilerParams(vmem_limit_bytes=VMEM_LIMIT),
    )(*outs)
    return (*outs[:4], outs[4].reshape(units))


def solution(mesh):
    placed = (
        P(("row", "col"), None),
        P("row", "col", None, None, None),
        P("row", "col", None),
        P("row", "col", None),
        P(),
        P(),
        P(),
        P(("row", "col"), None),
    )
    return jax.shard_map(
        body,
        mesh=mesh,
        in_specs=placed,
        out_specs=(P(("row", "col"), None), P(("row", "col"), None), P(), P(), P()),
        check_vma=False,
    )
```

```python
import functools

import jax
import jax.numpy as jnp
from jax import lax
from jax.experimental import pallas as pl
from jax.experimental.pallas import tpu as pltpu
from jax.sharding import PartitionSpec as P

MESH = pl.DeviceIdType.MESH
BLK = 128
F32 = jnp.float32
BF16 = jnp.bfloat16
VMEM_LIMIT = 64 * 2**20
PARTS = 4

NX, NC = 4, 2
NY = 4


def dot_nn(a, b):
    return lax.dot_general(a, b, (((1,), (0,)), ((), ())), preferred_element_type=F32)


def dot_nt(a, b):
    return lax.dot_general(a, b, (((1,), (1,)), ((), ())), preferred_element_type=F32)


def dot_tn(a, b):
    return lax.dot_general(a, b, (((0,), (0,)), ((), ())), preferred_element_type=F32)


class Links:
    def __init__(self, send_sems, recv_sems):
        self.send_sems, self.recv_sems, self.copies, self.sent = send_sems, recv_sems, [], 0

    def send(self, src, dst, device_id):
        at = len(self.copies)
        copy = pltpu.make_async_remote_copy(
            src_ref=src,
            dst_ref=dst,
            send_sem=self.send_sems.at[at],
            recv_sem=self.recv_sems.at[at],
            device_id=device_id,
            device_id_type=MESH,
        )
        copy.start()
        self.copies.append(copy)
        return copy

    def finish(self, upto=None):
        upto = len(self.copies) if upto is None else upto
        for copy in self.copies[self.sent : upto]:
            copy.wait_send()
        self.sent = max(self.sent, upto)


def iota(shape, axis):
    return lax.broadcasted_iota(jnp.int32, shape, axis)


def turned(line):
    n = line.shape[1]
    diagonal = iota((n, n), 0) == iota((n, n), 1)
    return jnp.sum(jnp.where(diagonal, line, 0), axis=1, keepdims=True)


def order_pairs(block, carried, n_blocks, index, at):
    tiles = block.shape[1]
    places = tiles + n_blocks
    shape = (tiles, tiles)
    block_down = turned(block)
    earlier = (block == block_down) & (iota(shape, 1) < iota(shape, 0))
    rank = jnp.sum(earlier.astype(jnp.int32), axis=1, keepdims=True)
    ids = iota((tiles, n_blocks), 1)
    held = jnp.sum((block_down == ids).astype(jnp.int32), axis=0, keepdims=True)
    padded = ((held + 1) // 2) * 2
    base = jnp.sum(jnp.where(ids < block_down, padded, 0), axis=1, keepdims=True)
    place = base + rank
    hot = place == iota((tiles, places), 1)

    def by_place(column):
        return jnp.sum(jnp.where(hot, column, 0), axis=0, keepdims=True)

    index[at : at + 1, :places] = tiles - by_place(tiles - iota((tiles, 1), 0))
    index[at + 1 : at + 2, :places] = by_place(turned(carried))
    index[at + 2 : at + 3, :places] = by_place(jnp.minimum(rank // 2, 1))
    small = (n_blocks, n_blocks)
    up_to = jnp.where(iota(small, 0) <= iota(small, 1), turned(padded), 0)
    last = jnp.sum(up_to, axis=0, keepdims=True) // 2 - 1
    index[at + 3 : at + 4, :n_blocks] = jnp.where(held > 0, last, tiles)


def order_tiles(block, carried, n_blocks, index, at):
    tiles = block.shape[1]
    shape = (tiles, tiles)
    block_down = turned(block)
    earlier = (block == block_down) & (iota(shape, 1) < iota(shape, 0))
    before = (block < block_down) | earlier
    place = jnp.sum(before.astype(jnp.int32), axis=1, keepdims=True)
    rank = jnp.sum(earlier.astype(jnp.int32), axis=1, keepdims=True)
    hot = place == iota(shape, 1)

    def by_place(column):
        return jnp.sum(jnp.where(hot, column, 0), axis=0, keepdims=True)

    index[at : at + 1, :tiles] = by_place(iota((tiles, 1), 0))
    index[at + 1 : at + 2, :tiles] = by_place(turned(carried))
    index[at + 2 : at + 3, :tiles] = by_place(jnp.minimum(rank, 1))
    ids = iota((tiles, n_blocks), 1)
    up_to = jnp.sum((block_down <= ids).astype(jnp.int32), axis=0, keepdims=True)
    held = jnp.sum((block_down == ids).astype(jnp.int32), axis=0, keepdims=True)
    index[at + 3 : at + 4, :n_blocks] = jnp.where(held > 0, up_to - 1, tiles)


def kernel(
    nz,
    tiles,
    x_hbm,
    ws_hbm,
    wn_hbm,
    bias_hbm,
    og_hbm,
    rows_hbm,
    cols_hbm,
    tiles_hbm,
    out_hbm,
    ingrad_hbm,
    gself_hbm,
    gneigh_hbm,
    gbias_hbm,
    out_ref,
    ingrad_ref,
    gself_ref,
    gneigh_ref,
    gbias_ref,
    ws_ref,
    wn_ref,
    bias_ref,
    nodes,
    rows_ref,
    cols_ref,
    index_buf,
    index,
    tile_buf,
    panels,
    runs,
    self_pre,
    self_grad,
    y_send,
    y_recv,
    zh_send,
    zh_recv,
    gt,
    core_send,
    core_recv,
    far_send,
    far_recv,
    near_send,
    near_recv,
    quad_send,
    quad_recv,
    pair_send,
    pair_recv,
    wy_send,
    wy_recv,
    wz_send,
    wz_recv,
    wp_send,
    wp_recv,
    wh_send,
    wh_recv,
    wx_recv,
    wc_send,
    wc_recv,
    w_out,
    load_sems,
    store_sems,
    send_sems,
    recv_sems,
):
    half = nz // 2
    n_cols = nz * NX * NC
    n_rows = 2 * NY
    row = lax.axis_index("row")
    col = lax.axis_index("col")
    core = lax.rem(row, NC)
    x = lax.rem(row // NC, NX)
    z = row // (NC * NX)
    zq = z // half
    zi = lax.rem(z, half)
    y = lax.rem(col, NY)
    zh = col // NY
    other = 1 - core

    def at_row(z_to, x_to, core_to):
        return {"row": (z_to * NX + x_to) * NC + core_to, "col": col}

    def at_col(zh_to, y_to):
        return {"row": row, "col": zh_to * NY + y_to}

    parts = PARTS
    width = BLK // parts

    def lines(p):
        return pl.ds(p * width, width)

    def turn_zi(d):
        return lax.rem(zi + d, half)

    def turn_x(d):
        return lax.rem(x + d, NX)

    def turn_y(d):
        return lax.rem(y + d, NY)

    def to_mate(e):
        return at_row(zq * half + turn_zi(e), x, core)

    def to_x(d):
        return at_row(z, turn_x(d), core)

    def to_y(d):
        return at_col(zh, turn_y(d))

    to_pair = at_row((1 - zq) * half + zi, x, core)
    to_core = at_row(z, x, other)
    to_zh = at_col(1 - zh, y)
    mates = (1, 3, 2)

    ord_r, pan, keep_r, end_r, ord_c, grow, keep_c, end_c = range(8)

    def slot(core_of, x_of, e, q=0):
        return ((core_of * NX + x_of) * 2 + q) * half + e

    own = slot(core, x, 0)
    loads = []
    for src, dst in (
        (x_hbm, panels.at[own]),
        (rows_hbm, rows_ref),
        (cols_hbm, cols_ref),
        (ws_hbm, ws_ref),
        (bias_hbm, bias_ref),
        (tiles_hbm.at[0, 0], tile_buf.at[pl.ds(0, tiles)]),
        (wn_hbm, wn_ref),
        (x_hbm, nodes.at[0, :, pl.ds(0, BLK)]),
        (og_hbm, nodes.at[0, :, pl.ds(BLK, 2 * BLK)]),
    ):
        loads.append(pltpu.make_async_copy(src, dst, load_sems.at[len(loads)]))
        loads[-1].start()
    load_x, load_rows, load_cols, load_ws, load_bias, load_tiles, load_wn, load_own, load_og = loads

    barrier = pltpu.get_barrier_semaphore()
    partners = [to_mate(e) for e in mates] + [to_pair] + [to_x(d) for d in range(1, NX)]
    partners += [to_y(d) for d in range(1, NY)] + [to_core, to_zh]
    for partner in partners:
        pl.semaphore_signal(barrier, inc=1, device_id=partner, device_id_type=MESH)
    load_x.wait()
    pl.semaphore_wait(barrier, len(partners))

    links = Links(send_sems, recv_sems)
    stores = []

    def store(src, dst):
        stores.append(pltpu.make_async_copy(src, dst, store_sems.at[len(stores)]))
        stores[-1].start()

    def panels_to(first, count, device_id, dst=None):
        return links.send(
            panels.at[pl.ds(first, count)],
            panels.at[pl.ds(first if dst is None else dst, count)],
            device_id,
        )

    order = [(0, 0), (1, 0), (3, 0), (0, 1), (2, 0), (1, 1), (3, 1), (2, 1)]
    along = {(0, 1): panels_to(own, 1, to_pair, dst=slot(core, x, 0, 1))}
    for e in mates:
        along[e, 0] = panels_to(own, 1, to_mate(e), dst=slot(core, x, e))
    plus, minus, far, crossed = {}, {}, {}, []

    def cross(x_of, i):
        if i in (half, nz - 1):
            crossed.append(panels_to(slot(core, x_of, 0, order[i][1]), half, to_core))

    def own_step(i):
        e, q = order[i]
        here = slot(core, x, e, q)
        if i:
            along[e, q].wait_recv()
        if (e, q) == (0, 1):
            for m in mates:
                along[m, 1] = panels_to(here, 1, to_mate(m), dst=slot(core, x, m, 1))
        plus[i] = panels_to(here, 1, to_x(1))
        minus[i] = panels_to(here, 1, to_x(NX - 1))
        cross(x, i)

    def near_step(i):
        plus[i].wait_recv()
        if i % 2 == 0:
            far[i] = panels_to(slot(core, turn_x(NX - 1), *order[i]), 1, to_x(1))
        cross(turn_x(NX - 1), i)
        minus[i].wait_recv()
        if i % 2 == 1:
            far[i] = panels_to(slot(core, turn_x(1), *order[i]), 1, to_x(NX - 1))
        cross(turn_x(1), i)

    def far_step(i):
        far[i].wait_recv()
        cross(turn_x(2), i)

    index_copy = pltpu.make_async_copy(index_buf, index, load_sems.at[len(loads)])

    def prepare():
        load_rows.wait()
        load_cols.wait()
        rows = rows_ref[...]
        cols = cols_ref[...]
        z_of = cols // (NC * NX)
        e_of = (zi - z_of) & (half - 1)
        slots = slot(cols & (NC - 1), (cols // NC) & (NX - 1), e_of, (z_of // half + zq) & 1)
        order_pairs(rows, slots, n_rows, index_buf, 0)
        order_tiles(slots, (rows & (NY - 1)) * 2 + rows // NY, n_cols, index_buf, 4)
        runs[tiles] = jnp.zeros((BLK, BLK), F32)
        tile_buf[tiles] = jnp.zeros((BLK, BLK), BF16)
        index_copy.start()
        load_ws.wait()
        load_bias.wait()
        self_pre[0] = dot_nn(panels[own], ws_ref[...]) + bias_ref[...]

    for i in range(nz + 2):
        if i < nz:
            own_step(i)
        if i == 0:
            prepare()
        if i == nz - 1:
            load_own.wait()
            load_og.wait()
            own_copy = links.send(nodes.at[0], nodes.at[1], to_zh)
        if 0 <= i - 1 < nz:
            near_step(i - 1)
        if 0 <= i - 2 < nz:
            far_step(i - 2)
    load_tiles.wait()
    load_wn.wait()
    index_copy.wait()
    for copy in crossed:
        copy.wait_recv()
    gathered = len(links.copies)

    n_pairs = (tiles + n_rows) // 2
    step = 4

    def collect(k, acc):
        for u in range(step):
            n = k * step + u
            here = [2 * n, 2 * n + 1]
            left = jnp.concatenate([tile_buf[index[ord_r, i]] for i in here], axis=1)
            right = jnp.concatenate([panels[index[pan, i]] for i in here], axis=0)
            acc = acc * index[keep_r, 2 * n].astype(F32) + dot_nn(left, right)
            runs[n] = acc
        return acc

    lax.fori_loop(0, n_pairs // step, collect, jnp.zeros((BLK, BLK), F32))

    def piece(p):
        return pl.ds(p * (BLK // 2), BLK // 2)

    def row_sum(r, p):
        return runs[index[end_r, r], piece(p), :]

    y_copies, zh_copies, totals = {}, {}, {}
    for p in range(2):
        for d in (2, 1, 3):
            for h in range(2):
                y_send[p, d - 1, h] = row_sum(h * NY + turn_y(d), p).astype(BF16)
            y_copies[p, d] = links.send(y_send.at[p, d - 1], y_recv.at[p, d - 1], to_y(d))
    own_copy.wait_recv()
    self_pre[1] = dot_nn(nodes[1, :, :BLK], ws_ref[...]) + bias_ref[...]
    links.finish(gathered)
    sides = (zh, 1 - zh)
    for p in range(2):
        for d in (1, 3, 2):
            y_copies[p, d].wait_recv()
        for k, h in enumerate(sides):
            value = row_sum(h * NY + y, p)
            for d in (1, 3, 2):
                value = value + y_recv[p, d - 1, h].astype(F32)
            totals[k, p] = value
            zh_send[p, h] = value.astype(BF16)
        zh_copies[p] = links.send(zh_send.at[p], zh_recv.at[p], to_zh)
    for p in range(2):
        zh_copies[p].wait_recv()
        for k, h in enumerate(sides):
            totals[k, p] = (totals[k, p] + zh_recv[p, h].astype(F32)).astype(BF16)

    def layer(k):
        sums = jnp.concatenate([totals[k, 0], totals[k, 1]], axis=0)
        pre = self_pre[k] + dot_nn(sums, wn_ref[...])
        sig = 1.0 / (1.0 + jnp.exp(-pre))
        slope = sig * (1.0 + pre * (1.0 - sig))
        return sums, pre * sig, (nodes[k, :, BLK:].astype(F32) * slope).astype(BF16)

    sums, activated, pre_grad = layer(0)
    gt[y * 2 + zh] = dot_nt(wn_ref[...], pre_grad).astype(BF16)
    gt[y * 2 + 1 - zh] = dot_nt(wn_ref[...], layer(1)[2]).astype(BF16)
    gt_here = gt.at[pl.ds(y * 2, 2)]
    gt_copies = [links.send(gt_here, gt_here, to_y(d)) for d in (2, 1, 3)]
    out_ref[...] = activated.astype(BF16)
    store(out_ref, out_hbm)
    self_grad[...] = dot_nt(ws_ref[...], pre_grad)

    wide_self = dot_tn(panels[own], pre_grad).astype(BF16)
    wide_neigh = dot_tn(sums, pre_grad).astype(BF16)
    for q, block in enumerate(
        (wide_self[:, :BLK], wide_self[:, BLK:], wide_neigh[:, :BLK], wide_neigh[:, BLK:])
    ):
        wy_send[q, :BLK] = block
    bias_sum = jnp.sum(pre_grad.astype(F32), axis=0, keepdims=True)
    spot = lax.broadcasted_iota(jnp.int32, (16, BLK), 0)
    bias_rows = jnp.where(
        spot == 0, bias_sum[:, :BLK], jnp.where(spot == 1, bias_sum[:, BLK:], 0.0)
    ).astype(BF16)
    for q in range(4):
        wy_send[q, BLK:] = bias_rows
    wy_recv[y] = wy_send[y]

    wy_copies = [links.send(wy_send.at[turn_y(d)], wy_recv.at[y], to_y(d)) for d in (2, 1, 3)]
    links.finish(len(links.copies) - 6)
    for copy in gt_copies:
        copy.wait_recv()

    def spread(k, acc):
        for u in range(8):
            n = k * 8 + u
            term = dot_nn(gt[index[grow, n]], tile_buf[index[ord_c, n]])
            acc = acc * index[keep_c, n].astype(F32) + term
            runs[n] = acc
        return acc

    steps = tiles // 8
    acc = lax.fori_loop(0, steps // 2, spread, jnp.zeros((BLK, BLK), F32))

    for copy in wy_copies:
        copy.wait_recv()
    w_sum = wy_recv[0].astype(F32)
    for q in range(1, NY):
        w_sum = w_sum + wy_recv[q].astype(F32)
    part = BLK // half
    for q in range(half):
        wz_send[q, :part] = w_sum[q * part : (q + 1) * part]
        wz_send[q, part:] = w_sum[BLK : BLK + 8]
    wz_recv[zi] = wz_send[zi]
    wz_copies = [links.send(wz_send.at[turn_zi(e)], wz_recv.at[zi], to_mate(e)) for e in mates]

    lax.fori_loop(steps // 2, steps, spread, acc)

    turns = (2, 1, 3, 0)

    def col_sum(c, p):
        return runs[index[end_c, c], lines(p), :]

    def paired(p, d, i):
        mine = col_sum(slot(core, turn_x(d), 0) + i, p)
        return mine + core_recv[p, turns.index(d) * nz + i].astype(F32)

    lower, upper = pl.ds(0, half), pl.ds(half, half)
    core_copies, far_copies, near_copies, quad_copies, pair_copies = {}, {}, {}, {}, {}

    def core_stage(p):
        for at, d in enumerate(turns):
            for i in range(nz):
                core_send[p, at * nz + i] = col_sum(slot(other, turn_x(d), 0) + i, p).astype(BF16)
            if at in (0, NX - 1):
                blocks = pl.ds(0, nz) if at == 0 else pl.ds(nz, (NX - 1) * nz)
                core_copies[p, at] = links.send(
                    core_send.at[p, blocks], core_recv.at[p, blocks], to_core
                )

    def far_stage(p):
        core_copies[p, 0].wait_recv()
        for i in range(nz):
            far_send[p, i] = paired(p, 2, i).astype(BF16)
        far_copies[p, 0] = links.send(far_send.at[p, lower], far_recv.at[p, lower], to_x(1))
        far_copies[p, 1] = links.send(far_send.at[p, upper], far_recv.at[p, upper], to_x(NX - 1))

    def near_stage(p):
        core_copies[p, NX - 1].wait_recv()
        for way, d in enumerate((1, NX - 1)):
            far_copies[p, way].wait_recv()
            for i in range(nz):
                value = paired(p, d, i)
                if i // half == way:
                    value = value + far_recv[p, i].astype(F32)
                near_send[p, way, i] = value.astype(BF16)
            near_copies[p, way] = links.send(near_send.at[p, way], near_recv.at[p, way], to_x(d))

    def z_total(p, i):
        return (
            paired(p, 0, i) + near_recv[p, 0, i].astype(F32) + near_recv[p, 1, i].astype(F32)
        )

    def quad_stage(p):
        for way in range(2):
            near_copies[p, way].wait_recv()
        for e in mates:
            for q in range(2):
                quad_send[p, e, q] = z_total(p, q * half + e).astype(BF16)
            quad_copies[p, e] = links.send(
                quad_send.at[p, e], quad_recv.at[p, e], to_mate(half - e)
            )

    def pair_stage(p):
        value = z_total(p, half)
        for e in mates:
            quad_copies[p, e].wait_recv()
            value = value + quad_recv[p, e, 1].astype(F32)
        pair_send[p] = value.astype(BF16)
        pair_copies[p] = links.send(pair_send.at[p], pair_recv.at[p], to_pair)

    def last_stage(p):
        value = z_total(p, 0) + self_grad[lines(p), :]
        for e in mates:
            value = value + quad_recv[p, e, 0].astype(F32)
        pair_copies[p].wait_recv()
        return value + pair_recv[p].astype(F32)

    for copy in wz_copies:
        copy.wait_recv()
    w_part = wz_recv[0]
    for q in range(1, half):
        w_part = w_part + wz_recv[q]
    wp_send[...] = w_part
    wp_copy = links.send(wp_send, wp_recv, to_pair)

    core_stage(0)
    core_stage(1)

    wp_copy.wait_recv()
    w_part = w_part + wp_recv[...]
    wh_send[...] = w_part
    wh_copy = links.send(wh_send, wh_recv, to_zh)

    far_stage(0)
    core_stage(2)
    far_stage(1)
    near_stage(0)
    core_stage(3)
    far_stage(2)

    wh_copy.wait_recv()
    w_part = w_part + wh_recv[...]
    wx_recv[x] = w_part
    wx_copies = [links.send(wx_recv.at[x], wx_recv.at[x], to_x(d)) for d in (2, 1, 3)]

    near_stage(1)
    quad_stage(0)
    far_stage(3)
    near_stage(2)
    quad_stage(1)
    pair_stage(0)

    for copy in wx_copies:
        copy.wait_recv()
    w_part = wx_recv[0]
    for q in range(1, NX):
        w_part = w_part + wx_recv[q]
    wc_send[...] = w_part
    wc_copy = links.send(wc_send, wc_recv, to_core)

    near_stage(3)
    quad_stage(2)
    pair_stage(1)

    wc_copy.wait_recv()
    w_part = w_part + wc_recv[...]
    gbias_ref[...] = jnp.concatenate(
        [w_part[part : part + 1], w_part[part + 1 : part + 2]], axis=1
    )
    store(gbias_ref, gbias_hbm)
    rows_here = pl.ds(pl.multiple_of(zi * part, part), part)
    w_out[y, rows_here] = w_part[:part].astype(BF16)
    gz_copies = [
        links.send(w_out.at[y, rows_here], w_out.at[y, rows_here], to_mate(e)) for e in mates
    ]

    quad_stage(3)
    pair_stage(2)
    for copy in gz_copies:
        copy.wait_recv()
    gy_copies = [links.send(w_out.at[y], w_out.at[y], to_y(d)) for d in (2, 1, 3)]
    pair_stage(3)
    links.finish(len(links.copies) - 8)
    grad = jnp.concatenate([last_stage(p) for p in range(parts)], axis=0)
    ingrad_ref[...] = jnp.transpose(grad).astype(BF16)
    store(ingrad_ref, ingrad_hbm)

    for copy in gy_copies:
        copy.wait_recv()
    gself_ref[:, :BLK] = w_out[0].astype(F32)
    gself_ref[:, BLK:] = w_out[1].astype(F32)
    gneigh_ref[:, :BLK] = w_out[2].astype(F32)
    gneigh_ref[:, BLK:] = w_out[3].astype(F32)
    store(gself_ref, gself_hbm)
    store(gneigh_ref, gneigh_hbm)
    links.finish()
    for copy in stores:
        copy.wait()


def place(*refs):
    count = (len(refs) - 2) // 3
    sources, targets, held = (refs[i * count : (i + 1) * count] for i in range(3))
    ins, outs = refs[-2:]
    moves = []
    for i in range(count):
        moves.append(
            (
                pltpu.make_async_copy(sources[i], held[i], ins.at[i]),
                pltpu.make_async_copy(held[i], targets[i], outs.at[i]),
            )
        )
        moves[-1][0].start()
    for into, out in moves:
        into.wait()
        out.start()
    for _, out in moves:
        out.wait()


def body(
    node_features,
    tile_values,
    tile_rows,
    tile_cols,
    weight_self,
    weight_neighbour,
    node_bias,
    output_grad,
):
    nz = lax.axis_size("row") // (NX * NC)
    half = nz // 2
    n_cols, n_rows = nz * NX * NC, lax.axis_size("col")
    tiles = tile_values.shape[2]
    feat, units = weight_self.shape
    hbm = pl.BlockSpec(memory_space=pltpu.HBM)
    block = (BLK, BLK)
    lines = (2, BLK // 2, BLK)
    part = BLK // half + 8
    sems = 256
    results = (
        jax.ShapeDtypeStruct((BLK, units), BF16),
        jax.ShapeDtypeStruct((BLK, feat), BF16),
        jax.ShapeDtypeStruct((feat, units), F32),
        jax.ShapeDtypeStruct((feat, units), F32),
        jax.ShapeDtypeStruct((1, units), F32),
    )

    def pieces(*lead):
        return pltpu.VMEM((PARTS,) + lead + (BLK // PARTS, BLK), BF16)

    outs = pl.pallas_call(
        functools.partial(kernel, nz, tiles),
        out_shape=results,
        in_specs=[hbm] * 8,
        out_specs=(hbm,) * 5,
        scratch_shapes=[
            *(pltpu.VMEM(result.shape, result.dtype) for result in results),
            pltpu.VMEM((feat, units), BF16),
            pltpu.VMEM((feat, units), BF16),
            pltpu.VMEM((1, units), F32),
            pltpu.VMEM((2, BLK, feat + units), BF16),
            pltpu.VMEM((1, tiles), jnp.int32),
            pltpu.VMEM((1, tiles), jnp.int32),
            pltpu.VMEM((8, BLK), jnp.int32),
            pltpu.SMEM((8, BLK), jnp.int32),
            pltpu.VMEM((tiles + 1,) + block, BF16),
            pltpu.VMEM((n_cols,) + block, BF16),
            pltpu.VMEM((tiles + 1,) + block, F32),
            pltpu.VMEM((2, BLK, units), F32),
            pltpu.VMEM(block, F32),
            pltpu.VMEM((2, 3, 2, BLK // 2, BLK), BF16),
            pltpu.VMEM((2, 3, 2, BLK // 2, BLK), BF16),
            pltpu.VMEM((2, 2, BLK // 2, BLK), BF16),
            pltpu.VMEM((2, 2, BLK // 2, BLK), BF16),
            pltpu.VMEM((n_rows,) + block, BF16),
            pieces(NX * nz),
            pieces(NX * nz),
            pieces(nz),
            pieces(nz),
            pieces(2, nz),
            pieces(2, nz),
            pieces(half, 2),
            pieces(half, 2),
            pieces(),
            pieces(),
            pltpu.VMEM((4, BLK + 16, BLK), BF16),
            pltpu.VMEM((4, BLK + 16, BLK), BF16),
            pltpu.VMEM((half, part, BLK), F32),
            pltpu.VMEM((half, part, BLK), F32),
            pltpu.VMEM((part, BLK), F32),
            pltpu.VMEM((part, BLK), F32),
            pltpu.VMEM((part, BLK), F32),
            pltpu.VMEM((part, BLK), F32),
            pltpu.VMEM((NX, part, BLK), F32),
            pltpu.VMEM((part, BLK), F32),
            pltpu.VMEM((part, BLK), F32),
            pltpu.VMEM((4,) + block, BF16),
            pltpu.SemaphoreType.DMA((10,)),
            pltpu.SemaphoreType.DMA((5,)),
            pltpu.SemaphoreType.DMA((sems,)),
            pltpu.SemaphoreType.DMA((sems,)),
        ],
        compiler_params=pltpu.CompilerParams(
            collective_id=0, has_side_effects=True, vmem_limit_bytes=VMEM_LIMIT
        ),
        cost_estimate=pl.CostEstimate(
            flops=4 * tiles * BLK**3, bytes_accessed=2 * tiles * BLK**2, transcendentals=BLK * units
        ),
    )(
        node_features,
        weight_self,
        weight_neighbour,
        node_bias.reshape(1, units),
        output_grad,
        tile_rows.reshape(1, tiles),
        tile_cols.reshape(1, tiles),
        tile_values,
    )
    outs = pl.pallas_call(
        place,
        out_shape=results,
        in_specs=[hbm] * 5,
        out_specs=(hbm,) * 5,
        scratch_shapes=[
            *(pltpu.VMEM(result.shape, result.dtype) for result in results),
            pltpu.SemaphoreType.DMA((5,)),
            pltpu.SemaphoreType.DMA((5,)),
        ],
        compiler_params=pltpu.CompilerParams(vmem_limit_bytes=VMEM_LIMIT),
    )(*outs)
    return (*outs[:4], outs[4].reshape(units))


def solution(mesh):
    placed = (
        P(("row", "col"), None),
        P("row", "col", None, None, None),
        P("row", "col", None),
        P("row", "col", None),
        P(),
        P(),
        P(),
        P(("row", "col"), None),
    )
    return jax.shard_map(
        body,
        mesh=mesh,
        in_specs=placed,
        out_specs=(P(("row", "col"), None), P(("row", "col"), None), P(), P(), P()),
        check_vma=False,
    )
```

```python
import functools

import jax
import jax.numpy as jnp
from jax import lax
from jax.experimental import pallas as pl
from jax.experimental.pallas import tpu as pltpu
from jax.sharding import PartitionSpec as P

MESH = pl.DeviceIdType.MESH
BLK = 128
F32 = jnp.float32
BF16 = jnp.bfloat16
VMEM_LIMIT = 64 * 2**20

NX, NC = 4, 2
NY = 4


def dot_nn(a, b):
    return lax.dot_general(a, b, (((1,), (0,)), ((), ())), preferred_element_type=F32)


def dot_nt(a, b):
    return lax.dot_general(a, b, (((1,), (1,)), ((), ())), preferred_element_type=F32)


def dot_tn(a, b):
    return lax.dot_general(a, b, (((0,), (0,)), ((), ())), preferred_element_type=F32)


class Links:
    def __init__(self, send_sems, recv_sems):
        self.send_sems, self.recv_sems, self.copies, self.sent = send_sems, recv_sems, [], 0

    def send(self, src, dst, device_id):
        at = len(self.copies)
        copy = pltpu.make_async_remote_copy(
            src_ref=src,
            dst_ref=dst,
            send_sem=self.send_sems.at[at],
            recv_sem=self.recv_sems.at[at],
            device_id=device_id,
            device_id_type=MESH,
        )
        copy.start()
        self.copies.append(copy)
        return copy

    def finish(self, upto=None):
        upto = len(self.copies) if upto is None else upto
        for copy in self.copies[self.sent : upto]:
            copy.wait_send()
        self.sent = max(self.sent, upto)


def iota(shape, axis):
    return lax.broadcasted_iota(jnp.int32, shape, axis)


def turned(line):
    n = line.shape[1]
    diagonal = iota((n, n), 0) == iota((n, n), 1)
    return jnp.sum(jnp.where(diagonal, line, 0), axis=1, keepdims=True)


def order_pairs(block, carried, n_blocks, index, at):
    tiles = block.shape[1]
    places = tiles + n_blocks
    shape = (tiles, tiles)
    block_down = turned(block)
    earlier = (block == block_down) & (iota(shape, 1) < iota(shape, 0))
    rank = jnp.sum(earlier.astype(jnp.int32), axis=1, keepdims=True)
    ids = iota((tiles, n_blocks), 1)
    held = jnp.sum((block_down == ids).astype(jnp.int32), axis=0, keepdims=True)
    padded = ((held + 1) // 2) * 2
    base = jnp.sum(jnp.where(ids < block_down, padded, 0), axis=1, keepdims=True)
    place = base + rank
    hot = place == iota((tiles, places), 1)

    def by_place(column):
        return jnp.sum(jnp.where(hot, column, 0), axis=0, keepdims=True)

    index[at : at + 1, :places] = tiles - by_place(tiles - iota((tiles, 1), 0))
    index[at + 1 : at + 2, :places] = by_place(turned(carried))
    index[at + 2 : at + 3, :places] = by_place(jnp.minimum(rank // 2, 1))
    small = (n_blocks, n_blocks)
    up_to = jnp.where(iota(small, 0) <= iota(small, 1), turned(padded), 0)
    last = jnp.sum(up_to, axis=0, keepdims=True) // 2 - 1
    index[at + 3 : at + 4, :n_blocks] = jnp.where(held > 0, last, tiles)


def order_tiles(block, carried, n_blocks, index, at):
    tiles = block.shape[1]
    shape = (tiles, tiles)
    block_down = turned(block)
    earlier = (block == block_down) & (iota(shape, 1) < iota(shape, 0))
    before = (block < block_down) | earlier
    place = jnp.sum(before.astype(jnp.int32), axis=1, keepdims=True)
    rank = jnp.sum(earlier.astype(jnp.int32), axis=1, keepdims=True)
    hot = place == iota(shape, 1)

    def by_place(column):
        return jnp.sum(jnp.where(hot, column, 0), axis=0, keepdims=True)

    index[at : at + 1, :tiles] = by_place(iota((tiles, 1), 0))
    index[at + 1 : at + 2, :tiles] = by_place(turned(carried))
    index[at + 2 : at + 3, :tiles] = by_place(jnp.minimum(rank, 1))
    ids = iota((tiles, n_blocks), 1)
    up_to = jnp.sum((block_down <= ids).astype(jnp.int32), axis=0, keepdims=True)
    held = jnp.sum((block_down == ids).astype(jnp.int32), axis=0, keepdims=True)
    index[at + 3 : at + 4, :n_blocks] = jnp.where(held > 0, up_to - 1, tiles)


def kernel(
    nz,
    tiles,
    x_hbm,
    ws_hbm,
    wn_hbm,
    bias_hbm,
    og_hbm,
    rows_hbm,
    cols_hbm,
    tiles_hbm,
    out_hbm,
    ingrad_hbm,
    gself_hbm,
    gneigh_hbm,
    gbias_hbm,
    out_ref,
    ingrad_ref,
    gself_ref,
    gneigh_ref,
    gbias_ref,
    ws_ref,
    wn_ref,
    bias_ref,
    nodes,
    rows_ref,
    cols_ref,
    index_buf,
    index,
    tile_buf,
    panels,
    runs,
    self_pre,
    self_grad,
    y_send,
    y_recv,
    zh_send,
    zh_recv,
    gt,
    core_send,
    core_recv,
    x_send,
    x_recv,
    quad_send,
    quad_recv,
    pair_send,
    pair_recv,
    wy_send,
    wy_recv,
    wz_send,
    wz_recv,
    wp_send,
    wp_recv,
    wh_send,
    wh_recv,
    wx_recv,
    wc_send,
    wc_recv,
    w_out,
    load_sems,
    store_sems,
    send_sems,
    recv_sems,
):
    half = nz // 2
    n_cols = nz * NX * NC
    n_rows = 2 * NY
    row = lax.axis_index("row")
    col = lax.axis_index("col")
    core = lax.rem(row, NC)
    x = lax.rem(row // NC, NX)
    z = row // (NC * NX)
    zq = z // half
    zi = lax.rem(z, half)
    y = lax.rem(col, NY)
    zh = col // NY
    other = 1 - core

    def at_row(z_to, x_to, core_to):
        return {"row": (z_to * NX + x_to) * NC + core_to, "col": col}

    def at_col(zh_to, y_to):
        return {"row": row, "col": zh_to * NY + y_to}

    parts = 2
    width = BLK // parts

    def lines(p):
        return pl.ds(p * width, width)

    def turn_zi(d):
        return lax.rem(zi + d, half)

    def turn_x(d):
        return lax.rem(x + d, NX)

    def turn_y(d):
        return lax.rem(y + d, NY)

    def to_mate(e):
        return at_row(zq * half + turn_zi(e), x, core)

    def to_x(d):
        return at_row(z, turn_x(d), core)

    def to_y(d):
        return at_col(zh, turn_y(d))

    to_pair = at_row((1 - zq) * half + zi, x, core)
    to_core = at_row(z, x, other)
    to_zh = at_col(1 - zh, y)
    mates = (1, 3, 2)

    ord_r, pan, keep_r, end_r, ord_c, grow, keep_c, end_c = range(8)

    def slot(core_of, x_of, e, q=0):
        return ((core_of * NX + x_of) * half + e) * 2 + q

    own = slot(core, x, 0)
    loads = []
    for src, dst in (
        (x_hbm, panels.at[own]),
        (rows_hbm, rows_ref),
        (cols_hbm, cols_ref),
        (ws_hbm, ws_ref),
        (bias_hbm, bias_ref),
        (tiles_hbm.at[0, 0], tile_buf.at[pl.ds(0, tiles)]),
        (wn_hbm, wn_ref),
        (x_hbm, nodes.at[0, :, pl.ds(0, BLK)]),
        (og_hbm, nodes.at[0, :, pl.ds(BLK, 2 * BLK)]),
    ):
        loads.append(pltpu.make_async_copy(src, dst, load_sems.at[len(loads)]))
        loads[-1].start()
    load_x, load_rows, load_cols, load_ws, load_bias, load_tiles, load_wn, load_own, load_og = loads

    barrier = pltpu.get_barrier_semaphore()
    partners = [to_mate(e) for e in mates] + [to_pair] + [to_x(d) for d in range(1, NX)]
    partners += [to_y(d) for d in range(1, NY)] + [to_core, to_zh]
    for partner in partners:
        pl.semaphore_signal(barrier, inc=1, device_id=partner, device_id_type=MESH)
    load_x.wait()
    pl.semaphore_wait(barrier, len(partners))

    links = Links(send_sems, recv_sems)
    stores = []

    def store(src, dst):
        stores.append(pltpu.make_async_copy(src, dst, store_sems.at[len(stores)]))
        stores[-1].start()

    def panels_to(first, count, device_id, dst=None):
        return links.send(
            panels.at[pl.ds(first, count)],
            panels.at[pl.ds(first if dst is None else dst, count)],
            device_id,
        )

    order = (0,) + mates
    steps_x = (2, 1, 3)
    along_x, crossed, from_mate = {}, [], {}

    def cross(x_of, i):
        if i % 2 == 1:
            first = slot(core, x_of, min(order[i - 1], order[i]))
            crossed.append(panels_to(first, half, to_core))

    def own_step(i):
        e = order[i]
        if e:
            from_mate[e].wait_recv()
        here = slot(core, x, e)
        for d in steps_x:
            along_x[i, d] = panels_to(here, 2, to_x(d))
        cross(x, i)

    def near_step(i, distances):
        for d in distances:
            along_x[i, d].wait_recv()
            cross(turn_x(NX - d), i)

    index_copy = pltpu.make_async_copy(index_buf, index, load_sems.at[len(loads)])

    def prepare():
        load_rows.wait()
        load_cols.wait()
        rows = rows_ref[...]
        cols = cols_ref[...]
        z_of = cols // (NC * NX)
        e_of = (zi - z_of) & (half - 1)
        slots = slot(cols & (NC - 1), (cols // NC) & (NX - 1), e_of, (z_of // half + zq) & 1)
        order_pairs(rows, slots, n_rows, index_buf, 0)
        order_tiles(slots, (rows & (NY - 1)) * 2 + rows // NY, n_cols, index_buf, 4)
        runs[tiles] = jnp.zeros((BLK, BLK), F32)
        tile_buf[tiles] = jnp.zeros((BLK, BLK), BF16)
        index_copy.start()
        load_ws.wait()
        load_bias.wait()
        self_pre[0] = dot_nn(panels[own], ws_ref[...]) + bias_ref[...]

    pair_copy = panels_to(own, 1, to_pair, dst=own + 1)
    pair_copy.wait_recv()
    for e in mates:
        from_mate[e] = panels_to(own, 2, to_mate(e), dst=slot(core, x, e))
    for i in range(half + 2):
        if i < half:
            own_step(i)
        if i == 0:
            prepare()
        if i == half - 1:
            load_own.wait()
            load_og.wait()
            own_copy = links.send(nodes.at[0], nodes.at[1], to_zh)
        if 0 <= i - 1 < half:
            near_step(i - 1, (1, 3))
        if 0 <= i - 2 < half:
            near_step(i - 2, (2,))
    load_tiles.wait()
    load_wn.wait()
    index_copy.wait()
    for copy in crossed:
        copy.wait_recv()
    gathered = len(links.copies)

    n_pairs = (tiles + n_rows) // 2
    step = 4

    def collect(k, acc):
        for u in range(step):
            n = k * step + u
            here = [2 * n, 2 * n + 1]
            left = jnp.concatenate([tile_buf[index[ord_r, i]] for i in here], axis=1)
            right = jnp.concatenate([panels[index[pan, i]] for i in here], axis=0)
            acc = acc * index[keep_r, 2 * n].astype(F32) + dot_nn(left, right)
            runs[n] = acc
        return acc

    lax.fori_loop(0, n_pairs // step, collect, jnp.zeros((BLK, BLK), F32))

    def row_sum(r):
        return runs[index[end_r, r]]

    y_copies = {}
    for d in (2, 1, 3):
        for h in range(2):
            y_send[d - 1, h] = row_sum(h * NY + turn_y(d)).astype(BF16)
        y_copies[d] = links.send(y_send.at[d - 1], y_recv.at[d - 1], to_y(d))
    own_copy.wait_recv()
    self_pre[1] = dot_nn(nodes[1, :, :BLK], ws_ref[...]) + bias_ref[...]
    links.finish(gathered)
    sides = (zh, 1 - zh)
    for d in (1, 3, 2):
        y_copies[d].wait_recv()
    totals = []
    for h in sides:
        value = row_sum(h * NY + y)
        for d in (1, 3, 2):
            value = value + y_recv[d - 1, h].astype(F32)
        totals.append(value)
        zh_send[h] = value.astype(BF16)
    zh_copy = links.send(zh_send, zh_recv, to_zh)
    zh_copy.wait_recv()
    totals = [
        (value + zh_recv[h].astype(F32)).astype(BF16) for value, h in zip(totals, sides)
    ]

    def layer(k):
        sums = totals[k]
        pre = self_pre[k] + dot_nn(sums, wn_ref[...])
        sig = 1.0 / (1.0 + jnp.exp(-pre))
        slope = sig * (1.0 + pre * (1.0 - sig))
        return sums, pre * sig, (nodes[k, :, BLK:].astype(F32) * slope).astype(BF16)

    sums, activated, pre_grad = layer(0)
    gt[y * 2 + zh] = dot_nt(wn_ref[...], pre_grad).astype(BF16)
    gt[y * 2 + 1 - zh] = dot_nt(wn_ref[...], layer(1)[2]).astype(BF16)
    gt_here = gt.at[pl.ds(y * 2, 2)]
    gt_copies = [links.send(gt_here, gt_here, to_y(d)) for d in (2, 1, 3)]
    out_ref[...] = activated.astype(BF16)
    store(out_ref, out_hbm)
    self_grad[...] = dot_nt(ws_ref[...], pre_grad)

    wide_self = dot_tn(panels[own], pre_grad).astype(BF16)
    wide_neigh = dot_tn(sums, pre_grad).astype(BF16)
    for q, block in enumerate(
        (wide_self[:, :BLK], wide_self[:, BLK:], wide_neigh[:, :BLK], wide_neigh[:, BLK:])
    ):
        wy_send[q, :BLK] = block
    bias_sum = jnp.sum(pre_grad.astype(F32), axis=0, keepdims=True)
    spot = lax.broadcasted_iota(jnp.int32, (16, BLK), 0)
    bias_rows = jnp.where(
        spot == 0, bias_sum[:, :BLK], jnp.where(spot == 1, bias_sum[:, BLK:], 0.0)
    ).astype(BF16)
    for q in range(4):
        wy_send[q, BLK:] = bias_rows
    wy_recv[y] = wy_send[y]

    wy_copies = [links.send(wy_send.at[turn_y(d)], wy_recv.at[y], to_y(d)) for d in (2, 1, 3)]
    links.finish(len(links.copies) - 6)
    for copy in gt_copies:
        copy.wait_recv()

    def spread(k, acc):
        for u in range(8):
            n = k * 8 + u
            term = dot_nn(gt[index[grow, n]], tile_buf[index[ord_c, n]])
            acc = acc * index[keep_c, n].astype(F32) + term
            runs[n] = acc
        return acc

    steps = tiles // 8
    acc = lax.fori_loop(0, steps // 2, spread, jnp.zeros((BLK, BLK), F32))

    for copy in wy_copies:
        copy.wait_recv()
    w_sum = wy_recv[0].astype(F32)
    for q in range(1, NY):
        w_sum = w_sum + wy_recv[q].astype(F32)
    part = BLK // half
    for q in range(half):
        wz_send[q, :part] = w_sum[q * part : (q + 1) * part]
        wz_send[q, part:] = w_sum[BLK : BLK + 8]
    wz_recv[zi] = wz_send[zi]
    wz_copies = [links.send(wz_send.at[turn_zi(e)], wz_recv.at[zi], to_mate(e)) for e in mates]

    lax.fori_loop(steps // 2, steps, spread, acc)

    turns = (2, 1, 3, 0)

    def col_sum(c, p):
        return runs[index[end_c, c], lines(p), :]

    def paired(p, d, i):
        mine = col_sum(slot(core, turn_x(d), 0) + i, p)
        return mine + core_recv[p, turns.index(d) * nz + i].astype(F32)

    core_copies, x_copies, quad_copies, pair_copies = {}, {}, {}, {}

    def core_stage(p):
        for at, d in enumerate(turns):
            for i in range(nz):
                core_send[p, at * nz + i] = col_sum(slot(other, turn_x(d), 0) + i, p).astype(BF16)
            if at in (0, NX - 1):
                blocks = pl.ds(0, nz) if at == 0 else pl.ds(nz, (NX - 1) * nz)
                core_copies[p, at] = links.send(
                    core_send.at[p, blocks], core_recv.at[p, blocks], to_core
                )

    def x_stage(p):
        for at, d in enumerate(steps_x):
            if at < 2:
                core_copies[p, at * (NX - 1)].wait_recv()
            for i in range(nz):
                x_send[p, at, i] = paired(p, d, i).astype(BF16)
            x_copies[p, d] = links.send(x_send.at[p, at], x_recv.at[p, at], to_x(d))

    def z_total(p, i):
        value = paired(p, 0, i)
        for at in range(NX - 1):
            value = value + x_recv[p, at, i].astype(F32)
        return value

    def quad_stage(p):
        for d in steps_x:
            x_copies[p, d].wait_recv()
        for e in mates:
            for q in range(2):
                quad_send[p, e, q] = z_total(p, 2 * e + q).astype(BF16)
            quad_copies[p, e] = links.send(
                quad_send.at[p, e], quad_recv.at[p, e], to_mate(half - e)
            )

    def pair_stage(p):
        value = z_total(p, 1)
        for e in mates:
            quad_copies[p, e].wait_recv()
            value = value + quad_recv[p, e, 1].astype(F32)
        pair_send[p] = value.astype(BF16)
        pair_copies[p] = links.send(pair_send.at[p], pair_recv.at[p], to_pair)

    def last_stage(p):
        value = z_total(p, 0) + self_grad[lines(p), :]
        for e in mates:
            value = value + quad_recv[p, e, 0].astype(F32)
        pair_copies[p].wait_recv()
        return value + pair_recv[p].astype(F32)

    for copy in wz_copies:
        copy.wait_recv()
    w_part = wz_recv[0]
    for q in range(1, half):
        w_part = w_part + wz_recv[q]
    wp_send[...] = w_part
    wp_copy = links.send(wp_send, wp_recv, to_pair)

    core_stage(0)
    core_stage(1)

    wp_copy.wait_recv()
    w_part = w_part + wp_recv[...]
    wh_send[...] = w_part
    wh_copy = links.send(wh_send, wh_recv, to_zh)

    x_stage(0)

    wh_copy.wait_recv()
    w_part = w_part + wh_recv[...]
    wx_recv[x] = w_part
    wx_copies = [links.send(wx_recv.at[x], wx_recv.at[x], to_x(d)) for d in (2, 1, 3)]

    x_stage(1)
    quad_stage(0)

    for copy in wx_copies:
        copy.wait_recv()
    w_part = wx_recv[0]
    for q in range(1, NX):
        w_part = w_part + wx_recv[q]
    wc_send[...] = w_part
    wc_copy = links.send(wc_send, wc_recv, to_core)

    pair_stage(0)

    wc_copy.wait_recv()
    w_part = w_part + wc_recv[...]
    gbias_ref[...] = jnp.concatenate(
        [w_part[part : part + 1], w_part[part + 1 : part + 2]], axis=1
    )
    store(gbias_ref, gbias_hbm)
    rows_here = pl.ds(pl.multiple_of(zi * part, part), part)
    w_out[y, rows_here] = w_part[:part].astype(BF16)
    gz_copies = [
        links.send(w_out.at[y, rows_here], w_out.at[y, rows_here], to_mate(e)) for e in mates
    ]

    quad_stage(1)
    for copy in gz_copies:
        copy.wait_recv()
    gy_copies = [links.send(w_out.at[y], w_out.at[y], to_y(d)) for d in (2, 1, 3)]
    pair_stage(1)
    links.finish(len(links.copies) - 8)
    grad = jnp.concatenate([last_stage(p) for p in range(parts)], axis=0)
    ingrad_ref[...] = jnp.transpose(grad).astype(BF16)
    store(ingrad_ref, ingrad_hbm)

    for copy in gy_copies:
        copy.wait_recv()
    gself_ref[:, :BLK] = w_out[0].astype(F32)
    gself_ref[:, BLK:] = w_out[1].astype(F32)
    gneigh_ref[:, :BLK] = w_out[2].astype(F32)
    gneigh_ref[:, BLK:] = w_out[3].astype(F32)
    store(gself_ref, gself_hbm)
    store(gneigh_ref, gneigh_hbm)
    links.finish()
    for copy in stores:
        copy.wait()


def place(*refs):
    count = (len(refs) - 2) // 3
    sources, targets, held = (refs[i * count : (i + 1) * count] for i in range(3))
    ins, outs = refs[-2:]
    moves = []
    for i in range(count):
        moves.append(
            (
                pltpu.make_async_copy(sources[i], held[i], ins.at[i]),
                pltpu.make_async_copy(held[i], targets[i], outs.at[i]),
            )
        )
        moves[-1][0].start()
    for into, out in moves:
        into.wait()
        out.start()
    for _, out in moves:
        out.wait()


def body(
    node_features,
    tile_values,
    tile_rows,
    tile_cols,
    weight_self,
    weight_neighbour,
    node_bias,
    output_grad,
):
    nz = lax.axis_size("row") // (NX * NC)
    half = nz // 2
    n_cols, n_rows = nz * NX * NC, lax.axis_size("col")
    tiles = tile_values.shape[2]
    feat, units = weight_self.shape
    hbm = pl.BlockSpec(memory_space=pltpu.HBM)
    block = (BLK, BLK)
    lines = (2, BLK // 2, BLK)
    part = BLK // half + 8
    sems = 256
    results = (
        jax.ShapeDtypeStruct((BLK, units), BF16),
        jax.ShapeDtypeStruct((BLK, feat), BF16),
        jax.ShapeDtypeStruct((feat, units), F32),
        jax.ShapeDtypeStruct((feat, units), F32),
        jax.ShapeDtypeStruct((1, units), F32),
    )

    def halves(*lead):
        return pltpu.VMEM((2,) + lead + (BLK // 2, BLK), BF16)

    outs = pl.pallas_call(
        functools.partial(kernel, nz, tiles),
        out_shape=results,
        in_specs=[hbm] * 8,
        out_specs=(hbm,) * 5,
        scratch_shapes=[
            *(pltpu.VMEM(result.shape, result.dtype) for result in results),
            pltpu.VMEM((feat, units), BF16),
            pltpu.VMEM((feat, units), BF16),
            pltpu.VMEM((1, units), F32),
            pltpu.VMEM((2, BLK, feat + units), BF16),
            pltpu.VMEM((1, tiles), jnp.int32),
            pltpu.VMEM((1, tiles), jnp.int32),
            pltpu.VMEM((8, BLK), jnp.int32),
            pltpu.SMEM((8, BLK), jnp.int32),
            pltpu.VMEM((tiles + 1,) + block, BF16),
            pltpu.VMEM((n_cols,) + block, BF16),
            pltpu.VMEM((tiles + 1,) + block, F32),
            pltpu.VMEM((2, BLK, units), F32),
            pltpu.VMEM(block, F32),
            pltpu.VMEM((3, 2) + block, BF16),
            pltpu.VMEM((3, 2) + block, BF16),
            pltpu.VMEM((2,) + block, BF16),
            pltpu.VMEM((2,) + block, BF16),
            pltpu.VMEM((n_rows,) + block, BF16),
            halves(NX * nz),
            halves(NX * nz),
            halves(NX - 1, nz),
            halves(NX - 1, nz),
            halves(half, 2),
            halves(half, 2),
            halves(),
            halves(),
            pltpu.VMEM((4, BLK + 16, BLK), BF16),
            pltpu.VMEM((4, BLK + 16, BLK), BF16),
            pltpu.VMEM((half, part, BLK), F32),
            pltpu.VMEM((half, part, BLK), F32),
            pltpu.VMEM((part, BLK), F32),
            pltpu.VMEM((part, BLK), F32),
            pltpu.VMEM((part, BLK), F32),
            pltpu.VMEM((part, BLK), F32),
            pltpu.VMEM((NX, part, BLK), F32),
            pltpu.VMEM((part, BLK), F32),
            pltpu.VMEM((part, BLK), F32),
            pltpu.VMEM((4,) + block, BF16),
            pltpu.SemaphoreType.DMA((10,)),
            pltpu.SemaphoreType.DMA((5,)),
            pltpu.SemaphoreType.DMA((sems,)),
            pltpu.SemaphoreType.DMA((sems,)),
        ],
        compiler_params=pltpu.CompilerParams(
            collective_id=0, has_side_effects=True, vmem_limit_bytes=VMEM_LIMIT
        ),
        cost_estimate=pl.CostEstimate(
            flops=4 * tiles * BLK**3, bytes_accessed=2 * tiles * BLK**2, transcendentals=BLK * units
        ),
    )(
        node_features,
        weight_self,
        weight_neighbour,
        node_bias.reshape(1, units),
        output_grad,
        tile_rows.reshape(1, tiles),
        tile_cols.reshape(1, tiles),
        tile_values,
    )
    outs = pl.pallas_call(
        place,
        out_shape=results,
        in_specs=[hbm] * 5,
        out_specs=(hbm,) * 5,
        scratch_shapes=[
            *(pltpu.VMEM(result.shape, result.dtype) for result in results),
            pltpu.SemaphoreType.DMA((5,)),
            pltpu.SemaphoreType.DMA((5,)),
        ],
        compiler_params=pltpu.CompilerParams(vmem_limit_bytes=VMEM_LIMIT),
    )(*outs)
    return (*outs[:4], outs[4].reshape(units))


def solution(mesh):
    placed = (
        P(("row", "col"), None),
        P("row", "col", None, None, None),
        P("row", "col", None),
        P("row", "col", None),
        P(),
        P(),
        P(),
        P(("row", "col"), None),
    )
    return jax.shard_map(
        body,
        mesh=mesh,
        in_specs=placed,
        out_specs=(P(("row", "col"), None), P(("row", "col"), None), P(), P(), P()),
        check_vma=False,
    )
```

```python
import functools

import jax
import jax.numpy as jnp
from jax import lax
from jax.experimental import pallas as pl
from jax.experimental.pallas import tpu as pltpu
from jax.sharding import PartitionSpec as P

MESH = pl.DeviceIdType.MESH
BLK = 128
F32 = jnp.float32
BF16 = jnp.bfloat16
VMEM_LIMIT = 64 * 2**20

NX, NC = 4, 2
NY = 4


def dot_nn(a, b):
    return lax.dot_general(a, b, (((1,), (0,)), ((), ())), preferred_element_type=F32)


def dot_nt(a, b):
    return lax.dot_general(a, b, (((1,), (1,)), ((), ())), preferred_element_type=F32)


def dot_tn(a, b):
    return lax.dot_general(a, b, (((0,), (0,)), ((), ())), preferred_element_type=F32)


class Links:
    def __init__(self, send_sems, recv_sems):
        self.send_sems, self.recv_sems, self.copies, self.sent = send_sems, recv_sems, [], 0

    def send(self, src, dst, device_id):
        at = len(self.copies)
        copy = pltpu.make_async_remote_copy(
            src_ref=src,
            dst_ref=dst,
            send_sem=self.send_sems.at[at],
            recv_sem=self.recv_sems.at[at],
            device_id=device_id,
            device_id_type=MESH,
        )
        copy.start()
        self.copies.append(copy)
        return copy

    def finish(self, upto=None):
        upto = len(self.copies) if upto is None else upto
        for copy in self.copies[self.sent : upto]:
            copy.wait_send()
        self.sent = max(self.sent, upto)


def iota(shape, axis):
    return lax.broadcasted_iota(jnp.int32, shape, axis)


def turned(line):
    n = line.shape[1]
    diagonal = iota((n, n), 0) == iota((n, n), 1)
    return jnp.sum(jnp.where(diagonal, line, 0), axis=1, keepdims=True)


def order_pairs(block, carried, n_blocks, index, at):
    tiles = block.shape[1]
    places = tiles + n_blocks
    shape = (tiles, tiles)
    block_down = turned(block)
    earlier = (block == block_down) & (iota(shape, 1) < iota(shape, 0))
    rank = jnp.sum(earlier.astype(jnp.int32), axis=1, keepdims=True)
    ids = iota((tiles, n_blocks), 1)
    held = jnp.sum((block_down == ids).astype(jnp.int32), axis=0, keepdims=True)
    padded = ((held + 1) // 2) * 2
    base = jnp.sum(jnp.where(ids < block_down, padded, 0), axis=1, keepdims=True)
    place = base + rank
    hot = place == iota((tiles, places), 1)

    def by_place(column):
        return jnp.sum(jnp.where(hot, column, 0), axis=0, keepdims=True)

    index[at : at + 1, :places] = tiles - by_place(tiles - iota((tiles, 1), 0))
    index[at + 1 : at + 2, :places] = by_place(turned(carried))
    index[at + 2 : at + 3, :places] = by_place(jnp.minimum(rank // 2, 1))
    small = (n_blocks, n_blocks)
    up_to = jnp.where(iota(small, 0) <= iota(small, 1), turned(padded), 0)
    last = jnp.sum(up_to, axis=0, keepdims=True) // 2 - 1
    index[at + 3 : at + 4, :n_blocks] = jnp.where(held > 0, last, tiles)


def order_tiles(block, carried, n_blocks, index, at):
    tiles = block.shape[1]
    shape = (tiles, tiles)
    block_down = turned(block)
    earlier = (block == block_down) & (iota(shape, 1) < iota(shape, 0))
    before = (block < block_down) | earlier
    place = jnp.sum(before.astype(jnp.int32), axis=1, keepdims=True)
    rank = jnp.sum(earlier.astype(jnp.int32), axis=1, keepdims=True)
    hot = place == iota(shape, 1)

    def by_place(column):
        return jnp.sum(jnp.where(hot, column, 0), axis=0, keepdims=True)

    index[at : at + 1, :tiles] = by_place(iota((tiles, 1), 0))
    index[at + 1 : at + 2, :tiles] = by_place(turned(carried))
    index[at + 2 : at + 3, :tiles] = by_place(jnp.minimum(rank, 1))
    ids = iota((tiles, n_blocks), 1)
    up_to = jnp.sum((block_down <= ids).astype(jnp.int32), axis=0, keepdims=True)
    held = jnp.sum((block_down == ids).astype(jnp.int32), axis=0, keepdims=True)
    index[at + 3 : at + 4, :n_blocks] = jnp.where(held > 0, up_to - 1, tiles)


def kernel(
    nz,
    tiles,
    x_hbm,
    ws_hbm,
    wn_hbm,
    bias_hbm,
    og_hbm,
    rows_hbm,
    cols_hbm,
    tiles_hbm,
    out_hbm,
    ingrad_hbm,
    gself_hbm,
    gneigh_hbm,
    gbias_hbm,
    out_ref,
    ingrad_ref,
    gself_ref,
    gneigh_ref,
    gbias_ref,
    ws_ref,
    wn_ref,
    bias_ref,
    nodes,
    rows_ref,
    cols_ref,
    index_buf,
    index,
    tile_buf,
    panels,
    runs,
    self_pre,
    self_grad,
    y_send,
    y_recv,
    zh_send,
    zh_recv,
    gt,
    core_send,
    core_recv,
    x_send,
    x_recv,
    z_send,
    z_recv,
    wy_send,
    wy_recv,
    wz_send,
    wz_recv,
    wp_send,
    wp_recv,
    wh_send,
    wh_recv,
    wx_recv,
    wc_send,
    wc_recv,
    w_out,
    load_sems,
    store_sems,
    send_sems,
    recv_sems,
):
    half = nz // 2
    n_cols = nz * NX * NC
    n_rows = 2 * NY
    row = lax.axis_index("row")
    col = lax.axis_index("col")
    core = lax.rem(row, NC)
    x = lax.rem(row // NC, NX)
    z = row // (NC * NX)
    zq = z // half
    zi = lax.rem(z, half)
    y = lax.rem(col, NY)
    zh = col // NY
    other = 1 - core

    def at_row(z_to, x_to, core_to):
        return {"row": (z_to * NX + x_to) * NC + core_to, "col": col}

    def at_col(zh_to, y_to):
        return {"row": row, "col": zh_to * NY + y_to}

    parts = 2
    width = BLK // parts

    def lines(p):
        return pl.ds(p * width, width)

    def turn_zi(d):
        return lax.rem(zi + d, half)

    def turn_x(d):
        return lax.rem(x + d, NX)

    def turn_y(d):
        return lax.rem(y + d, NY)

    def to_mate(e):
        return at_row(zq * half + turn_zi(e), x, core)

    def to_x(d):
        return at_row(z, turn_x(d), core)

    def to_y(d):
        return at_col(zh, turn_y(d))

    def to_far(e):
        return at_row((1 - zq) * half + turn_zi(e), x, core)

    to_pair = at_row((1 - zq) * half + zi, x, core)
    to_core = at_row(z, x, other)
    to_zh = at_col(1 - zh, y)
    mates = (1, 3, 2)

    ord_r, pan, keep_r, end_r, ord_c, grow, keep_c, end_c = range(8)

    def slot(core_of, x_of, e, q=0):
        return ((core_of * NX + x_of) * half + e) * 2 + q

    own = slot(core, x, 0)
    loads = []
    for src, dst in (
        (x_hbm, panels.at[own]),
        (rows_hbm, rows_ref),
        (cols_hbm, cols_ref),
        (ws_hbm, ws_ref),
        (bias_hbm, bias_ref),
        (tiles_hbm.at[0, 0], tile_buf.at[pl.ds(0, tiles)]),
        (wn_hbm, wn_ref),
        (x_hbm, nodes.at[0, :, pl.ds(0, BLK)]),
        (og_hbm, nodes.at[0, :, pl.ds(BLK, 2 * BLK)]),
    ):
        loads.append(pltpu.make_async_copy(src, dst, load_sems.at[len(loads)]))
        loads[-1].start()
    load_x, load_rows, load_cols, load_ws, load_bias, load_tiles, load_wn, load_own, load_og = loads

    barrier = pltpu.get_barrier_semaphore()
    partners = [to_mate(e) for e in mates] + [to_far(e) for e in range(half)] + [to_x(d) for d in range(1, NX)]
    partners += [to_y(d) for d in range(1, NY)] + [to_core, to_zh]
    for partner in partners:
        pl.semaphore_signal(barrier, inc=1, device_id=partner, device_id_type=MESH)
    load_x.wait()
    pl.semaphore_wait(barrier, len(partners))

    links = Links(send_sems, recv_sems)
    stores = []

    def store(src, dst):
        stores.append(pltpu.make_async_copy(src, dst, store_sems.at[len(stores)]))
        stores[-1].start()

    def panels_to(first, count, device_id, dst=None):
        return links.send(
            panels.at[pl.ds(first, count)],
            panels.at[pl.ds(first if dst is None else dst, count)],
            device_id,
        )

    order = (0,) + mates
    steps_x = (2, 1, 3)
    along_x, crossed, from_mate = {}, [], {}

    def cross(x_of, i):
        if i % 2 == 1:
            first = slot(core, x_of, min(order[i - 1], order[i]))
            crossed.append(panels_to(first, half, to_core))

    def own_step(i):
        e = order[i]
        for copy in from_mate[e]:
            copy.wait_recv()
        here = slot(core, x, e)
        for d in steps_x:
            along_x[i, d] = panels_to(here, 2, to_x(d))
        cross(x, i)

    def near_step(i, distances):
        for d in distances:
            along_x[i, d].wait_recv()
            cross(turn_x(NX - d), i)

    index_copy = pltpu.make_async_copy(index_buf, index, load_sems.at[len(loads)])

    def prepare():
        load_rows.wait()
        load_cols.wait()
        rows = rows_ref[...]
        cols = cols_ref[...]
        z_of = cols // (NC * NX)
        e_of = (zi - z_of) & (half - 1)
        slots = slot(cols & (NC - 1), (cols // NC) & (NX - 1), e_of, (z_of // half + zq) & 1)
        order_pairs(rows, slots, n_rows, index_buf, 0)
        order_tiles(slots, (rows & (NY - 1)) * 2 + rows // NY, n_cols, index_buf, 4)
        runs[tiles] = jnp.zeros((BLK, BLK), F32)
        tile_buf[tiles] = jnp.zeros((BLK, BLK), BF16)
        index_copy.start()
        load_ws.wait()
        load_bias.wait()
        self_pre[0] = dot_nn(panels[own], ws_ref[...]) + bias_ref[...]

    for e in mates:
        from_mate[e] = [panels_to(own, 1, to_mate(e), dst=slot(core, x, e))]
    from_mate[0] = [panels_to(own, 1, to_pair, dst=own + 1)]
    for e in mates:
        from_mate[e].append(panels_to(own, 1, to_far(e), dst=slot(core, x, e, 1)))
    for i in range(half + 2):
        if i < half:
            own_step(i)
        if i == 0:
            prepare()
        if i == half - 1:
            load_own.wait()
            load_og.wait()
            own_copy = links.send(nodes.at[0], nodes.at[1], to_zh)
        if 0 <= i - 1 < half:
            near_step(i - 1, (1, 3))
        if 0 <= i - 2 < half:
            near_step(i - 2, (2,))
    load_tiles.wait()
    load_wn.wait()
    index_copy.wait()
    for copy in crossed:
        copy.wait_recv()
    gathered = len(links.copies)

    n_pairs = (tiles + n_rows) // 2
    step = 4

    def collect(k, acc):
        for u in range(step):
            n = k * step + u
            here = [2 * n, 2 * n + 1]
            left = jnp.concatenate([tile_buf[index[ord_r, i]] for i in here], axis=1)
            right = jnp.concatenate([panels[index[pan, i]] for i in here], axis=0)
            acc = acc * index[keep_r, 2 * n].astype(F32) + dot_nn(left, right)
            runs[n] = acc
        return acc

    lax.fori_loop(0, n_pairs // step, collect, jnp.zeros((BLK, BLK), F32))

    def row_sum(r):
        return runs[index[end_r, r]]

    y_copies = {}
    for d in (2, 1, 3):
        for h in range(2):
            y_send[d - 1, h] = row_sum(h * NY + turn_y(d)).astype(BF16)
        y_copies[d] = links.send(y_send.at[d - 1], y_recv.at[d - 1], to_y(d))
    own_copy.wait_recv()
    self_pre[1] = dot_nn(nodes[1, :, :BLK], ws_ref[...]) + bias_ref[...]
    links.finish(gathered)
    sides = (zh, 1 - zh)
    for d in (1, 3, 2):
        y_copies[d].wait_recv()
    totals = []
    for h in sides:
        value = row_sum(h * NY + y)
        for d in (1, 3, 2):
            value = value + y_recv[d - 1, h].astype(F32)
        totals.append(value)
        zh_send[h] = value.astype(BF16)
    zh_copy = links.send(zh_send, zh_recv, to_zh)
    zh_copy.wait_recv()
    totals = [
        (value + zh_recv[h].astype(F32)).astype(BF16) for value, h in zip(totals, sides)
    ]

    def layer(k):
        sums = totals[k]
        pre = self_pre[k] + dot_nn(sums, wn_ref[...])
        sig = 1.0 / (1.0 + jnp.exp(-pre))
        slope = sig * (1.0 + pre * (1.0 - sig))
        return sums, pre * sig, (nodes[k, :, BLK:].astype(F32) * slope).astype(BF16)

    sums, activated, pre_grad = layer(0)
    gt[y * 2 + zh] = dot_nt(wn_ref[...], pre_grad).astype(BF16)
    gt[y * 2 + 1 - zh] = dot_nt(wn_ref[...], layer(1)[2]).astype(BF16)
    gt_here = gt.at[pl.ds(y * 2, 2)]
    gt_copies = [links.send(gt_here, gt_here, to_y(d)) for d in (2, 1, 3)]
    out_ref[...] = activated.astype(BF16)
    store(out_ref, out_hbm)
    self_grad[...] = dot_nt(ws_ref[...], pre_grad)

    wide_self = dot_tn(panels[own], pre_grad).astype(BF16)
    wide_neigh = dot_tn(sums, pre_grad).astype(BF16)
    for q, block in enumerate(
        (wide_self[:, :BLK], wide_self[:, BLK:], wide_neigh[:, :BLK], wide_neigh[:, BLK:])
    ):
        wy_send[q, :BLK] = block
    bias_sum = jnp.sum(pre_grad.astype(F32), axis=0, keepdims=True)
    spot = lax.broadcasted_iota(jnp.int32, (16, BLK), 0)
    bias_rows = jnp.where(
        spot == 0, bias_sum[:, :BLK], jnp.where(spot == 1, bias_sum[:, BLK:], 0.0)
    ).astype(BF16)
    for q in range(4):
        wy_send[q, BLK:] = bias_rows
    wy_recv[y] = wy_send[y]

    wy_copies = [links.send(wy_send.at[turn_y(d)], wy_recv.at[y], to_y(d)) for d in (2, 1, 3)]
    links.finish(len(links.copies) - 6)
    for copy in gt_copies:
        copy.wait_recv()

    def spread(k, acc):
        for u in range(8):
            n = k * 8 + u
            term = dot_nn(gt[index[grow, n]], tile_buf[index[ord_c, n]])
            acc = acc * index[keep_c, n].astype(F32) + term
            runs[n] = acc
        return acc

    steps = tiles // 8
    acc = lax.fori_loop(0, steps // 2, spread, jnp.zeros((BLK, BLK), F32))

    for copy in wy_copies:
        copy.wait_recv()
    w_sum = wy_recv[0].astype(F32)
    for q in range(1, NY):
        w_sum = w_sum + wy_recv[q].astype(F32)
    part = BLK // half
    for q in range(half):
        wz_send[q, :part] = w_sum[q * part : (q + 1) * part]
        wz_send[q, part:] = w_sum[BLK : BLK + 8]
    wz_recv[zi] = wz_send[zi]
    wz_copies = [links.send(wz_send.at[turn_zi(e)], wz_recv.at[zi], to_mate(e)) for e in mates]

    lax.fori_loop(steps // 2, steps, spread, acc)

    turns = (2, 1, 3, 0)

    def col_sum(c, p):
        return runs[index[end_c, c], lines(p), :]

    def paired(p, d, i):
        mine = col_sum(slot(core, turn_x(d), 0) + i, p)
        return mine + core_recv[p, turns.index(d) * nz + i].astype(F32)

    core_copies, x_copies, z_copies = {}, {}, {}

    def core_stage(p):
        for at, d in enumerate(turns):
            for i in range(nz):
                core_send[p, at * nz + i] = col_sum(slot(other, turn_x(d), 0) + i, p).astype(BF16)
            if at in (0, NX - 1):
                blocks = pl.ds(0, nz) if at == 0 else pl.ds(nz, (NX - 1) * nz)
                core_copies[p, at] = links.send(
                    core_send.at[p, blocks], core_recv.at[p, blocks], to_core
                )

    def x_stage(p):
        for at, d in enumerate(steps_x):
            if at < 2:
                core_copies[p, at * (NX - 1)].wait_recv()
            for i in range(nz):
                x_send[p, at, i] = paired(p, d, i).astype(BF16)
            x_copies[p, d] = links.send(x_send.at[p, at], x_recv.at[p, at], to_x(d))

    def z_total(p, i):
        value = paired(p, 0, i)
        for at in range(NX - 1):
            value = value + x_recv[p, at, i].astype(F32)
        return value

    def z_stage(p):
        for d in steps_x:
            x_copies[p, d].wait_recv()
        for q in (1, 0):
            for e in mates if q == 0 else (2, 1, 3, 0):
                z_send[p, q, e] = z_total(p, 2 * e + q).astype(BF16)
                to = to_far(half - e) if q else to_mate(half - e)
                z_copies[p, q, e] = links.send(z_send.at[p, q, e], z_recv.at[p, q, e], to)

    def last_stage(p):
        value = z_total(p, 0) + self_grad[lines(p), :]
        for (part_of, q, e), copy in z_copies.items():
            if part_of == p:
                copy.wait_recv()
                value = value + z_recv[p, q, e].astype(F32)
        return value

    for copy in wz_copies:
        copy.wait_recv()
    w_part = wz_recv[0]
    for q in range(1, half):
        w_part = w_part + wz_recv[q]
    wp_send[...] = w_part
    wp_copy = links.send(wp_send, wp_recv, to_pair)

    core_stage(0)
    core_stage(1)

    wp_copy.wait_recv()
    w_part = w_part + wp_recv[...]
    wh_send[...] = w_part
    wh_copy = links.send(wh_send, wh_recv, to_zh)

    x_stage(0)

    wh_copy.wait_recv()
    w_part = w_part + wh_recv[...]
    wx_recv[x] = w_part
    wx_copies = [links.send(wx_recv.at[x], wx_recv.at[x], to_x(d)) for d in (2, 1, 3)]

    x_stage(1)
    z_stage(0)

    for copy in wx_copies:
        copy.wait_recv()
    w_part = wx_recv[0]
    for q in range(1, NX):
        w_part = w_part + wx_recv[q]
    wc_send[...] = w_part
    wc_copy = links.send(wc_send, wc_recv, to_core)


    wc_copy.wait_recv()
    w_part = w_part + wc_recv[...]
    gbias_ref[...] = jnp.concatenate(
        [w_part[part : part + 1], w_part[part + 1 : part + 2]], axis=1
    )
    store(gbias_ref, gbias_hbm)
    rows_here = pl.ds(pl.multiple_of(zi * part, part), part)
    w_out[y, rows_here] = w_part[:part].astype(BF16)
    gz_copies = [
        links.send(w_out.at[y, rows_here], w_out.at[y, rows_here], to_mate(e)) for e in mates
    ]

    z_stage(1)
    for copy in gz_copies:
        copy.wait_recv()
    gy_copies = [links.send(w_out.at[y], w_out.at[y], to_y(d)) for d in (2, 1, 3)]
    links.finish(len(links.copies) - 12)
    grad = jnp.concatenate([last_stage(p) for p in range(parts)], axis=0)
    ingrad_ref[...] = jnp.transpose(grad).astype(BF16)
    store(ingrad_ref, ingrad_hbm)

    for copy in gy_copies:
        copy.wait_recv()
    gself_ref[:, :BLK] = w_out[0].astype(F32)
    gself_ref[:, BLK:] = w_out[1].astype(F32)
    gneigh_ref[:, :BLK] = w_out[2].astype(F32)
    gneigh_ref[:, BLK:] = w_out[3].astype(F32)
    store(gself_ref, gself_hbm)
    store(gneigh_ref, gneigh_hbm)
    links.finish()
    for copy in stores:
        copy.wait()


def place(*refs):
    count = (len(refs) - 2) // 3
    sources, targets, held = (refs[i * count : (i + 1) * count] for i in range(3))
    ins, outs = refs[-2:]
    moves = []
    for i in range(count):
        moves.append(
            (
                pltpu.make_async_copy(sources[i], held[i], ins.at[i]),
                pltpu.make_async_copy(held[i], targets[i], outs.at[i]),
            )
        )
        moves[-1][0].start()
    for into, out in moves:
        into.wait()
        out.start()
    for _, out in moves:
        out.wait()


def body(
    node_features,
    tile_values,
    tile_rows,
    tile_cols,
    weight_self,
    weight_neighbour,
    node_bias,
    output_grad,
):
    nz = lax.axis_size("row") // (NX * NC)
    half = nz // 2
    n_cols, n_rows = nz * NX * NC, lax.axis_size("col")
    tiles = tile_values.shape[2]
    feat, units = weight_self.shape
    hbm = pl.BlockSpec(memory_space=pltpu.HBM)
    block = (BLK, BLK)
    lines = (2, BLK // 2, BLK)
    part = BLK // half + 8
    sems = 256
    results = (
        jax.ShapeDtypeStruct((BLK, units), BF16),
        jax.ShapeDtypeStruct((BLK, feat), BF16),
        jax.ShapeDtypeStruct((feat, units), F32),
        jax.ShapeDtypeStruct((feat, units), F32),
        jax.ShapeDtypeStruct((1, units), F32),
    )

    def halves(*lead):
        return pltpu.VMEM((2,) + lead + (BLK // 2, BLK), BF16)

    outs = pl.pallas_call(
        functools.partial(kernel, nz, tiles),
        out_shape=results,
        in_specs=[hbm] * 8,
        out_specs=(hbm,) * 5,
        scratch_shapes=[
            *(pltpu.VMEM(result.shape, result.dtype) for result in results),
            pltpu.VMEM((feat, units), BF16),
            pltpu.VMEM((feat, units), BF16),
            pltpu.VMEM((1, units), F32),
            pltpu.VMEM((2, BLK, feat + units), BF16),
            pltpu.VMEM((1, tiles), jnp.int32),
            pltpu.VMEM((1, tiles), jnp.int32),
            pltpu.VMEM((8, BLK), jnp.int32),
            pltpu.SMEM((8, BLK), jnp.int32),
            pltpu.VMEM((tiles + 1,) + block, BF16),
            pltpu.VMEM((n_cols,) + block, BF16),
            pltpu.VMEM((tiles + 1,) + block, F32),
            pltpu.VMEM((2, BLK, units), F32),
            pltpu.VMEM(block, F32),
            pltpu.VMEM((3, 2) + block, BF16),
            pltpu.VMEM((3, 2) + block, BF16),
            pltpu.VMEM((2,) + block, BF16),
            pltpu.VMEM((2,) + block, BF16),
            pltpu.VMEM((n_rows,) + block, BF16),
            halves(NX * nz),
            halves(NX * nz),
            halves(NX - 1, nz),
            halves(NX - 1, nz),
            halves(2, half),
            halves(2, half),
            pltpu.VMEM((4, BLK + 16, BLK), BF16),
            pltpu.VMEM((4, BLK + 16, BLK), BF16),
            pltpu.VMEM((half, part, BLK), F32),
            pltpu.VMEM((half, part, BLK), F32),
            pltpu.VMEM((part, BLK), F32),
            pltpu.VMEM((part, BLK), F32),
            pltpu.VMEM((part, BLK), F32),
            pltpu.VMEM((part, BLK), F32),
            pltpu.VMEM((NX, part, BLK), F32),
            pltpu.VMEM((part, BLK), F32),
            pltpu.VMEM((part, BLK), F32),
            pltpu.VMEM((4,) + block, BF16),
            pltpu.SemaphoreType.DMA((10,)),
            pltpu.SemaphoreType.DMA((5,)),
            pltpu.SemaphoreType.DMA((sems,)),
            pltpu.SemaphoreType.DMA((sems,)),
        ],
        compiler_params=pltpu.CompilerParams(
            collective_id=0, has_side_effects=True, vmem_limit_bytes=VMEM_LIMIT
        ),
        cost_estimate=pl.CostEstimate(
            flops=4 * tiles * BLK**3, bytes_accessed=2 * tiles * BLK**2, transcendentals=BLK * units
        ),
    )(
        node_features,
        weight_self,
        weight_neighbour,
        node_bias.reshape(1, units),
        output_grad,
        tile_rows.reshape(1, tiles),
        tile_cols.reshape(1, tiles),
        tile_values,
    )
    outs = pl.pallas_call(
        place,
        out_shape=results,
        in_specs=[hbm] * 5,
        out_specs=(hbm,) * 5,
        scratch_shapes=[
            *(pltpu.VMEM(result.shape, result.dtype) for result in results),
            pltpu.SemaphoreType.DMA((5,)),
            pltpu.SemaphoreType.DMA((5,)),
        ],
        compiler_params=pltpu.CompilerParams(vmem_limit_bytes=VMEM_LIMIT),
    )(*outs)
    return (*outs[:4], outs[4].reshape(units))


def solution(mesh):
    placed = (
        P(("row", "col"), None),
        P("row", "col", None, None, None),
        P("row", "col", None),
        P("row", "col", None),
        P(),
        P(),
        P(),
        P(("row", "col"), None),
    )
    return jax.shard_map(
        body,
        mesh=mesh,
        in_specs=placed,
        out_specs=(P(("row", "col"), None), P(("row", "col"), None), P(), P(), P()),
        check_vma=False,
    )
```
